32 devices in a mesh: src: 8 (over z, x), row: 4 (over y, core).
Axes of the slice: x: 2, y: 2, z: 4, core: 2. Of those that a mesh axis runs over, the one named last changes fastest.
Arguments:
- factor: float32 [10240, 1024], P(('row', 'src')), as said below
- right_side: float32 [10240, 4096], P('row', 'src'), may hold values from -6 to 6
Outputs:
- advanced: float32 [10240, 4096], P('row', 'src')
The draws below stay inside these ranges and needn't reach their ends.
Inputs may be any that keep to these rules, and one draw needn't show every extreme that they name: factor is zero where its column index exceeds its row index, and its entries where the two are equal lie between 1 and 2.
All inputs are finite; a program needn't handle non-finite values.
Results may differ from the reference program's by a relative error of at most 0.0001.
Values sent between devices are 32-bit elements; how exact they have to be, the bound alone decides.
No kernel may reach another device: no remote copies, remote signals or barrier semaphores. Data moves between devices by JAX's collectives and lax.ppermute only.
A program may use at most 64 MiB of HBM per device.

```python
import jax
import jax.numpy as jnp
from jax import lax

PB = 512
ROWS = 10240
RHS = 4096


def draw_factor(key, part):
    key_off = jax.random.fold_in(key, 11)
    key_diag = jax.random.fold_in(key, 23)
    shape = (ROWS, 2 * PB)
    spread = jax.random.normal(key_off, shape, jnp.float32)
    offdiag = spread * (0.4 / PB ** 0.5)
    diagval = jax.random.uniform(key_diag, shape, jnp.float32, 1.0, 2.0)
    row_ids = jnp.arange(ROWS)[:, None]
    col_ids = jnp.arange(2 * PB)[None, :]
    result = jnp.where(col_ids > row_ids, 0.0, jnp.where(col_ids == row_ids, diagval, offdiag))
    return result.astype(jnp.float32)


def level_of(own_key, extent, split, least, largest):
    level = 1.0
    for position, blocks in split:
        heights = jax.random.uniform(jax.random.fold_in(jax.random.fold_in(own_key, 6), position), (blocks,), jnp.float32, least / len(split), largest / len(split))
        level = level * jnp.repeat(jnp.exp(heights), extent[position] // blocks).reshape((-1,) + (1,) * (len(extent) - 1 - position))
    return level


def noise(own_key, shape, width, bound, split=(), held_as=jnp.bfloat16):
    drawn = width * jax.random.normal(own_key, shape, jnp.float32)
    if split:
        drawn = drawn * level_of(own_key, shape, split, -0.22, 0.18)
    return jnp.clip(drawn, -bound, bound).astype(held_as)


def setup_inputs(seed: int = 0) -> dict:
    key_list = jax.random.split(jax.random.key(seed), 3)
    factor = draw_factor(jax.random.fold_in(key_list[2], 71), 0)
    right_side = noise(key_list[1], (ROWS, RHS), 1.0, 6.0, ((0, 4), (1, 8)), jnp.float32)
    return dict(factor=factor, right_side=right_side)


def reference(factor, right_side):
    current = right_side
    for section in range(2):
        offset = section * PB
        diag_block = factor[offset:offset + PB, offset:offset + PB]
        solved = lax.linalg.triangular_solve(diag_block, current[offset:offset + PB], left_side=True, lower=True)
        below = factor[offset + PB:, offset:offset + PB]
        product = jnp.dot(below.astype(jnp.float32), solved.astype(jnp.float32), preferred_element_type=jnp.float32, precision=lax.Precision.HIGHEST)
        current = current.at[offset + PB:].set(current[offset + PB:] - product)
        current = current.at[offset:offset + PB].set(solved)
    return current
```

```python
import functools
import math

import jax
import jax.numpy as jnp
from jax import lax
from jax.experimental import pallas as pl
from jax.experimental.pallas import tpu as pltpu
from jax.sharding import PartitionSpec as P

VMEM_BYTES = 52 * 1024 * 1024
RING_LIMIT = 16
HIGHEST = lax.Precision.HIGHEST


def dot32(a, b):
    return jnp.dot(a, b, preferred_element_type=jnp.float32, precision=HIGHEST)


def dot16(a, b):
    return jnp.dot(a, b, preferred_element_type=jnp.float32)


def split16(value):
    high = value.astype(jnp.bfloat16)
    return high, (value - high.astype(jnp.float32)).astype(jnp.bfloat16)


def invert_lower(block):
    size = block.shape[0]
    row = lax.broadcasted_iota(jnp.int32, (size, size), 0)
    col = lax.broadcasted_iota(jnp.int32, (size, size), 1)
    diag = jnp.where(row == col, block, 0.0)
    down = 1.0 / jnp.sum(diag, axis=1, keepdims=True)
    across = 1.0 / jnp.sum(diag, axis=0, keepdims=True)
    below = (row % 2 == 1) & (col == row - 1)
    inverse = jnp.where(row == col, down, 0.0) - jnp.where(below, down * block * across, 0.0)
    half = 2
    while half < size:
        below = (row // half % 2 == 1) & (col // half == row // half - 1)
        coupling = jnp.where(below, block, 0.0)
        inverse = inverse - dot32(inverse, dot32(coupling, inverse))
        half *= 2
    return inverse


def solve_kernel(pieces, rows, width, chunk, panel, ids, place, *refs):
    panels = panel + 1
    held = refs[: pieces * panels]
    rhs = refs[pieces * panels]
    earlier = refs[pieces * panels + 1 : pieces * panels + 1 + panel]
    solved = refs[pieces * panels + 1 + panel]
    lower, piece_sem, rhs_sem = refs[pieces * panels + 2 + panel :]
    first, last = panel * width, (panel + 1) * width

    @pl.when(place[0] == 0)
    def _():
        def copies(i, k):
            at = pl.multiple_of(ids[i] * rows, 8)
            return pltpu.make_async_copy(
                held[k * pieces + i],
                lower.at[pl.ds(at, rows), pl.ds(k * width, width)],
                piece_sem.at[k, i],
            )

        def needed(i):
            return (ids[i] * rows < last) & ((ids[i] + 1) * rows > first)

        for i in range(pieces):

            @pl.when(needed(i))
            def _(i=i):
                for k in range(panels):
                    copies(i, k).start()

        load = pltpu.make_async_copy(rhs.at[pl.ds(first, width)], solved, rhs_sem)
        load.start()
        for i in range(pieces):

            @pl.when(needed(i))
            def _(i=i):
                for k in range(panels):
                    copies(i, k).wait()

        load.wait()
        inverses = []
        for j in range(0, width, chunk):
            inverses.append(
                invert_lower(lower[first + j : first + j + chunk, first + j : first + j + chunk])
            )
        for j in range(0, width, chunk):
            at = slice(first + j, first + j + chunk)
            value = solved[j : j + chunk]
            for k in range(panel):
                value = value - dot32(lower[at, k * width : (k + 1) * width], earlier[k][...])
            if j:
                value = value - dot32(lower[at, first : first + j], solved[:j])
            solved[j : j + chunk] = dot32(inverses[j // chunk], value)


def solve_panel(panel, ids, place, held, rhs, earlier, width):
    pieces = len(held[0])
    rows = held[0][0].shape[0]
    columns = rhs.shape[1]
    tall = -(-(panel + 1) * width // rows) * rows
    any_space = pl.BlockSpec(memory_space=pl.ANY)
    scalars = pl.BlockSpec(memory_space=pltpu.SMEM)
    whole = pl.BlockSpec(memory_space=pltpu.VMEM)
    return pl.pallas_call(
        functools.partial(solve_kernel, pieces, rows, width, math.gcd(width, 256), panel),
        out_shape=jax.ShapeDtypeStruct((width, columns), jnp.float32),
        in_specs=[scalars] * 2 + [any_space] * (pieces * (panel + 1) + 1) + [whole] * panel,
        out_specs=whole,
        scratch_shapes=[
            pltpu.VMEM((tall, (panel + 1) * width), jnp.float32),
            pltpu.SemaphoreType.DMA((panel + 1, pieces)),
            pltpu.SemaphoreType.DMA,
        ],
        compiler_params=pltpu.CompilerParams(vmem_limit_bytes=VMEM_BYTES),
        cost_estimate=pl.CostEstimate(
            flops=12 * width * width * columns, bytes_accessed=12 * width * columns, transcendentals=0
        ),
    )(ids, place, *[piece for group in held for piece in group], rhs, *earlier)


def product_kernel(pieces, rows, width, tile, step, places, ids, place, *refs):
    held, refs = refs[: 2 * pieces], refs[2 * pieces :]
    rhs, refs = refs[0], refs[1:]
    solved, refs = refs[: 2 * places], refs[2 * places :]
    out, lower, block, found, piece_sem, rhs_sem, found_sem, out_sem = refs
    depth = 2 * width
    start = place[0] * rhs.shape[0]

    def fetch(k, r):
        return pltpu.make_async_copy(
            solved[k * places + r], found.at[pl.ds(k * width, width)], found_sem.at[k]
        )

    for r in range(places):

        @pl.when(place[0] == r)
        def _(r=r):
            for k in range(2):
                fetch(k, r).start()

    def at(i):
        return pl.ds(pl.multiple_of(ids[i] * rows, 8), rows)

    def loads(i):
        return [
            pltpu.make_async_copy(
                held[k * pieces + i], lower.at[i, :, pl.ds(k * width, width)], piece_sem.at[k, i]
            )
            for k in range(2)
        ] + [pltpu.make_async_copy(rhs.at[at(i)], block.at[i], rhs_sem.at[i])]

    for i in range(pieces):
        for load in loads(i):
            load.start()
    for k in range(2):
        fetch(k, 0).wait()
    high, low = split16(found[...])
    for i in range(pieces):
        for load in loads(i):
            load.wait()
        for t in range(0, rows, tile):
            left, left_low = split16(lower[i, t : t + tile])
            product = dot16(left, high) + dot16(left, low) + dot16(left_low, high)
            for u in range(0, tile, step):
                inside = slice(t + u, t + u + step)
                row = start + ids[i] * rows + t + u

                @pl.when(row < depth)
                def _():
                    block[i, inside] = found[pl.ds(pl.multiple_of(row, 8), step)]

                @pl.when(row >= depth)
                def _():
                    block[i, inside] = block[i, inside] - product[u : u + step]

        pltpu.make_async_copy(block.at[i], out.at[at(i)], out_sem.at[i]).start()
    for i in range(pieces):
        pltpu.make_async_copy(block.at[i], out.at[at(i)], out_sem.at[i]).wait()


def product_update(ids, place, held, rhs, solved, width):
    pieces, places = len(held[0]), len(solved[0])
    rows, columns = held[0][0].shape[0], rhs.shape[1]
    step = math.gcd(rows, 2 * width)
    tile = step * max(m for m in range(1, rows // step + 1) if rows // step % m == 0 and step * m <= 512)
    any_space = pl.BlockSpec(memory_space=pl.ANY)
    scalars = pl.BlockSpec(memory_space=pltpu.SMEM)
    return pl.pallas_call(
        functools.partial(product_kernel, pieces, rows, width, tile, step, places),
        out_shape=jax.ShapeDtypeStruct(rhs.shape, jnp.float32),
        in_specs=[scalars] * 2 + [any_space] * (2 * pieces + 1 + 2 * places),
        out_specs=any_space,
        scratch_shapes=[
            pltpu.VMEM((pieces, rows, 2 * width), jnp.float32),
            pltpu.VMEM((pieces, rows, columns), jnp.float32),
            pltpu.VMEM((2 * width, columns), jnp.float32),
            pltpu.SemaphoreType.DMA((2, pieces)),
            pltpu.SemaphoreType.DMA((pieces,)),
            pltpu.SemaphoreType.DMA((2,)),
            pltpu.SemaphoreType.DMA((pieces,)),
        ],
        compiler_params=pltpu.CompilerParams(vmem_limit_bytes=VMEM_BYTES),
        cost_estimate=pl.CostEstimate(
            flops=12 * pieces * rows * width * columns,
            bytes_accessed=8 * pieces * rows * (width + columns),
            transcendentals=0,
        ),
    )(ids, place, *held[0], *held[1], rhs, *solved[0], *solved[1])


def gather_pieces(factor, width, count):
    panels = [factor[:, :width], factor[:, width:]]
    me = lax.axis_index("src")
    if count % 2 or count > RING_LIMIT:
        gathered = [lax.all_gather(panel, "src", axis=0, tiled=True) for panel in panels]
        return [[piece] for piece in gathered], [jnp.zeros_like(me)]
    ring = list(range(0, count, 2)) + list(range(count - 1, 0, -2))
    onward = [(ring[i], ring[(i + 1) % count]) for i in range(count)]
    back = [(b, a) for a, b in onward]
    position = jnp.where(me % 2 == 0, me // 2, count - 1 - me // 2)

    def shard_at(spot):
        spot = (spot + count) % count
        return jnp.where(spot < count // 2, 2 * spot, 2 * (count - 1 - spot) + 1)

    held = [[panel] for panel in panels]
    ids = [me]
    going = [[panel, panel] for panel in panels]
    for step in range(1, count // 2 + 1):
        last = step == count // 2
        for k in range(2):
            for way, pairs in enumerate((onward, back)):
                if last and way != k:
                    continue
                going[k][way] = lax.ppermute(going[k][way], "src", pairs)
                held[k].append(going[k][way])
        ids += [shard_at(position - step)] + ([] if last else [shard_at(position + step)])
    return held, ids


def spread_rows(block, count):
    found = {0: block}
    stride = count // 2
    while stride:
        for r in list(found):
            found[r + stride] = lax.ppermute(found[r], "row", [(r, r + stride)])
        stride //= 2
    return [found[r] for r in range(count)]


def solution(mesh):
    sources, places = mesh.shape["src"], mesh.shape["row"]

    def local(factor, right_side):
        width = factor.shape[1] // 2
        place = lax.axis_index("row").reshape(1).astype(jnp.int32)
        held, ids = gather_pieces(factor, width, sources)
        ids = jnp.stack(ids).astype(jnp.int32)
        first = solve_panel(0, ids, place, held[:1], right_side, [], width)
        second = solve_panel(1, ids, place, held, right_side, [first], width)
        solved = [spread_rows(first, places), spread_rows(second, places)]
        return product_update(ids, place, held, right_side, solved, width)

    placed = (P(("row", "src"), None), P("row", "src"))
    return jax.shard_map(
        local, mesh=mesh, in_specs=placed, out_specs=P("row", "src"), check_vma=False
    )
```

```python
import functools
import math

import jax
import jax.numpy as jnp
from jax import lax
from jax.experimental import pallas as pl
from jax.experimental.pallas import tpu as pltpu
from jax.sharding import PartitionSpec as P

VMEM_BYTES = 40 * 1024 * 1024
LANES = 128
RING_LIMIT = 16

ANY = pl.BlockSpec(memory_space=pl.ANY)
SCALARS = pl.BlockSpec(memory_space=pltpu.SMEM)
WHOLE = pl.BlockSpec(memory_space=pltpu.VMEM)


def dot32(a, b):
    return jnp.dot(a, b, preferred_element_type=jnp.float32, precision=lax.Precision.HIGHEST)


def split16(value):
    high = value.astype(jnp.bfloat16)
    return high, (value - high.astype(jnp.float32)).astype(jnp.bfloat16)


def dot_split(a, b):
    (a_high, a_low), (b_high, b_low) = a, b
    dot = functools.partial(jnp.dot, preferred_element_type=jnp.float32)
    return dot(a_high, b_high) + dot(a_high, b_low) + dot(a_low, b_high)


def grid_ids(size):
    return [lax.broadcasted_iota(jnp.int32, (size, size), axis) for axis in range(2)]


def below_blocks(half, row, col):
    return (row // half % 2 == 1) & (col // half == row // half - 1)


def invert_lower(blocks):
    size = blocks[0].shape[0]
    row, col = grid_ids(size)
    inverses = []
    for block in blocks:
        diag = jnp.where(row == col, block, 0.0)
        down = 1.0 / jnp.sum(diag, axis=1, keepdims=True)
        across = 1.0 / jnp.sum(diag, axis=0, keepdims=True)
        below = below_blocks(1, row, col)
        inverses.append(
            jnp.where(row == col, down, 0.0) - jnp.where(below, down * block * across, 0.0)
        )
    half = 2
    while half < size:
        below = below_blocks(half, row, col)
        inner = [
            dot32(jnp.where(below, block, 0.0), inverse) for block, inverse in zip(blocks, inverses)
        ]
        inverses = [inverse - dot32(inverse, part) for inverse, part in zip(inverses, inner)]
        half *= 2
    return inverses


def prepare_kernel(rows, block, depth, me, place, factor, out):
    width = depth // 2
    out[...] = factor[:, width:]
    first = me[0] * rows

    @pl.when((place[0] == 0) & (first < depth))
    def _():
        blocks = []
        for j in range(0, rows, block):
            at = jnp.minimum(first + j, depth - block)
            near = pl.multiple_of(at // LANES * LANES, LANES)
            value = factor[j : j + block, pl.ds(near, LANES)]
            value = pltpu.roll(value, (LANES - at % LANES) % LANES, 1)
            blocks.append(value[:, :block])
        row, col = grid_ids(block)
        blocks = [
            jnp.where(first + i * block < depth, value, jnp.where(row == col, 1.0, 0.0))
            for i, value in enumerate(blocks)
        ]
        for i, inverse in enumerate(invert_lower(blocks)):

            @pl.when(first + i * block < depth)
            def _(i=i, inverse=inverse):
                out[i * block : (i + 1) * block, width - block :] = inverse


def prepare(me, place, factor, block):
    rows, depth = factor.shape
    return pl.pallas_call(
        functools.partial(prepare_kernel, rows, block, depth),
        out_shape=jax.ShapeDtypeStruct((rows, depth // 2), jnp.float32),
        in_specs=[SCALARS] * 2 + [WHOLE],
        out_specs=WHOLE,
        compiler_params=pltpu.CompilerParams(vmem_limit_bytes=VMEM_BYTES // 2),
        cost_estimate=pl.CostEstimate(
            flops=24 * rows * block * block, bytes_accessed=6 * rows * depth, transcendentals=0
        ),
    )(me, place, factor)


def solve_kernel(pieces, rows, width, chunk, block, panel, ids, place, *refs):
    held, refs = refs[: 2 * pieces], refs[2 * pieces :]
    rhs, refs = refs[0], refs[1:]
    earlier, refs = refs[:panel], refs[panel:]
    solved, lower, piece_sem, rhs_sem = refs
    first, last = panel * width, (panel + 1) * width
    side = lower.shape[1] - LANES

    @pl.when(place[0] == 0)
    def _():
        def copies(i):
            at = pl.ds(pl.multiple_of(ids[i] * rows, 8), rows)
            cut = 0 if panel else width - LANES
            return [
                pltpu.make_async_copy(
                    held[i], lower.at[at, pl.ds(0, width)], piece_sem.at[0, i]
                ),
                pltpu.make_async_copy(
                    held[pieces + i].at[:, pl.ds(cut, width - cut)],
                    lower.at[at, pl.ds(width, width - cut)],
                    piece_sem.at[1, i],
                ),
            ]

        def needed(i):
            return (ids[i] * rows < last) & ((ids[i] + 1) * rows > first)

        for i in range(pieces):

            @pl.when(needed(i))
            def _(i=i):
                for copy in copies(i):
                    copy.start()

        load = pltpu.make_async_copy(rhs.at[pl.ds(first, width)], solved, rhs_sem)
        load.start()
        for i in range(pieces):

            @pl.when(needed(i))
            def _(i=i):
                for copy in copies(i):
                    copy.wait()

        load.wait()
        row, col = grid_ids(chunk)
        lane = lax.broadcasted_iota(jnp.int32, (chunk, LANES), 1)
        starts = range(0, width, chunk)
        inverses = []
        for j in starts:
            value = lower[first + j : first + j + chunk, side:]
            value = jnp.where(lane >= LANES - block, value, 0.0)
            shift = block
            while shift < LANES:
                value = value + pltpu.roll(value, LANES - shift, 1)
                shift *= 2
            value = jnp.concatenate([value] * (chunk // LANES), axis=1)
            inverses.append(jnp.where(row // block == col // block, value, 0.0))
        half = block
        while half < chunk:
            below = below_blocks(half, row, col)
            parts = [split16(inverse) for inverse in inverses]
            inner = [
                dot_split(
                    split16(
                        jnp.where(
                            below,
                            lower[first + j : first + j + chunk, first + j : first + j + chunk],
                            0.0,
                        )
                    ),
                    part,
                )
                for j, part in zip(starts, parts)
            ]
            inverses = [
                inverse - dot_split(part, split16(value))
                for inverse, part, value in zip(inverses, parts, inner)
            ]
            half *= 2
        for k in range(panel):
            solved[...] = solved[...] - dot_split(
                split16(lower[first:last, k * width : (k + 1) * width]), split16(earlier[k][...])
            )
        for j in starts:
            value = solved[j : j + chunk]
            if j:
                at = slice(first + j, first + j + chunk)
                value = value - dot_split(
                    split16(lower[at, first : first + j]), split16(solved[:j])
                )
            solved[j : j + chunk] = dot_split(split16(inverses[j // chunk]), split16(value))


def solve_panel(panel, ids, place, held, rhs, earlier, width, block):
    pieces = len(held[0])
    rows = held[0][0].shape[0]
    columns = rhs.shape[1]
    tall = -(-(panel + 1) * width // rows) * rows
    chunk = math.gcd(width, 2 * LANES)
    return pl.pallas_call(
        functools.partial(solve_kernel, pieces, rows, width, chunk, block, panel),
        out_shape=jax.ShapeDtypeStruct((width, columns), jnp.float32),
        in_specs=[SCALARS] * 2 + [ANY] * (2 * pieces + 1) + [WHOLE] * panel,
        out_specs=WHOLE,
        scratch_shapes=[
            pltpu.VMEM((tall, 2 * width if panel else width + LANES), jnp.float32),
            pltpu.SemaphoreType.DMA((2, pieces)),
            pltpu.SemaphoreType.DMA,
        ],
        compiler_params=pltpu.CompilerParams(vmem_limit_bytes=VMEM_BYTES // 2),
        cost_estimate=pl.CostEstimate(
            flops=6 * (panel + 1) * width * width * columns,
            bytes_accessed=12 * width * columns,
            transcendentals=0,
        ),
    )(ids, place, *held[0], *held[1], rhs, *earlier)


def update_kernel(pieces, rows, width, tile, step, places, panel, ids, place, *refs):
    held, refs = refs[:pieces], refs[pieces:]
    current, refs = refs[0], refs[1:]
    solved, refs = refs[:places], refs[places:]
    out, lower, block, found, high, low, product, piece_sem, block_sem, found_sem, out_sem = refs
    first, last = panel * width, (panel + 1) * width
    start = place[0] * current.shape[0]

    def fetch(r):
        return pltpu.make_async_copy(solved[r], found, found_sem)

    for r in range(places):

        @pl.when(place[0] == r)
        def _(r=r):
            fetch(r).start()

    def at(i):
        return pl.ds(pl.multiple_of(ids[i] * rows, 8), rows)

    def loads(i, source):
        return [
            pltpu.make_async_copy(held[source], lower.at[i], piece_sem.at[i]),
            pltpu.make_async_copy(current.at[at(i)], block.at[i], block_sem.at[i]),
        ]

    def store(i):
        return pltpu.make_async_copy(block.at[i], out.at[at(i)], out_sem.at[i])

    for i in range(pieces):
        for load in loads(i, i):
            load.start()
    fetch(0).wait()
    high[...], low[...] = split16(found[...])

    @pl.loop(0, pieces)
    def _(i):
        for load in loads(i, 0):
            load.wait()

        @pl.loop(0, rows // tile)
        def _(t):
            inside = pl.multiple_of(t * tile, 8)
            top = start + ids[i] * rows + inside
            product[...] = dot_split(
                split16(lower[i, pl.ds(inside, tile)]), (high[...], low[...])
            )

            @pl.when(top >= last)
            def _():
                block[i, pl.ds(inside, tile)] = block[i, pl.ds(inside, tile)] - product[...]

            @pl.when(top < last)
            def _():
                @pl.loop(0, tile // step)
                def _(u):
                    part = pl.multiple_of(u * step, 8)
                    row = top + part
                    here = pl.ds(inside + part, step)

                    @pl.when((row >= first) & (row < last))
                    def _():
                        block[i, here] = found[pl.ds(pl.multiple_of(row - first, 8), step)]

                    @pl.when(row >= last)
                    def _():
                        block[i, here] = block[i, here] - product[pl.ds(part, step)]

        store(i).start()

    @pl.loop(0, pieces)
    def _(i):
        store(i).wait()


def update(panel, ids, place, held, current, solved, width):
    pieces, places = len(held), len(solved)
    rows, columns = held[0].shape[0], current.shape[1]
    step = math.gcd(rows, width)
    tile = step * max(m for m in range(1, rows // step + 1) if rows // step % m == 0 and step * m <= 512)
    return pl.pallas_call(
        functools.partial(update_kernel, pieces, rows, width, tile, step, places, panel),
        out_shape=jax.ShapeDtypeStruct(current.shape, jnp.float32),
        in_specs=[SCALARS] * 2 + [ANY] * (pieces + 1 + places),
        out_specs=ANY,
        scratch_shapes=[
            pltpu.VMEM((pieces, rows, width), jnp.float32),
            pltpu.VMEM((pieces, rows, columns), jnp.float32),
            pltpu.VMEM((width, columns), jnp.float32),
            pltpu.VMEM((width, columns), jnp.bfloat16),
            pltpu.VMEM((width, columns), jnp.bfloat16),
            pltpu.VMEM((tile, columns), jnp.float32),
            pltpu.SemaphoreType.DMA((pieces,)),
            pltpu.SemaphoreType.DMA((pieces,)),
            pltpu.SemaphoreType.DMA,
            pltpu.SemaphoreType.DMA((pieces,)),
        ],
        compiler_params=pltpu.CompilerParams(vmem_limit_bytes=VMEM_BYTES),
        cost_estimate=pl.CostEstimate(
            flops=6 * pieces * rows * width * columns,
            bytes_accessed=4 * pieces * rows * (width + 2 * columns),
            transcendentals=0,
        ),
    )(ids, place, *held, current, *solved)


def gather_pieces(panels, count):
    me = lax.axis_index("src")
    if count % 2 or count > RING_LIMIT:
        gathered = [lax.all_gather(panel, "src", axis=0, tiled=True) for panel in panels]
        return [[piece] for piece in gathered], [jnp.zeros_like(me)]
    ring = list(range(0, count, 2)) + list(range(count - 1, 0, -2))
    onward = [(ring[i], ring[(i + 1) % count]) for i in range(count)]
    back = [(b, a) for a, b in onward]
    position = jnp.where(me % 2 == 0, me // 2, count - 1 - me // 2)

    def shard_at(spot):
        spot = (spot + count) % count
        return jnp.where(spot < count // 2, 2 * spot, 2 * (count - 1 - spot) + 1)

    held = [[panel] for panel in panels]
    ids = [me]
    going = [[panel, panel] for panel in panels]
    for step in range(1, count // 2 + 1):
        last = step == count // 2
        for k in range(2):
            for way, pairs in enumerate((onward, back)):
                if last and way != k:
                    continue
                going[k][way] = lax.ppermute(going[k][way], "src", pairs)
                held[k].append(going[k][way])
        ids += [shard_at(position - step)] + ([] if last else [shard_at(position + step)])
    return held, ids


def spread_rows(block, count):
    found = {0: block}
    stride = count // 2
    while stride:
        for r in list(found):
            found[r + stride] = lax.ppermute(found[r], "row", [(r, r + stride)])
        stride //= 2
    return [found[r] for r in range(count)]


def solution(mesh):
    sources, places = mesh.shape["src"], mesh.shape["row"]

    def local(factor, right_side):
        rows, depth = factor.shape
        width = depth // 2
        block = math.gcd(math.gcd(rows, width), LANES)
        me = lax.axis_index("src").reshape(1).astype(jnp.int32)
        place = lax.axis_index("row").reshape(1).astype(jnp.int32)
        panels = [factor[:, :width], prepare(me, place, factor, block)]
        held, ids = gather_pieces(panels, sources)
        ids = jnp.stack(ids).astype(jnp.int32)
        first = solve_panel(0, ids, place, held, right_side, [], width, block)
        second = solve_panel(1, ids, place, held, right_side, [first], width, block)
        current = update(0, ids, place, held[0], right_side, spread_rows(first, places), width)
        return update(1, ids, place, held[1], current, spread_rows(second, places), width)

    placed = (P(("row", "src"), None), P("row", "src"))
    return jax.shard_map(
        local, mesh=mesh, in_specs=placed, out_specs=P("row", "src"), check_vma=False
    )
```

```python
import functools
import math

import jax
import jax.numpy as jnp
from jax import lax
from jax.experimental import pallas as pl
from jax.experimental.pallas import tpu as pltpu
from jax.sharding import PartitionSpec as P

VMEM_BYTES = 60 * 1024 * 1024
LANES = 128
RING_LIMIT = 16
TOKEN_STEP = 2

ANY = pl.BlockSpec(memory_space=pltpu.HBM)
SCALARS = pl.BlockSpec(memory_space=pltpu.SMEM)
WHOLE = pl.BlockSpec(memory_space=pltpu.VMEM)


def dot32(a, b):
    return jnp.dot(a, b, preferred_element_type=jnp.float32, precision=lax.Precision.HIGHEST)


def split16(value):
    high = value.astype(jnp.bfloat16)
    return high, (value - high.astype(jnp.float32)).astype(jnp.bfloat16)


def dot_split(a, b):
    (a_high, a_low), (b_high, b_low) = a, b
    dot = functools.partial(jnp.dot, preferred_element_type=jnp.float32)
    return dot(a_high, b_high) + dot(a_high, b_low) + dot(a_low, b_high)


def grid_ids(size):
    return [lax.broadcasted_iota(jnp.int32, (size, size), axis) for axis in range(2)]


def below_blocks(half, row, col):
    return (row // half % 2 == 1) & (col // half == row // half - 1)


def invert_lower(blocks):
    size = blocks[0].shape[0]
    row, col = grid_ids(size)
    inverses = []
    for block in blocks:
        diag = jnp.where(row == col, block, 0.0)
        down = 1.0 / jnp.sum(diag, axis=1, keepdims=True)
        across = 1.0 / jnp.sum(diag, axis=0, keepdims=True)
        below = below_blocks(1, row, col)
        inverses.append(
            jnp.where(row == col, down, 0.0) - jnp.where(below, down * block * across, 0.0)
        )
    half = 2
    while half < size:
        below = below_blocks(half, row, col)
        inner = [
            dot32(jnp.where(below, block, 0.0), inverse) for block, inverse in zip(blocks, inverses)
        ]
        inverses = [inverse - dot32(inverse, part) for inverse, part in zip(inverses, inner)]
        half *= 2
    return inverses


def prepare_kernel(rows, block, depth, me, place, source, out, factor, sem):
    width = depth // 2
    load = pltpu.make_async_copy(source, factor, sem)
    load.start()
    load.wait()
    out[...] = factor[:, width:]
    first = me[0] * rows

    @pl.when((place[0] == 0) & (first < depth))
    def _():
        blocks = []
        for j in range(0, rows, block):
            at = jnp.minimum(first + j, depth - block)
            near = pl.multiple_of(at // LANES * LANES, LANES)
            value = factor[j : j + block, pl.ds(near, LANES)]
            value = pltpu.roll(value, (LANES - at % LANES) % LANES, 1)
            blocks.append(value[:, :block])
        row, col = grid_ids(block)
        blocks = [
            jnp.where(first + i * block < depth, value, jnp.where(row == col, 1.0, 0.0))
            for i, value in enumerate(blocks)
        ]
        for i, inverse in enumerate(invert_lower(blocks)):

            @pl.when(first + i * block < depth)
            def _(i=i, inverse=inverse):
                out[i * block : (i + 1) * block, width - block :] = inverse


def prepare(me, place, factor, block):
    rows, depth = factor.shape
    return pl.pallas_call(
        functools.partial(prepare_kernel, rows, block, depth),
        out_shape=jax.ShapeDtypeStruct((rows, depth // 2), jnp.float32),
        in_specs=[SCALARS] * 2 + [ANY],
        out_specs=WHOLE,
        scratch_shapes=[pltpu.VMEM((rows, depth), jnp.float32), pltpu.SemaphoreType.DMA],
        compiler_params=pltpu.CompilerParams(vmem_limit_bytes=VMEM_BYTES),
        cost_estimate=pl.CostEstimate(
            flops=24 * rows * block * block, bytes_accessed=6 * rows * depth, transcendentals=0
        ),
    )(me, place, factor)


def solve_kernel(pieces, rows, width, chunk, block, panel, ids, place, *refs):
    held, refs = refs[: 2 * pieces], refs[2 * pieces :]
    rhs, refs = refs[0], refs[1:]
    earlier, refs = refs[:panel], refs[panel:]
    solved, lower, piece_sem, rhs_sem = refs
    first, last = panel * width, (panel + 1) * width
    side = lower.shape[1] - LANES

    @pl.when(place[0] == 0)
    def _():
        def copies(i):
            at = pl.ds(pl.multiple_of(ids[i] * rows, 8), rows)
            cut = 0 if panel else width - LANES
            return [
                pltpu.make_async_copy(
                    held[i], lower.at[at, pl.ds(0, width)], piece_sem.at[0, i]
                ),
                pltpu.make_async_copy(
                    held[pieces + i].at[:, pl.ds(cut, width - cut)],
                    lower.at[at, pl.ds(width, width - cut)],
                    piece_sem.at[1, i],
                ),
            ]

        def needed(i):
            return (ids[i] * rows < last) & ((ids[i] + 1) * rows > first)

        for i in range(pieces):

            @pl.when(needed(i))
            def _(i=i):
                for copy in copies(i):
                    copy.start()

        load = pltpu.make_async_copy(rhs.at[pl.ds(first, width)], solved, rhs_sem)
        load.start()
        for i in range(pieces):

            @pl.when(needed(i))
            def _(i=i):
                for copy in copies(i):
                    copy.wait()

        load.wait()
        row, col = grid_ids(chunk)
        lane = lax.broadcasted_iota(jnp.int32, (chunk, LANES), 1)
        starts = range(0, width, chunk)
        inverses = []
        for j in starts:
            value = lower[first + j : first + j + chunk, side:]
            value = jnp.where(lane >= LANES - block, value, 0.0)
            shift = block
            while shift < LANES:
                value = value + pltpu.roll(value, LANES - shift, 1)
                shift *= 2
            value = jnp.concatenate([value] * (chunk // LANES), axis=1)
            inverses.append(jnp.where(row // block == col // block, value, 0.0))
        half = block
        while half < chunk:
            below = below_blocks(half, row, col)
            parts = [split16(inverse) for inverse in inverses]
            inner = [
                dot_split(
                    split16(
                        jnp.where(
                            below,
                            lower[first + j : first + j + chunk, first + j : first + j + chunk],
                            0.0,
                        )
                    ),
                    part,
                )
                for j, part in zip(starts, parts)
            ]
            inverses = [
                inverse - dot_split(part, split16(value))
                for inverse, part, value in zip(inverses, parts, inner)
            ]
            half *= 2
        for k in range(panel):
            solved[...] = solved[...] - dot_split(
                split16(lower[first:last, k * width : (k + 1) * width]), split16(earlier[k][...])
            )
        for j in starts:
            value = solved[j : j + chunk]
            if j:
                at = slice(first + j, first + j + chunk)
                value = value - dot_split(
                    split16(lower[at, first : first + j]), split16(solved[:j])
                )
            solved[j : j + chunk] = dot_split(split16(inverses[j // chunk]), split16(value))


def solve_panel(panel, ids, place, held, rhs, earlier, width, block):
    pieces = len(held[0])
    rows = held[0][0].shape[0]
    columns = rhs.shape[1]
    tall = -(-(panel + 1) * width // rows) * rows
    chunk = math.gcd(width, 2 * LANES)
    return pl.pallas_call(
        functools.partial(solve_kernel, pieces, rows, width, chunk, block, panel),
        out_shape=jax.ShapeDtypeStruct((width, columns), jnp.float32),
        in_specs=[SCALARS] * 2 + [ANY] * (2 * pieces + 1) + [WHOLE] * panel,
        out_specs=WHOLE,
        scratch_shapes=[
            pltpu.VMEM((tall, 2 * width if panel else width + LANES), jnp.float32),
            pltpu.SemaphoreType.DMA((2, pieces)),
            pltpu.SemaphoreType.DMA,
        ],
        compiler_params=pltpu.CompilerParams(vmem_limit_bytes=VMEM_BYTES),
        cost_estimate=pl.CostEstimate(
            flops=6 * (panel + 1) * width * width * columns,
            bytes_accessed=12 * width * columns,
            transcendentals=0,
        ),
    )(ids, place, *held[0], *held[1], rhs, *earlier)


def update_kernel(pieces, rows, width, tile, step, places, behind, ids, place, *refs):
    held, refs = refs[: 4 * pieces], refs[4 * pieces :]
    rhs, refs = refs[0], refs[1:]
    solved, refs = refs[: 2 * places], refs[2 * places :]
    refs = refs[len(refs) - 11 :]
    out, lower, block, found, high, low, product, piece_sem, block_sem, found_sem, out_sem = refs
    depth = 2 * width
    start = place[0] * rhs.shape[0]

    def fetch(k, r):
        return pltpu.make_async_copy(
            solved[k * places + r], found.at[pl.ds(k * width, width)], found_sem.at[k]
        )

    def at(i):
        return pl.ds(pl.multiple_of(ids[i] * rows, 8), rows)

    def load(k, i, source):
        return pltpu.make_async_copy(
            held[source], lower.at[i, :, pl.ds(k * width, width)], piece_sem.at[k, i]
        )

    def load_block(i):
        return pltpu.make_async_copy(rhs.at[at(i)], block.at[i], block_sem.at[i])

    def store(i):
        return pltpu.make_async_copy(block.at[i], out.at[at(i)], out_sem.at[i])

    for r in range(places):

        @pl.when(place[0] == r)
        def _(r=r):
            for k in range(2):
                fetch(k, r).start()

    for group in range(2):

        @pl.when((place[0] == behind) == (group == 1))
        def _(group=group):
            for i in range(pieces):
                for k in range(2):
                    load(k, i, (2 * group + k) * pieces + i).start()

    for i in range(pieces):
        load_block(i).start()
    for k in range(2):
        fetch(k, 0).wait()
    high[...], low[...] = split16(found[...])

    @pl.loop(0, pieces)
    def _(i):
        for k in range(2):
            load(k, i, 0).wait()
        load_block(i).wait()

        @pl.loop(0, rows // tile)
        def _(t):
            inside = pl.multiple_of(t * tile, 8)
            top = start + ids[i] * rows + inside
            product[...] = dot_split(
                split16(lower[i, pl.ds(inside, tile)]), (high[...], low[...])
            )

            @pl.when(top >= depth)
            def _():
                block[i, pl.ds(inside, tile)] = block[i, pl.ds(inside, tile)] - product[...]

            @pl.when(top < depth)
            def _():
                @pl.loop(0, tile // step)
                def _(u):
                    part = pl.multiple_of(u * step, 8)
                    row = top + part
                    here = pl.ds(inside + part, step)

                    @pl.when(row < depth)
                    def _():
                        block[i, here] = found[pl.ds(pl.multiple_of(row, 8), step)]

                    @pl.when(row >= depth)
                    def _():
                        block[i, here] = block[i, here] - product[pl.ds(part, step)]

        store(i).start()

    @pl.loop(0, pieces)
    def _(i):
        store(i).wait()


def update(ids, place, held, rhs, solved, width, behind, written=None):
    pieces, places = len(held[0]), len(solved[0])
    rows, columns = held[0][0].shape[0], rhs.shape[1]
    step = math.gcd(rows, 2 * width)
    tile = step * max(m for m in range(1, rows // step + 1) if rows // step % m == 0 and step * m <= 512)
    operands = [ids, place, *[piece for group in held for piece in group], rhs, *solved[0], *solved[1]]
    extra = [] if written is None else [written]
    return pl.pallas_call(
        functools.partial(update_kernel, pieces, rows, width, tile, step, places, behind),
        out_shape=jax.ShapeDtypeStruct(rhs.shape, jnp.float32),
        in_specs=[SCALARS] * 2 + [ANY] * (len(operands) - 2 + len(extra)),
        out_specs=ANY,
        input_output_aliases={len(operands): 0} if extra else {},
        scratch_shapes=[
            pltpu.VMEM((pieces, rows, 2 * width), jnp.float32),
            pltpu.VMEM((pieces, rows, columns), jnp.float32),
            pltpu.VMEM((2 * width, columns), jnp.float32),
            pltpu.VMEM((2 * width, columns), jnp.bfloat16),
            pltpu.VMEM((2 * width, columns), jnp.bfloat16),
            pltpu.VMEM((tile, columns), jnp.float32),
            pltpu.SemaphoreType.DMA((2, pieces)),
            pltpu.SemaphoreType.DMA((pieces,)),
            pltpu.SemaphoreType.DMA((2,)),
            pltpu.SemaphoreType.DMA((pieces,)),
        ],
        compiler_params=pltpu.CompilerParams(vmem_limit_bytes=VMEM_BYTES),
        cost_estimate=pl.CostEstimate(
            flops=12 * pieces * rows * width * columns,
            bytes_accessed=8 * pieces * rows * (width + columns),
            transcendentals=0,
        ),
    )(*operands, *extra)


def gate_kernel(first, second, token, first_out, second_out):
    pass


def gate(panels, token):
    return pl.pallas_call(
        gate_kernel,
        out_shape=[jax.ShapeDtypeStruct(panel.shape, panel.dtype) for panel in panels],
        in_specs=[ANY] * 3,
        out_specs=[ANY] * 2,
        input_output_aliases={0: 0, 1: 1},
        compiler_params=pltpu.CompilerParams(vmem_limit_bytes=VMEM_BYTES),
    )(*panels, token)


def ring_steps(panels, ring, members, number):
    count = len(ring)
    ways = [
        [(number(ring[i], r), number(ring[(i + way) % count], r)) for i in range(count) for r in members]
        for way in (1, -1)
    ]
    going = [[panel, panel] for panel in panels]
    for step in range(1, count // 2 + 1):
        arrived = [[], []]
        for k in range(2):
            for way in range(2):
                if step == count // 2 and way != k:
                    continue
                going[k][way] = lax.ppermute(going[k][way], number.axes, ways[way])
                arrived[k].append(going[k][way])
        yield arrived


class Number:
    def __init__(self, mesh):
        self.axes = tuple(mesh.axis_names)
        self.shape = dict(mesh.shape)

    def __call__(self, source, row):
        at = {"src": source, "row": row}
        place = 0
        for axis in self.axes:
            place = place * self.shape[axis] + at[axis]
        return place


def spread_rows(block, count):
    found = {0: block}
    stride = count // 2
    while stride:
        for r in list(found):
            found[r + stride] = lax.ppermute(found[r], "row", [(r, r + stride)])
        stride //= 2
    return [found[r] for r in range(count)]


def solution(mesh):
    count, places = mesh.shape["src"], mesh.shape["row"]
    number = Number(mesh)
    behind = 1

    def local(factor, right_side):
        rows, depth = factor.shape
        width = depth // 2
        block = math.gcd(math.gcd(rows, width), LANES)
        me = lax.axis_index("src").reshape(1).astype(jnp.int32)
        place = lax.axis_index("row").reshape(1).astype(jnp.int32)
        panels = [factor[:, :width], prepare(me, place, factor, block)]
        if count % 2 or count > RING_LIMIT or places < 2:
            held = [[lax.all_gather(panel, "src", axis=0, tiled=True)] for panel in panels]
            late, ids, cut = held, jnp.zeros_like(me), 1
        else:
            ring = list(range(0, count, 2)) + list(range(count - 1, 0, -2))
            spot = jnp.where(me % 2 == 0, me // 2, count - 1 - me // 2)
            half = count // 2
            away = [0] + [d for step in range(1, half) for d in (-step, step)] + [half]
            spot = (spot + jnp.array(away, jnp.int32) + count) % count
            ids = jnp.where(spot < half, 2 * spot, 2 * (count - 1 - spot) + 1)
            held = [[panel] for panel in panels]
            ahead = [r for r in range(places) if r != behind]
            for step, arrived in enumerate(ring_steps(panels, ring, ahead, number)):
                for k in range(2):
                    held[k] += arrived[k]
                if step == TOKEN_STEP:
                    token = lax.ppermute(arrived[0][0][:8, :LANES], "row", [(0, behind)])
            late = [[panel] for panel in panels]
            for arrived in ring_steps(gate(panels, token), ring, [behind], number):
                for k in range(2):
                    late[k] += arrived[k]
            cut = 5
        first = solve_panel(0, ids, place, held, right_side, [], width, block)
        second = solve_panel(1, ids, place, held, right_side, [first], width, block)
        solved = [spread_rows(first, places), spread_rows(second, places)]
        result = None
        for part in (slice(0, cut), slice(cut, None)):
            group = [pieces[part] for pieces in held + late]
            if group[0]:
                result = update(ids[part], place, group, right_side, solved, width, behind, result)
        return result

    placed = (P(("row", "src"), None), P("row", "src"))
    return jax.shard_map(
        local, mesh=mesh, in_specs=placed, out_specs=P("row", "src"), check_vma=False
    )
```

```python
import functools
import math

import jax
import jax.numpy as jnp
from jax import lax
from jax.experimental import pallas as pl
from jax.experimental.pallas import tpu as pltpu
from jax.sharding import PartitionSpec as P

VMEM_BYTES = 52 * 1024 * 1024
LANES = 128
RING_LIMIT = 16

ANY = pl.BlockSpec(memory_space=pl.ANY)
SCALARS = pl.BlockSpec(memory_space=pltpu.SMEM)
WHOLE = pl.BlockSpec(memory_space=pltpu.VMEM)


def dot32(a, b):
    return jnp.dot(a, b, preferred_element_type=jnp.float32, precision=lax.Precision.HIGHEST)


def split16(value):
    high = value.astype(jnp.bfloat16)
    return high, (value - high.astype(jnp.float32)).astype(jnp.bfloat16)


def dot_split(a, b):
    (a_high, a_low), (b_high, b_low) = a, b
    dot = functools.partial(jnp.dot, preferred_element_type=jnp.float32)
    return dot(a_high, b_high) + dot(a_high, b_low) + dot(a_low, b_high)


def grid_ids(size):
    return [lax.broadcasted_iota(jnp.int32, (size, size), axis) for axis in range(2)]


def below_blocks(half, row, col):
    return (row // half % 2 == 1) & (col // half == row // half - 1)


def invert_lower(blocks):
    size = blocks[0].shape[0]
    row, col = grid_ids(size)
    inverses = []
    for block in blocks:
        diag = jnp.where(row == col, block, 0.0)
        down = 1.0 / jnp.sum(diag, axis=1, keepdims=True)
        across = 1.0 / jnp.sum(diag, axis=0, keepdims=True)
        below = below_blocks(1, row, col)
        inverses.append(
            jnp.where(row == col, down, 0.0) - jnp.where(below, down * block * across, 0.0)
        )
    half = 2
    while half < size:
        below = below_blocks(half, row, col)
        inner = [
            dot32(jnp.where(below, block, 0.0), inverse) for block, inverse in zip(blocks, inverses)
        ]
        inverses = [inverse - dot32(inverse, part) for inverse, part in zip(inverses, inner)]
        half *= 2
    return inverses


def prepare_kernel(rows, block, depth, me, place, source, out, factor, sem):
    width = depth // 2
    load = pltpu.make_async_copy(source, factor, sem)
    load.start()
    load.wait()
    out[...] = factor[:, width:]
    first = me[0] * rows

    @pl.when((place[0] == 0) & (first < depth))
    def _():
        blocks = []
        for j in range(0, rows, block):
            at = jnp.minimum(first + j, depth - block)
            near = pl.multiple_of(at // LANES * LANES, LANES)
            value = factor[j : j + block, pl.ds(near, LANES)]
            value = pltpu.roll(value, (LANES - at % LANES) % LANES, 1)
            blocks.append(value[:, :block])
        row, col = grid_ids(block)
        blocks = [
            jnp.where(first + i * block < depth, value, jnp.where(row == col, 1.0, 0.0))
            for i, value in enumerate(blocks)
        ]
        for i, inverse in enumerate(invert_lower(blocks)):

            @pl.when(first + i * block < depth)
            def _(i=i, inverse=inverse):
                out[i * block : (i + 1) * block, width - block :] = inverse


def prepare(me, place, factor, block):
    rows, depth = factor.shape
    return pl.pallas_call(
        functools.partial(prepare_kernel, rows, block, depth),
        out_shape=jax.ShapeDtypeStruct((rows, depth // 2), jnp.float32),
        in_specs=[SCALARS] * 2 + [ANY],
        out_specs=WHOLE,
        scratch_shapes=[pltpu.VMEM((rows, depth), jnp.float32), pltpu.SemaphoreType.DMA],
        compiler_params=pltpu.CompilerParams(vmem_limit_bytes=VMEM_BYTES),
        cost_estimate=pl.CostEstimate(
            flops=24 * rows * block * block, bytes_accessed=6 * rows * depth, transcendentals=0
        ),
    )(me, place, factor)


def solve_kernel(pieces, rows, width, chunk, block, panel, ids, place, *refs):
    held, refs = refs[: 2 * pieces], refs[2 * pieces :]
    rhs, refs = refs[0], refs[1:]
    earlier, refs = refs[:panel], refs[panel:]
    solved, lower, piece_sem, rhs_sem = refs
    first, last = panel * width, (panel + 1) * width
    side = lower.shape[1] - LANES

    @pl.when(place[0] == 0)
    def _():
        def copies(i):
            at = pl.ds(pl.multiple_of(ids[i] * rows, 8), rows)
            cut = 0 if panel else width - LANES
            return [
                pltpu.make_async_copy(
                    held[i], lower.at[at, pl.ds(0, width)], piece_sem.at[0, i]
                ),
                pltpu.make_async_copy(
                    held[pieces + i].at[:, pl.ds(cut, width - cut)],
                    lower.at[at, pl.ds(width, width - cut)],
                    piece_sem.at[1, i],
                ),
            ]

        def needed(i):
            return (ids[i] * rows < last) & ((ids[i] + 1) * rows > first)

        for i in range(pieces):

            @pl.when(needed(i))
            def _(i=i):
                for copy in copies(i):
                    copy.start()

        load = pltpu.make_async_copy(rhs.at[pl.ds(first, width)], solved, rhs_sem)
        load.start()
        for i in range(pieces):

            @pl.when(needed(i))
            def _(i=i):
                for copy in copies(i):
                    copy.wait()

        load.wait()
        row, col = grid_ids(chunk)
        lane = lax.broadcasted_iota(jnp.int32, (chunk, LANES), 1)
        starts = range(0, width, chunk)
        inverses = []
        for j in starts:
            value = lower[first + j : first + j + chunk, side:]
            value = jnp.where(lane >= LANES - block, value, 0.0)
            shift = block
            while shift < LANES:
                value = value + pltpu.roll(value, LANES - shift, 1)
                shift *= 2
            value = jnp.concatenate([value] * (chunk // LANES), axis=1)
            inverses.append(jnp.where(row // block == col // block, value, 0.0))
        half = block
        while half < chunk:
            below = below_blocks(half, row, col)
            parts = [split16(inverse) for inverse in inverses]
            inner = [
                dot_split(
                    split16(
                        jnp.where(
                            below,
                            lower[first + j : first + j + chunk, first + j : first + j + chunk],
                            0.0,
                        )
                    ),
                    part,
                )
                for j, part in zip(starts, parts)
            ]
            inverses = [
                inverse - dot_split(part, split16(value))
                for inverse, part, value in zip(inverses, parts, inner)
            ]
            half *= 2
        for k in range(panel):
            solved[...] = solved[...] - dot_split(
                split16(lower[first:last, k * width : (k + 1) * width]), split16(earlier[k][...])
            )
        for j in starts:
            value = solved[j : j + chunk]
            if j:
                at = slice(first + j, first + j + chunk)
                value = value - dot_split(
                    split16(lower[at, first : first + j]), split16(solved[:j])
                )
            solved[j : j + chunk] = dot_split(split16(inverses[j // chunk]), split16(value))


def solve_panel(panel, ids, place, held, rhs, earlier, width, block):
    pieces = len(held[0])
    rows = held[0][0].shape[0]
    columns = rhs.shape[1]
    tall = -(-(panel + 1) * width // rows) * rows
    chunk = math.gcd(width, 2 * LANES)
    return pl.pallas_call(
        functools.partial(solve_kernel, pieces, rows, width, chunk, block, panel),
        out_shape=jax.ShapeDtypeStruct((width, columns), jnp.float32),
        in_specs=[SCALARS] * 2 + [ANY] * (2 * pieces + 1) + [WHOLE] * panel,
        out_specs=WHOLE,
        scratch_shapes=[
            pltpu.VMEM((tall, 2 * width if panel else width + LANES), jnp.float32),
            pltpu.SemaphoreType.DMA((2, pieces)),
            pltpu.SemaphoreType.DMA,
        ],
        compiler_params=pltpu.CompilerParams(vmem_limit_bytes=VMEM_BYTES),
        cost_estimate=pl.CostEstimate(
            flops=6 * (panel + 1) * width * width * columns,
            bytes_accessed=12 * width * columns,
            transcendentals=0,
        ),
    )(ids, place, *held[0], *held[1], rhs, *earlier)


def update_kernel(pieces, rows, width, tile, step, places, panel, ids, place, *refs):
    held, refs = refs[:pieces], refs[pieces:]
    current, refs = refs[0], refs[1:]
    solved, refs = refs[:places], refs[places:]
    out, lower, block, found, high, low, product, piece_sem, block_sem, found_sem, out_sem = refs
    first, last = panel * width, (panel + 1) * width
    start = place[0] * current.shape[0]

    def fetch(r):
        return pltpu.make_async_copy(solved[r], found, found_sem)

    for r in range(places):

        @pl.when(place[0] == r)
        def _(r=r):
            fetch(r).start()

    def at(i):
        return pl.ds(pl.multiple_of(ids[i] * rows, 8), rows)

    def loads(i, source):
        return [
            pltpu.make_async_copy(held[source], lower.at[i], piece_sem.at[i]),
            pltpu.make_async_copy(current.at[at(i)], block.at[i], block_sem.at[i]),
        ]

    def store(i):
        return pltpu.make_async_copy(block.at[i], out.at[at(i)], out_sem.at[i])

    for i in range(pieces):
        for load in loads(i, i):
            load.start()
    fetch(0).wait()
    high[...], low[...] = split16(found[...])

    @pl.loop(0, pieces)
    def _(i):
        for load in loads(i, 0):
            load.wait()

        @pl.loop(0, rows // tile)
        def _(t):
            inside = pl.multiple_of(t * tile, 8)
            top = start + ids[i] * rows + inside
            product[...] = dot_split(
                split16(lower[i, pl.ds(inside, tile)]), (high[...], low[...])
            )

            @pl.when(top >= last)
            def _():
                block[i, pl.ds(inside, tile)] = block[i, pl.ds(inside, tile)] - product[...]

            @pl.when(top < last)
            def _():
                @pl.loop(0, tile // step)
                def _(u):
                    part = pl.multiple_of(u * step, 8)
                    row = top + part
                    here = pl.ds(inside + part, step)

                    @pl.when((row >= first) & (row < last))
                    def _():
                        block[i, here] = found[pl.ds(pl.multiple_of(row - first, 8), step)]

                    @pl.when(row >= last)
                    def _():
                        block[i, here] = block[i, here] - product[pl.ds(part, step)]

        store(i).start()

    @pl.loop(0, pieces)
    def _(i):
        store(i).wait()


def update(panel, ids, place, held, current, solved, width):
    pieces, places = len(held), len(solved)
    rows, columns = held[0].shape[0], current.shape[1]
    step = math.gcd(rows, width)
    tile = step * max(m for m in range(1, rows // step + 1) if rows // step % m == 0 and step * m <= 512)
    return pl.pallas_call(
        functools.partial(update_kernel, pieces, rows, width, tile, step, places, panel),
        out_shape=jax.ShapeDtypeStruct(current.shape, jnp.float32),
        in_specs=[SCALARS] * 2 + [ANY] * (pieces + 1 + places),
        out_specs=ANY,
        scratch_shapes=[
            pltpu.VMEM((pieces, rows, width), jnp.float32),
            pltpu.VMEM((pieces, rows, columns), jnp.float32),
            pltpu.VMEM((width, columns), jnp.float32),
            pltpu.VMEM((width, columns), jnp.bfloat16),
            pltpu.VMEM((width, columns), jnp.bfloat16),
            pltpu.VMEM((tile, columns), jnp.float32),
            pltpu.SemaphoreType.DMA((pieces,)),
            pltpu.SemaphoreType.DMA((pieces,)),
            pltpu.SemaphoreType.DMA,
            pltpu.SemaphoreType.DMA((pieces,)),
        ],
        compiler_params=pltpu.CompilerParams(vmem_limit_bytes=VMEM_BYTES),
        cost_estimate=pl.CostEstimate(
            flops=6 * pieces * rows * width * columns,
            bytes_accessed=4 * pieces * rows * (width + 2 * columns),
            transcendentals=0,
        ),
    )(ids, place, *held, current, *solved)


def gate_kernel(block, token, out):
    pass


def gate(block, token):
    return pl.pallas_call(
        gate_kernel,
        out_shape=jax.ShapeDtypeStruct(block.shape, block.dtype),
        in_specs=[ANY] * 2,
        out_specs=ANY,
        input_output_aliases={0: 0},
        compiler_params=pltpu.CompilerParams(vmem_limit_bytes=VMEM_BYTES),
    )(block, token)


def gather_pieces(panels, count):
    me = lax.axis_index("src")
    if count % 2 or count > RING_LIMIT:
        gathered = [lax.all_gather(panel, "src", axis=0, tiled=True) for panel in panels]
        return [[piece] for piece in gathered], [jnp.zeros_like(me)]
    ring = list(range(0, count, 2)) + list(range(count - 1, 0, -2))
    onward = [(ring[i], ring[(i + 1) % count]) for i in range(count)]
    back = [(b, a) for a, b in onward]
    position = jnp.where(me % 2 == 0, me // 2, count - 1 - me // 2)

    def shard_at(spot):
        spot = (spot + count) % count
        return jnp.where(spot < count // 2, 2 * spot, 2 * (count - 1 - spot) + 1)

    held = [[panel] for panel in panels]
    ids = [me]
    going = [[panel, panel] for panel in panels]
    for step in range(1, count // 2 + 1):
        last = step == count // 2
        for k in range(2):
            for way, pairs in enumerate((onward, back)):
                if last and way != k:
                    continue
                going[k][way] = lax.ppermute(going[k][way], "src", pairs)
                held[k].append(going[k][way])
        ids += [shard_at(position - step)] + ([] if last else [shard_at(position + step)])
    return held, ids


def spread_far(block, count):
    found = {0: block}
    stride = count // 2
    while stride > 1:
        for r in list(found):
            found[r + stride] = lax.ppermute(found[r], "row", [(r, r + stride)])
        stride //= 2
    return found


def spread_near(found, count, token=None):
    found = dict(found)
    for r in sorted(found):
        if r and token is not None:
            found[r] = gate(found[r], token)
        if r + 1 < count:
            found[r + 1] = lax.ppermute(found[r], "row", [(r, r + 1)])
    return [found[r] for r in range(count)]


def solution(mesh):
    sources, places = mesh.shape["src"], mesh.shape["row"]

    def local(factor, right_side):
        rows, depth = factor.shape
        width = depth // 2
        block = math.gcd(math.gcd(rows, width), LANES)
        me = lax.axis_index("src").reshape(1).astype(jnp.int32)
        place = lax.axis_index("row").reshape(1).astype(jnp.int32)
        panels = [factor[:, :width], prepare(me, place, factor, block)]
        held, ids = gather_pieces(panels, sources)
        ids = jnp.stack(ids).astype(jnp.int32)
        first = solve_panel(0, ids, place, held, right_side, [], width, block)
        second = solve_panel(1, ids, place, held, right_side, [first], width, block)
        near = spread_near(spread_far(first, places), places)
        far = spread_far(second, places)
        current = update(0, ids, place, held[0], right_side, near, width)
        return update(1, ids, place, held[1], current, spread_near(far, places, current), width)

    placed = (P(("row", "src"), None), P("row", "src"))
    return jax.shard_map(
        local, mesh=mesh, in_specs=placed, out_specs=P("row", "src"), check_vma=False
    )
```

```python
import functools
import math

import jax
import jax.numpy as jnp
from jax import lax
from jax.experimental import pallas as pl
from jax.experimental.pallas import tpu as pltpu
from jax.sharding import PartitionSpec as P

VMEM_BYTES = 52 * 1024 * 1024
LANES = 128
SHORT = pl.CostEstimate(flops=1000, bytes_accessed=1000, transcendentals=0)
RING_LIMIT = 16

ANY = pl.BlockSpec(memory_space=pltpu.HBM)
SCALARS = pl.BlockSpec(memory_space=pltpu.SMEM)
WHOLE = pl.BlockSpec(memory_space=pltpu.VMEM)


def dot32(a, b):
    return jnp.dot(a, b, preferred_element_type=jnp.float32, precision=lax.Precision.HIGHEST)


def split16(value):
    high = value.astype(jnp.bfloat16)
    return high, (value - high.astype(jnp.float32)).astype(jnp.bfloat16)


def dot_split(a, b):
    (a_high, a_low), (b_high, b_low) = a, b
    dot = functools.partial(jnp.dot, preferred_element_type=jnp.float32)
    return dot(a_high, b_high) + dot(a_high, b_low) + dot(a_low, b_high)


def grid_ids(size):
    return [lax.broadcasted_iota(jnp.int32, (size, size), axis) for axis in range(2)]


def below_blocks(half, row, col):
    return (row // half % 2 == 1) & (col // half == row // half - 1)


def invert_lower(blocks):
    size = blocks[0].shape[0]
    row, col = grid_ids(size)
    inverses = []
    for block in blocks:
        diag = jnp.where(row == col, block, 0.0)
        down = 1.0 / jnp.sum(diag, axis=1, keepdims=True)
        across = 1.0 / jnp.sum(diag, axis=0, keepdims=True)
        below = below_blocks(1, row, col)
        inverses.append(
            jnp.where(row == col, down, 0.0) - jnp.where(below, down * block * across, 0.0)
        )
    half = 2
    while half < size:
        below = below_blocks(half, row, col)
        inner = [
            dot32(jnp.where(below, block, 0.0), inverse) for block, inverse in zip(blocks, inverses)
        ]
        inverses = [inverse - dot32(inverse, part) for inverse, part in zip(inverses, inner)]
        half *= 2
    return inverses


def prepare_kernel(rows, block, depth, cuts, movers, me, place, source, *refs):
    *outs, factor, load_sem, store_sem = refs
    width, part = depth // 2, rows // cuts
    load = pltpu.make_async_copy(source, factor, load_sem)
    load.start()
    load.wait()
    first = me[0] * rows

    @pl.when((place[0] == 0) & (first < depth))
    def _():
        blocks = []
        for j in range(0, rows, block):
            at = jnp.minimum(first + j, depth - block)
            near = pl.multiple_of(at // LANES * LANES, LANES)
            value = factor[j : j + block, pl.ds(near, LANES)]
            value = pltpu.roll(value, (LANES - at % LANES) % LANES, 1)
            blocks.append(value[:, :block])
        row, col = grid_ids(block)
        blocks = [
            jnp.where(first + i * block < depth, value, jnp.where(row == col, 1.0, 0.0))
            for i, value in enumerate(blocks)
        ]
        for i, inverse in enumerate(invert_lower(blocks)):

            @pl.when(first + i * block < depth)
            def _(i=i, inverse=inverse):
                factor[i * block : (i + 1) * block, depth - block :] = inverse

    moves = me[0] < movers
    copies = []
    for k in range(2):
        panel = pl.ds(k * width, width)
        for cut in range(cuts):
            at = pl.ds(cut * part, part)
            copies.append((factor.at[at, panel], outs[2 * cut + k], store_sem.at[2 * cut + k]))
        if cuts > 1:
            sent = pl.ds(pl.multiple_of(jnp.where(moves, part, 0), 8), part)
            copies.append((factor.at[sent, panel], outs[4 + k], store_sem.at[4 + k]))
    copies = [pltpu.make_async_copy(*copy) for copy in copies]
    for copy in copies:
        copy.start()
    for copy in copies:
        copy.wait()


def prepare(me, place, factor, block, cuts, movers):
    rows, depth = factor.shape
    count = 2 * cuts + (2 if cuts > 1 else 0)
    return pl.pallas_call(
        functools.partial(prepare_kernel, rows, block, depth, cuts, movers),
        out_shape=[jax.ShapeDtypeStruct((rows // cuts, depth // 2), jnp.float32)] * count,
        in_specs=[SCALARS] * 2 + [ANY],
        out_specs=[ANY] * count,
        scratch_shapes=[
            pltpu.VMEM((rows, depth), jnp.float32),
            pltpu.SemaphoreType.DMA,
            pltpu.SemaphoreType.DMA((count,)),
        ],
        compiler_params=pltpu.CompilerParams(vmem_limit_bytes=VMEM_BYTES),
        cost_estimate=SHORT,
    )(me, place, factor)


def solve_kernel(pieces, rows, width, chunk, block, panel, ids, place, *refs):
    held, refs = refs[: 2 * pieces], refs[2 * pieces :]
    rhs, refs = refs[0], refs[1:]
    earlier, refs = refs[:panel], refs[panel:]
    solved, lower, piece_sem, rhs_sem = refs
    first, last = panel * width, (panel + 1) * width
    side = lower.shape[1] - LANES

    @pl.when(place[0] == 0)
    def _():
        def copies(i):
            at = pl.ds(pl.multiple_of(ids[i] * rows, 8), rows)
            cut = 0 if panel else width - LANES
            return [
                pltpu.make_async_copy(
                    held[i], lower.at[at, pl.ds(0, width)], piece_sem.at[0, i]
                ),
                pltpu.make_async_copy(
                    held[pieces + i].at[:, pl.ds(cut, width - cut)],
                    lower.at[at, pl.ds(width, width - cut)],
                    piece_sem.at[1, i],
                ),
            ]

        def needed(i):
            return (ids[i] * rows < last) & ((ids[i] + 1) * rows > first)

        for i in range(pieces):

            @pl.when(needed(i))
            def _(i=i):
                for copy in copies(i):
                    copy.start()

        load = pltpu.make_async_copy(rhs.at[pl.ds(first, width)], solved, rhs_sem)
        load.start()
        for i in range(pieces):

            @pl.when(needed(i))
            def _(i=i):
                for copy in copies(i):
                    copy.wait()

        load.wait()
        row, col = grid_ids(chunk)
        lane = lax.broadcasted_iota(jnp.int32, (chunk, LANES), 1)
        starts = range(0, width, chunk)
        inverses = []
        for j in starts:
            value = lower[first + j : first + j + chunk, side:]
            value = jnp.where(lane >= LANES - block, value, 0.0)
            shift = block
            while shift < LANES:
                value = value + pltpu.roll(value, LANES - shift, 1)
                shift *= 2
            value = jnp.concatenate([value] * (chunk // LANES), axis=1)
            inverses.append(jnp.where(row // block == col // block, value, 0.0))
        half = block
        while half < chunk:
            below = below_blocks(half, row, col)
            parts = [split16(inverse) for inverse in inverses]
            inner = [
                dot_split(
                    split16(
                        jnp.where(
                            below,
                            lower[first + j : first + j + chunk, first + j : first + j + chunk],
                            0.0,
                        )
                    ),
                    part,
                )
                for j, part in zip(starts, parts)
            ]
            inverses = [
                inverse - dot_split(part, split16(value))
                for inverse, part, value in zip(inverses, parts, inner)
            ]
            half *= 2
        for k in range(panel):
            solved[...] = solved[...] - dot_split(
                split16(lower[first:last, k * width : (k + 1) * width]), split16(earlier[k][...])
            )
        for j in starts:
            value = solved[j : j + chunk]
            if j:
                at = slice(first + j, first + j + chunk)
                value = value - dot_split(
                    split16(lower[at, first : first + j]), split16(solved[:j])
                )
            solved[j : j + chunk] = dot_split(split16(inverses[j // chunk]), split16(value))


def solve_panel(panel, ids, place, held, rhs, earlier, width, block):
    pieces = len(held[0])
    rows = held[0][0].shape[0]
    columns = rhs.shape[1]
    tall = -(-(panel + 1) * width // rows) * rows
    chunk = math.gcd(width, 2 * LANES)
    return pl.pallas_call(
        functools.partial(solve_kernel, pieces, rows, width, chunk, block, panel),
        out_shape=jax.ShapeDtypeStruct((width, columns), jnp.float32),
        in_specs=[SCALARS] * 2 + [ANY] * (2 * pieces + 1) + [WHOLE] * panel,
        out_specs=WHOLE,
        scratch_shapes=[
            pltpu.VMEM((tall, 2 * width if panel else width + LANES), jnp.float32),
            pltpu.SemaphoreType.DMA((2, pieces)),
            pltpu.SemaphoreType.DMA,
        ],
        compiler_params=pltpu.CompilerParams(vmem_limit_bytes=VMEM_BYTES),
        cost_estimate=SHORT,
    )(ids, place, *held[0], *held[1], rhs, *earlier)


def update_kernel(pieces, rows, width, tile, step, places, ids, place, *refs):
    held, refs = refs[: 2 * pieces], refs[2 * pieces :]
    rhs, refs = refs[0], refs[1:]
    solved, refs = refs[: 2 * places], refs[2 * places :]
    refs = refs[len(refs) - 11 :]
    out, lower, block, found, high, low, product, piece_sem, block_sem, found_sem, out_sem = refs
    depth = 2 * width
    start = place[0] * rhs.shape[0]

    def fetch(k, r):
        return pltpu.make_async_copy(
            solved[k * places + r], found.at[pl.ds(k * width, width)], found_sem.at[k]
        )

    def at(i):
        return pl.ds(pl.multiple_of(ids[i] * rows, 8), rows)

    def load(k, i, source):
        return pltpu.make_async_copy(
            held[source], lower.at[i, :, pl.ds(k * width, width)], piece_sem.at[k, i]
        )

    def load_block(i):
        return pltpu.make_async_copy(rhs.at[at(i)], block.at[i], block_sem.at[i])

    def store(i):
        return pltpu.make_async_copy(block.at[i], out.at[at(i)], out_sem.at[i])

    for r in range(places):

        @pl.when(place[0] == r)
        def _(r=r):
            for k in range(2):
                fetch(k, r).start()

    for i in range(pieces):
        for k in range(2):
            load(k, i, k * pieces + i).start()
        load_block(i).start()
    for k in range(2):
        fetch(k, 0).wait()
    high[...], low[...] = split16(found[...])

    @pl.loop(0, pieces)
    def _(i):
        for k in range(2):
            load(k, i, 0).wait()
        load_block(i).wait()

        @pl.loop(0, rows // tile)
        def _(t):
            inside = pl.multiple_of(t * tile, 8)
            top = start + ids[i] * rows + inside
            product[...] = dot_split(
                split16(lower[i, pl.ds(inside, tile)]), (high[...], low[...])
            )

            @pl.when(top >= depth)
            def _():
                block[i, pl.ds(inside, tile)] = block[i, pl.ds(inside, tile)] - product[...]

            @pl.when(top < depth)
            def _():
                @pl.loop(0, tile // step)
                def _(u):
                    part = pl.multiple_of(u * step, 8)
                    row = top + part
                    here = pl.ds(inside + part, step)

                    @pl.when(row < depth)
                    def _():
                        block[i, here] = found[pl.ds(pl.multiple_of(row, 8), step)]

                    @pl.when(row >= depth)
                    def _():
                        block[i, here] = block[i, here] - product[pl.ds(part, step)]

        store(i).start()

    @pl.loop(0, pieces)
    def _(i):
        store(i).wait()


def update(ids, place, held, rhs, solved, width, written=None):
    pieces, places = len(held[0]), len(solved[0])
    rows, columns = held[0][0].shape[0], rhs.shape[1]
    step = math.gcd(rows, 2 * width)
    tile = step * max(m for m in range(1, rows // step + 1) if rows // step % m == 0 and step * m <= 512)
    operands = [ids, place, *[piece for group in held for piece in group], rhs, *solved[0], *solved[1]]
    extra = [] if written is None else [written]
    return pl.pallas_call(
        functools.partial(update_kernel, pieces, rows, width, tile, step, places),
        out_shape=jax.ShapeDtypeStruct(rhs.shape, jnp.float32),
        in_specs=[SCALARS] * 2 + [ANY] * (len(operands) - 2 + len(extra)),
        out_specs=ANY,
        input_output_aliases={len(operands): 0} if extra else {},
        scratch_shapes=[
            pltpu.VMEM((pieces, rows, 2 * width), jnp.float32),
            pltpu.VMEM((pieces, rows, columns), jnp.float32),
            pltpu.VMEM((2 * width, columns), jnp.float32),
            pltpu.VMEM((2 * width, columns), jnp.bfloat16),
            pltpu.VMEM((2 * width, columns), jnp.bfloat16),
            pltpu.VMEM((tile, columns), jnp.float32),
            pltpu.SemaphoreType.DMA((2, pieces)),
            pltpu.SemaphoreType.DMA((pieces,)),
            pltpu.SemaphoreType.DMA((2,)),
            pltpu.SemaphoreType.DMA((pieces,)),
        ],
        compiler_params=pltpu.CompilerParams(vmem_limit_bytes=VMEM_BYTES),
        cost_estimate=SHORT,
    )(*operands, *extra)


def gate_kernel(count, *refs):
    pass


def gate(blocks, token):
    count = len(blocks)
    return pl.pallas_call(
        functools.partial(gate_kernel, count),
        out_shape=[jax.ShapeDtypeStruct(block.shape, block.dtype) for block in blocks],
        in_specs=[ANY] * (count + 1),
        out_specs=[ANY] * count,
        input_output_aliases={i: i for i in range(count)},
        compiler_params=pltpu.CompilerParams(vmem_limit_bytes=VMEM_BYTES),
    )(*blocks, token)


def ring_pass(panels, ring, cut):
    count = len(ring)
    onward = [(ring[i], ring[(i + 1) % count]) for i in range(count)]
    back = [(b, a) for a, b in onward]
    held = [[panel] for panel in panels]
    going = [[panel, panel] for panel in panels]
    for step in range(1, count // 2 + 1):
        for k in range(2):
            for way, pairs in enumerate((onward, back)):
                if step == count // 2 and way != k:
                    continue
                going[k][way] = lax.ppermute(going[k][way], "src", pairs)
                held[k].append(going[k][way])
        if step == cut:
            token = going[0][1]
    return held, token


def spread_far(block, count):
    found = {0: block}
    stride = count // 2
    while stride > 1:
        for r in list(found):
            found[r + stride] = lax.ppermute(found[r], "row", [(r, r + stride)])
        stride //= 2
    return found


def spread_near(found, count, token=None):
    found = dict(found)
    for r in sorted(found):
        if r and token is not None:
            (found[r],) = gate([found[r]], token)
        if r + 1 < count:
            found[r + 1] = lax.ppermute(found[r], "row", [(r, r + 1)])
    return [found[r] for r in range(count)]


def swap_partners(count, tops):
    free = [s for s in range(count) if 2 * s >= tops]
    partners = []
    for s in range(count):
        if 2 * s + 1 < tops:
            pool = [f for f in free if f % 2 == s % 2] or free
            if not pool:
                return None
            partners.append(pool[-1])
            free.remove(pool[-1])
    return partners


def lookup(table, index):
    hit = index[:, None] == jnp.arange(len(table), dtype=jnp.int32)[None, :]
    return jnp.sum(jnp.where(hit, jnp.array(table, jnp.int32)[None, :], 0), axis=1)


def solution(mesh):
    count, places = mesh.shape["src"], mesh.shape["row"]
    axes = tuple(mesh.axis_names)

    def number(source, row):
        at, place = {"src": source, "row": row}, 0
        for axis in axes:
            place = place * mesh.shape[axis] + at[axis]
        return place

    def local(factor, right_side):
        rows, depth = factor.shape
        width, part = depth // 2, rows // 2
        block = math.gcd(math.gcd(rows, width), LANES)
        me = lax.axis_index("src").reshape(1).astype(jnp.int32)
        place = lax.axis_index("row").reshape(1).astype(jnp.int32)
        partners = swap_partners(count, -(-depth // part))
        ringed = count % 2 == 0 and count <= RING_LIMIT and part % 8 == 0 and partners is not None
        if not ringed:
            held = [
                [lax.all_gather(panel, "src", axis=0, tiled=True)]
                for panel in prepare(me, place, factor, block, 1, 0)
            ]
            top, top_spots = held, jnp.zeros_like(me)
            groups = [(held, top_spots)]
        else:
            movers = len(partners)
            *halves, sent_first, sent_second = prepare(me, place, factor, block, 2, movers)
            pairs = [(s, f) for s, f in enumerate(partners)]
            swap = [(number(a, 0), number(b, 0)) for s, f in pairs for a, b in ((s, f), (f, s))]
            got = [lax.ppermute(sent, axes, swap) for sent in (sent_first, sent_second)]
            source = me[0]
            paired = functools.reduce(jnp.logical_or, [source == f for f in partners])
            takes = [(place[0] == 0) & paired, (place[0] == 0) & (source < movers)]
            own = [
                [jnp.where(takes[h], got[k], halves[2 * h + k]) for k in range(2)] for h in range(2)
            ]
            ring = list(range(0, count, 2)) + list(range(count - 1, 0, -2))
            position = jnp.where(source % 2 == 0, source // 2, count - 1 - source // 2)
            half = count // 2
            away = [0] + [d for step in range(1, half) for d in (-step, step)] + [half]
            position = (position + jnp.array(away, jnp.int32) + count) % count
            ids = jnp.where(position < half, 2 * position, 2 * (count - 1 - position) + 1)
            tables = [[2 * s + h for s in range(count)] for h in range(2)]
            for s, f in pairs:
                tables[0][f], tables[1][s] = 2 * s + 1, 2 * f
            spots = [
                jnp.where(place[0] == 0, lookup(tables[h], ids), 2 * ids + h).astype(jnp.int32)
                for h in range(2)
            ]
            top, token = ring_pass(own[0], ring, half - 1)
            rest, _ = ring_pass(gate(own[1], token), ring, half - 1)
            top_spots, cut = spots[0], 2 * half - 3
            groups = [
                (
                    [top[k] + rest[k][:cut] for k in range(2)],
                    jnp.concatenate([spots[0], spots[1][:cut]]),
                ),
                ([rest[k][cut:] for k in range(2)], spots[1][cut:]),
            ]
        first = solve_panel(0, top_spots, place, top, right_side, [], width, block)
        second = solve_panel(1, top_spots, place, top, right_side, [first], width, block)
        solved = [
            spread_near(spread_far(first, places), places, second),
            spread_near(spread_far(second, places), places),
        ]
        result = None
        for held, spots in groups:
            result = update(spots, place, held, right_side, solved, width, result)
        return result

    placed = (P(("row", "src"), None), P("row", "src"))
    return jax.shard_map(
        local, mesh=mesh, in_specs=placed, out_specs=P("row", "src"), check_vma=False
    )
```

```python
import functools
import math

import jax
import jax.numpy as jnp
from jax import lax
from jax.experimental import pallas as pl
from jax.experimental.pallas import tpu as pltpu
from jax.sharding import PartitionSpec as P

VMEM_BYTES = 52 * 1024 * 1024
LANES = 128
SHORT = pl.CostEstimate(flops=1000, bytes_accessed=1000, transcendentals=0)
RING_LIMIT = 16

ANY = pl.BlockSpec(memory_space=pltpu.HBM)
SCALARS = pl.BlockSpec(memory_space=pltpu.SMEM)
WHOLE = pl.BlockSpec(memory_space=pltpu.VMEM)


def dot32(a, b):
    return jnp.dot(a, b, preferred_element_type=jnp.float32, precision=lax.Precision.HIGHEST)


def split16(value):
    high = value.astype(jnp.bfloat16)
    return high, (value - high.astype(jnp.float32)).astype(jnp.bfloat16)


def dot_split(a, b):
    (a_high, a_low), (b_high, b_low) = a, b
    dot = functools.partial(jnp.dot, preferred_element_type=jnp.float32)
    return dot(a_high, b_high) + dot(a_high, b_low) + dot(a_low, b_high)


def grid_ids(size):
    return [lax.broadcasted_iota(jnp.int32, (size, size), axis) for axis in range(2)]


def below_blocks(half, row, col):
    return (row // half % 2 == 1) & (col // half == row // half - 1)


def invert_lower(blocks):
    size = blocks[0].shape[0]
    row, col = grid_ids(size)
    inverses = []
    for block in blocks:
        diag = jnp.where(row == col, block, 0.0)
        down = 1.0 / jnp.sum(diag, axis=1, keepdims=True)
        across = 1.0 / jnp.sum(diag, axis=0, keepdims=True)
        below = below_blocks(1, row, col)
        inverses.append(
            jnp.where(row == col, down, 0.0) - jnp.where(below, down * block * across, 0.0)
        )
    half = 2
    while half < size:
        below = below_blocks(half, row, col)
        inner = [
            dot32(jnp.where(below, block, 0.0), inverse) for block, inverse in zip(blocks, inverses)
        ]
        inverses = [inverse - dot32(inverse, part) for inverse, part in zip(inverses, inner)]
        half *= 2
    return inverses


def prepare_kernel(rows, block, depth, cuts, movers, me, place, source, *refs):
    *outs, factor, load_sem, store_sem = refs
    width, part = depth // 2, rows // cuts
    load = pltpu.make_async_copy(source, factor, load_sem)
    load.start()
    load.wait()
    first = me[0] * rows

    @pl.when((place[0] == 0) & (first < depth))
    def _():
        blocks = []
        for j in range(0, rows, block):
            at = jnp.minimum(first + j, depth - block)
            near = pl.multiple_of(at // LANES * LANES, LANES)
            value = factor[j : j + block, pl.ds(near, LANES)]
            value = pltpu.roll(value, (LANES - at % LANES) % LANES, 1)
            blocks.append(value[:, :block])
        row, col = grid_ids(block)
        blocks = [
            jnp.where(first + i * block < depth, value, jnp.where(row == col, 1.0, 0.0))
            for i, value in enumerate(blocks)
        ]
        for i, inverse in enumerate(invert_lower(blocks)):

            @pl.when(first + i * block < depth)
            def _(i=i, inverse=inverse):
                factor[i * block : (i + 1) * block, depth - block :] = inverse

    moves = me[0] < movers
    copies = []
    for k in range(2):
        panel = pl.ds(k * width, width)
        for cut in range(cuts):
            at = pl.ds(cut * part, part)
            copies.append((factor.at[at, panel], outs[2 * cut + k], store_sem.at[2 * cut + k]))
        if cuts > 1:
            sent = pl.ds(pl.multiple_of(jnp.where(moves, part, 0), 8), part)
            copies.append((factor.at[sent, panel], outs[4 + k], store_sem.at[4 + k]))
    copies = [pltpu.make_async_copy(*copy) for copy in copies]
    for copy in copies:
        copy.start()
    for copy in copies:
        copy.wait()


def prepare(me, place, factor, block, cuts, movers):
    rows, depth = factor.shape
    count = 2 * cuts + (2 if cuts > 1 else 0)
    return pl.pallas_call(
        functools.partial(prepare_kernel, rows, block, depth, cuts, movers),
        out_shape=[jax.ShapeDtypeStruct((rows // cuts, depth // 2), jnp.float32)] * count,
        in_specs=[SCALARS] * 2 + [ANY],
        out_specs=[ANY] * count,
        scratch_shapes=[
            pltpu.VMEM((rows, depth), jnp.float32),
            pltpu.SemaphoreType.DMA,
            pltpu.SemaphoreType.DMA((count,)),
        ],
        compiler_params=pltpu.CompilerParams(vmem_limit_bytes=VMEM_BYTES),
        cost_estimate=SHORT,
    )(me, place, factor)


def solve_kernel(pieces, rows, width, chunk, block, panel, ids, place, *refs):
    held, refs = refs[: 2 * pieces], refs[2 * pieces :]
    rhs, refs = refs[0], refs[1:]
    earlier = refs[:panel]
    solved, lower, piece_sem, rhs_sem = refs[len(refs) - 4 :]
    first, last = panel * width, (panel + 1) * width
    side = lower.shape[1] - LANES

    @pl.when(place[0] == 0)
    def _():
        def copies(i):
            at = pl.ds(pl.multiple_of(ids[i] * rows, 8), rows)
            cut = 0 if panel else width - LANES
            return [
                pltpu.make_async_copy(
                    held[i], lower.at[at, pl.ds(0, width)], piece_sem.at[0, i]
                ),
                pltpu.make_async_copy(
                    held[pieces + i].at[:, pl.ds(cut, width - cut)],
                    lower.at[at, pl.ds(width, width - cut)],
                    piece_sem.at[1, i],
                ),
            ]

        def needed(i):
            return (ids[i] * rows < last) & ((ids[i] + 1) * rows > first)

        for i in range(pieces):

            @pl.when(needed(i))
            def _(i=i):
                for copy in copies(i):
                    copy.start()

        load = pltpu.make_async_copy(rhs.at[pl.ds(first, width)], solved, rhs_sem)
        load.start()
        for i in range(pieces):

            @pl.when(needed(i))
            def _(i=i):
                for copy in copies(i):
                    copy.wait()

        load.wait()
        row, col = grid_ids(chunk)
        lane = lax.broadcasted_iota(jnp.int32, (chunk, LANES), 1)
        starts = range(0, width, chunk)
        inverses = []
        for j in starts:
            value = lower[first + j : first + j + chunk, side:]
            value = jnp.where(lane >= LANES - block, value, 0.0)
            shift = block
            while shift < LANES:
                value = value + pltpu.roll(value, LANES - shift, 1)
                shift *= 2
            value = jnp.concatenate([value] * (chunk // LANES), axis=1)
            inverses.append(jnp.where(row // block == col // block, value, 0.0))
        half = block
        while half < chunk:
            below = below_blocks(half, row, col)
            parts = [split16(inverse) for inverse in inverses]
            inner = [
                dot_split(
                    split16(
                        jnp.where(
                            below,
                            lower[first + j : first + j + chunk, first + j : first + j + chunk],
                            0.0,
                        )
                    ),
                    part,
                )
                for j, part in zip(starts, parts)
            ]
            inverses = [
                inverse - dot_split(part, split16(value))
                for inverse, part, value in zip(inverses, parts, inner)
            ]
            half *= 2
        for k in range(panel):
            solved[...] = solved[...] - dot_split(
                split16(lower[first:last, k * width : (k + 1) * width]), split16(earlier[k][...])
            )
        for j in starts:
            value = solved[j : j + chunk]
            if j:
                at = slice(first + j, first + j + chunk)
                value = value - dot_split(
                    split16(lower[at, first : first + j]), split16(solved[:j])
                )
            solved[j : j + chunk] = dot_split(split16(inverses[j // chunk]), split16(value))


def solve_panel(panel, ids, place, held, rhs, earlier, after, width, block):
    pieces = len(held[0])
    rows = held[0][0].shape[0]
    columns = rhs.shape[1]
    tall = -(-(panel + 1) * width // rows) * rows
    chunk = math.gcd(width, 2 * LANES)
    return pl.pallas_call(
        functools.partial(solve_kernel, pieces, rows, width, chunk, block, panel),
        out_shape=jax.ShapeDtypeStruct((width, columns), jnp.float32),
        in_specs=[SCALARS] * 2
        + [ANY] * (2 * pieces + 1)
        + [WHOLE] * panel
        + [ANY] * len(after),
        out_specs=WHOLE,
        scratch_shapes=[
            pltpu.VMEM((tall, 2 * width if panel else width + LANES), jnp.float32),
            pltpu.SemaphoreType.DMA((2, pieces)),
            pltpu.SemaphoreType.DMA,
        ],
        compiler_params=pltpu.CompilerParams(vmem_limit_bytes=VMEM_BYTES),
        cost_estimate=pl.CostEstimate(
            flops=24 * (panel + 1) * width * width * columns,
            bytes_accessed=12 * width * columns,
            transcendentals=0,
        ),
    )(ids, place, *held[0], *held[1], rhs, *earlier, *after)


def update_kernel(pieces, rows, width, tile, step, places, ids, place, *refs):
    held, refs = refs[: 2 * pieces], refs[2 * pieces :]
    rhs, refs = refs[0], refs[1:]
    solved, refs = refs[: 2 * places], refs[2 * places :]
    refs = refs[len(refs) - 11 :]
    out, lower, block, found, high, low, product, piece_sem, block_sem, found_sem, out_sem = refs
    depth = 2 * width
    start = place[0] * rhs.shape[0]

    def fetch(k, r):
        return pltpu.make_async_copy(
            solved[k * places + r], found.at[pl.ds(k * width, width)], found_sem.at[k]
        )

    def at(i):
        return pl.ds(pl.multiple_of(ids[i] * rows, 8), rows)

    def load(k, i, source):
        return pltpu.make_async_copy(
            held[source], lower.at[i, :, pl.ds(k * width, width)], piece_sem.at[k, i]
        )

    def load_block(i):
        return pltpu.make_async_copy(rhs.at[at(i)], block.at[i], block_sem.at[i])

    def store(i):
        return pltpu.make_async_copy(block.at[i], out.at[at(i)], out_sem.at[i])

    for r in range(places):

        @pl.when(place[0] == r)
        def _(r=r):
            for k in range(2):
                fetch(k, r).start()

    for i in range(pieces):
        for k in range(2):
            load(k, i, k * pieces + i).start()
        load_block(i).start()
    for k in range(2):
        fetch(k, 0).wait()
    high[...], low[...] = split16(found[...])

    @pl.loop(0, pieces)
    def _(i):
        for k in range(2):
            load(k, i, 0).wait()
        load_block(i).wait()

        @pl.loop(0, rows // tile)
        def _(t):
            inside = pl.multiple_of(t * tile, 8)
            top = start + ids[i] * rows + inside
            product[...] = dot_split(
                split16(lower[i, pl.ds(inside, tile)]), (high[...], low[...])
            )

            @pl.when(top >= depth)
            def _():
                block[i, pl.ds(inside, tile)] = block[i, pl.ds(inside, tile)] - product[...]

            @pl.when(top < depth)
            def _():
                @pl.loop(0, tile // step)
                def _(u):
                    part = pl.multiple_of(u * step, 8)
                    row = top + part
                    here = pl.ds(inside + part, step)

                    @pl.when(row < depth)
                    def _():
                        block[i, here] = found[pl.ds(pl.multiple_of(row, 8), step)]

                    @pl.when(row >= depth)
                    def _():
                        block[i, here] = block[i, here] - product[pl.ds(part, step)]

        store(i).start()

    @pl.loop(0, pieces)
    def _(i):
        store(i).wait()


def update(ids, place, held, rhs, solved, width, written=None):
    pieces, places = len(held[0]), len(solved[0])
    rows, columns = held[0][0].shape[0], rhs.shape[1]
    step = math.gcd(rows, 2 * width)
    tile = step * max(m for m in range(1, rows // step + 1) if rows // step % m == 0 and step * m <= 512)
    operands = [ids, place, *[piece for group in held for piece in group], rhs, *solved[0], *solved[1]]
    extra = [] if written is None else [written]
    return pl.pallas_call(
        functools.partial(update_kernel, pieces, rows, width, tile, step, places),
        out_shape=jax.ShapeDtypeStruct(rhs.shape, jnp.float32),
        in_specs=[SCALARS] * 2 + [ANY] * (len(operands) - 2 + len(extra)),
        out_specs=ANY,
        input_output_aliases={len(operands): 0} if extra else {},
        scratch_shapes=[
            pltpu.VMEM((pieces, rows, 2 * width), jnp.float32),
            pltpu.VMEM((pieces, rows, columns), jnp.float32),
            pltpu.VMEM((2 * width, columns), jnp.float32),
            pltpu.VMEM((2 * width, columns), jnp.bfloat16),
            pltpu.VMEM((2 * width, columns), jnp.bfloat16),
            pltpu.VMEM((tile, columns), jnp.float32),
            pltpu.SemaphoreType.DMA((2, pieces)),
            pltpu.SemaphoreType.DMA((pieces,)),
            pltpu.SemaphoreType.DMA((2,)),
            pltpu.SemaphoreType.DMA((pieces,)),
        ],
        compiler_params=pltpu.CompilerParams(vmem_limit_bytes=VMEM_BYTES),
        cost_estimate=pl.CostEstimate(
            flops=12 * pieces * rows * width * columns,
            bytes_accessed=8 * pieces * rows * (width + columns),
            transcendentals=0,
        ),
    )(*operands, *extra)


def gate_kernel(count, *refs):
    pass


def gate(blocks, tokens):
    count = len(blocks)
    return pl.pallas_call(
        functools.partial(gate_kernel, count),
        out_shape=[jax.ShapeDtypeStruct(block.shape, block.dtype) for block in blocks],
        in_specs=[ANY] * (count + len(tokens)),
        out_specs=[ANY] * count,
        input_output_aliases={i: i for i in range(count)},
        compiler_params=pltpu.CompilerParams(vmem_limit_bytes=VMEM_BYTES),
    )(*blocks, *tokens)


def ring_pass(starts, ring):
    count = len(ring)
    onward = [(ring[i], ring[(i + 1) % count]) for i in range(count)]
    back = [(b, a) for a, b in onward]
    held = [[starts[k][k]] for k in range(2)]
    going = [list(ways) for ways in starts]
    steps = []
    for step in range(1, count // 2 + 1):
        for k in range(2):
            for way, pairs in enumerate((onward, back)):
                if step == count // 2 and way != k:
                    continue
                going[k][way] = lax.ppermute(going[k][way], "src", pairs)
                held[k].append(going[k][way])
        steps.append([list(ways) for ways in going])
    return held, steps


def spread_far(block, count):
    found = {0: block}
    stride = count // 2
    while stride > 1:
        for r in list(found):
            found[r + stride] = lax.ppermute(found[r], "row", [(r, r + stride)])
        stride //= 2
    return found


def spread_near(found, count, tokens):
    found = dict(found)
    for r in sorted(found):
        if r and tokens:
            (found[r],) = gate([found[r]], tokens)
        if r + 1 < count:
            found[r + 1] = lax.ppermute(found[r], "row", [(r, r + 1)])
    return [found[r] for r in range(count)]


def swap_partners(count, tops):
    free = [s for s in range(count) if 2 * s >= tops]
    partners = []
    for s in range(count):
        if 2 * s + 1 < tops:
            pool = [f for f in free if f % 2 == s % 2] or free
            if not pool:
                return None
            partners.append(pool[-1])
            free.remove(pool[-1])
    return partners


def lookup(table, index):
    hit = index[:, None] == jnp.arange(len(table), dtype=jnp.int32)[None, :]
    return jnp.sum(jnp.where(hit, jnp.array(table, jnp.int32)[None, :], 0), axis=1)


def solution(mesh):
    count, places = mesh.shape["src"], mesh.shape["row"]
    axes = tuple(mesh.axis_names)

    def number(source, row):
        at, place = {"src": source, "row": row}, 0
        for axis in axes:
            place = place * mesh.shape[axis] + at[axis]
        return place

    def local(factor, right_side):
        rows, depth = factor.shape
        width, part = depth // 2, rows // 2
        block = math.gcd(math.gcd(rows, width), LANES)
        me = lax.axis_index("src").reshape(1).astype(jnp.int32)
        place = lax.axis_index("row").reshape(1).astype(jnp.int32)
        partners = swap_partners(count, -(-depth // part))
        ringed = count % 2 == 0 and count <= RING_LIMIT and part % 8 == 0 and partners is not None
        if not ringed:
            held = [
                [lax.all_gather(panel, "src", axis=0, tiled=True)]
                for panel in prepare(me, place, factor, block, 1, 0)
            ]
            top, top_spots = held, jnp.zeros_like(me)
            groups = [(held, top_spots)]
            after, near = [[], []], [[], []]
        else:
            movers = len(partners)
            *halves, sent_first, sent_second = prepare(me, place, factor, block, 2, movers)
            pairs = [(s, f) for s, f in enumerate(partners)]
            swap = [(number(a, 0), number(b, 0)) for s, f in pairs for a, b in ((s, f), (f, s))]
            got = [lax.ppermute(sent, axes, swap) for sent in (sent_first, sent_second)]
            source = me[0]
            paired = functools.reduce(jnp.logical_or, [source == f for f in partners])
            takes = [(place[0] == 0) & paired, (place[0] == 0) & (source < movers)]
            own = [
                [jnp.where(takes[h], got[k], halves[2 * h + k]) for k in range(2)] for h in range(2)
            ]
            ring = list(range(0, count, 2)) + list(range(count - 1, 0, -2))
            position = jnp.where(source % 2 == 0, source // 2, count - 1 - source // 2)
            half = count // 2
            away = [0] + [d for step in range(1, half) for d in (-step, step)] + [half]
            position = (position + jnp.array(away, jnp.int32) + count) % count
            ids = jnp.where(position < half, 2 * position, 2 * (count - 1 - position) + 1)
            tables = [[2 * s + h for s in range(count)] for h in range(2)]
            for s, f in pairs:
                tables[0][f], tables[1][s] = 2 * s + 1, 2 * f
            spots = [
                jnp.where(place[0] == 0, lookup(tables[h], ids), 2 * ids + h).astype(jnp.int32)
                for h in range(2)
            ]
            top, steps = ring_pass([[piece] * 2 for piece in own[0]], ring)
            free = gate(own[1], [steps[-2][0][0]])
            full = gate(free, [steps[-1][0][0]])
            rest, steps = ring_pass([[full[0], free[0]], [free[1], full[1]]], ring)
            after = [[steps[0][0][1], steps[0][1][0]], [steps[0][0][0], steps[0][1][1]]]
            near = [steps[i][0] + steps[i][1] for i in (1, -2)]
            top_spots, cut = spots[0], 2 * half - 3
            groups = [
                (
                    [top[k] + rest[k][:cut] for k in range(2)],
                    jnp.concatenate([spots[0], spots[1][:cut]]),
                ),
                ([rest[k][cut:] for k in range(2)], spots[1][cut:]),
            ]
        first = solve_panel(0, top_spots, place, top, right_side, [], after[0], width, block)
        second = solve_panel(1, top_spots, place, top, right_side, [first], after[1], width, block)
        solved = [
            spread_near(spread_far(first, places), places, near[0]),
            spread_near(spread_far(second, places), places, near[1]),
        ]
        result = None
        for held, spots in groups:
            result = update(spots, place, held, right_side, solved, width, result)
        return result

    placed = (P(("row", "src"), None), P("row", "src"))
    return jax.shard_map(
        local, mesh=mesh, in_specs=placed, out_specs=P("row", "src"), check_vma=False
    )
```

```python
import functools
import math

import jax
import jax.numpy as jnp
from jax import lax
from jax.experimental import pallas as pl
from jax.experimental.pallas import tpu as pltpu
from jax.sharding import PartitionSpec as P

VMEM_BYTES = 52 * 1024 * 1024
LANES = 128
SHORT = pl.CostEstimate(flops=1000, bytes_accessed=1000, transcendentals=0)
RING_LIMIT = 16

ANY = pl.BlockSpec(memory_space=pltpu.HBM)
SCALARS = pl.BlockSpec(memory_space=pltpu.SMEM)
WHOLE = pl.BlockSpec(memory_space=pltpu.VMEM)


def dot32(a, b):
    return jnp.dot(a, b, preferred_element_type=jnp.float32, precision=lax.Precision.HIGHEST)


def split16(value):
    high = value.astype(jnp.bfloat16)
    return high, (value - high.astype(jnp.float32)).astype(jnp.bfloat16)


def dot_split(a, b):
    (a_high, a_low), (b_high, b_low) = a, b
    dot = functools.partial(jnp.dot, preferred_element_type=jnp.float32)
    return dot(a_high, b_high) + dot(a_high, b_low) + dot(a_low, b_high)


def grid_ids(size):
    return [lax.broadcasted_iota(jnp.int32, (size, size), axis) for axis in range(2)]


def below_blocks(half, row, col):
    return (row // half % 2 == 1) & (col // half == row // half - 1)


def invert_lower(blocks):
    size = blocks[0].shape[0]
    row, col = grid_ids(size)
    inverses = []
    for block in blocks:
        diag = jnp.where(row == col, block, 0.0)
        down = 1.0 / jnp.sum(diag, axis=1, keepdims=True)
        across = 1.0 / jnp.sum(diag, axis=0, keepdims=True)
        below = below_blocks(1, row, col)
        inverses.append(
            jnp.where(row == col, down, 0.0) - jnp.where(below, down * block * across, 0.0)
        )
    half = 2
    while half < size:
        below = below_blocks(half, row, col)
        inner = [
            dot32(jnp.where(below, block, 0.0), inverse) for block, inverse in zip(blocks, inverses)
        ]
        inverses = [inverse - dot32(inverse, part) for inverse, part in zip(inverses, inner)]
        half *= 2
    return inverses


def prepare_kernel(rows, block, depth, cuts, movers, me, place, source, *refs):
    *outs, factor, load_sem, store_sem = refs
    width, part = depth // 2, rows // cuts
    load = pltpu.make_async_copy(source, factor, load_sem)
    load.start()
    load.wait()
    first = me[0] * rows

    @pl.when((place[0] == 0) & (first < depth))
    def _():
        blocks = []
        for j in range(0, rows, block):
            at = jnp.minimum(first + j, depth - block)
            near = pl.multiple_of(at // LANES * LANES, LANES)
            value = factor[j : j + block, pl.ds(near, LANES)]
            value = pltpu.roll(value, (LANES - at % LANES) % LANES, 1)
            blocks.append(value[:, :block])
        row, col = grid_ids(block)
        blocks = [
            jnp.where(first + i * block < depth, value, jnp.where(row == col, 1.0, 0.0))
            for i, value in enumerate(blocks)
        ]
        for i, inverse in enumerate(invert_lower(blocks)):

            @pl.when(first + i * block < depth)
            def _(i=i, inverse=inverse):
                factor[i * block : (i + 1) * block, depth - block :] = inverse

    moves = me[0] < movers
    copies = []
    for k in range(2):
        panel = pl.ds(k * width, width)
        for cut in range(cuts):
            at = pl.ds(cut * part, part)
            copies.append((factor.at[at, panel], outs[2 * cut + k], store_sem.at[2 * cut + k]))
        if cuts > 1:
            sent = pl.ds(pl.multiple_of(jnp.where(moves, part, 0), 8), part)
            copies.append((factor.at[sent, panel], outs[4 + k], store_sem.at[4 + k]))
    copies = [pltpu.make_async_copy(*copy) for copy in copies]
    for copy in copies:
        copy.start()
    for copy in copies:
        copy.wait()


def prepare(me, place, factor, block, cuts, movers):
    rows, depth = factor.shape
    count = 2 * cuts + (2 if cuts > 1 else 0)
    return pl.pallas_call(
        functools.partial(prepare_kernel, rows, block, depth, cuts, movers),
        out_shape=[jax.ShapeDtypeStruct((rows // cuts, depth // 2), jnp.float32)] * count,
        in_specs=[SCALARS] * 2 + [ANY],
        out_specs=[ANY] * count,
        scratch_shapes=[
            pltpu.VMEM((rows, depth), jnp.float32),
            pltpu.SemaphoreType.DMA,
            pltpu.SemaphoreType.DMA((count,)),
        ],
        compiler_params=pltpu.CompilerParams(vmem_limit_bytes=VMEM_BYTES),
        cost_estimate=SHORT,
    )(me, place, factor)


def solve_kernel(pieces, rows, width, chunk, block, ids, place, *refs):
    held, rhs = refs[: 2 * pieces], refs[2 * pieces]
    *outs, lower, solved, piece_sem, rhs_sem, out_sem = refs[len(refs) - 7 :]
    depth = 2 * width

    @pl.when(place[0] == 0)
    def _():
        def copies(i):
            at = pl.ds(pl.multiple_of(ids[i] * rows, 8), rows)
            return [
                pltpu.make_async_copy(
                    held[k * pieces + i], lower.at[at, pl.ds(k * width, width)], piece_sem.at[k, i]
                )
                for k in range(2)
            ]

        for i in range(pieces):

            @pl.when(ids[i] * rows < depth)
            def _(i=i):
                for copy in copies(i):
                    copy.start()

        load = pltpu.make_async_copy(rhs.at[pl.ds(0, depth)], solved, rhs_sem)
        load.start()
        for i in range(pieces):

            @pl.when(ids[i] * rows < depth)
            def _(i=i):
                for copy in copies(i):
                    copy.wait()

        row, col = grid_ids(chunk)
        lane = lax.broadcasted_iota(jnp.int32, (chunk, LANES), 1)
        starts = range(0, depth, chunk)
        inverses = []
        for j in starts:
            value = lower[j : j + chunk, depth - LANES :]
            value = jnp.where(lane >= LANES - block, value, 0.0)
            shift = block
            while shift < LANES:
                value = value + pltpu.roll(value, LANES - shift, 1)
                shift *= 2
            value = jnp.concatenate([value] * (chunk // LANES), axis=1)
            inverses.append(jnp.where(row // block == col // block, value, 0.0))
        half = block
        while half < chunk:
            below = below_blocks(half, row, col)
            parts = [split16(inverse) for inverse in inverses]
            inner = [
                dot_split(
                    split16(jnp.where(below, lower[j : j + chunk, j : j + chunk], 0.0)), part
                )
                for j, part in zip(starts, parts)
            ]
            inverses = [
                inverse - dot_split(part, split16(value))
                for inverse, part, value in zip(inverses, parts, inner)
            ]
            half *= 2
        load.wait()
        stores = [
            pltpu.make_async_copy(solved.at[pl.ds(k * width, width)], outs[k], out_sem.at[k])
            for k in range(2)
        ]
        for j in starts:
            value = solved[j : j + chunk]
            if j:
                value = value - dot_split(
                    split16(lower[j : j + chunk, :j]), split16(solved[:j])
                )
            solved[j : j + chunk] = dot_split(split16(inverses[j // chunk]), split16(value))
            if (j + chunk) % width == 0:
                stores[j // width].start()
        for store in stores:
            store.wait()


def solve_panels(ids, place, held, rhs, after, width, block):
    pieces = len(held[0])
    rows = held[0][0].shape[0]
    columns, depth = rhs.shape[1], 2 * width
    tall = -(-depth // rows) * rows
    chunk = math.gcd(width, 2 * LANES)
    return pl.pallas_call(
        functools.partial(solve_kernel, pieces, rows, width, chunk, block),
        out_shape=[jax.ShapeDtypeStruct((width, columns), jnp.float32)] * 2,
        in_specs=[SCALARS] * 2 + [ANY] * (2 * pieces + 1 + len(after)),
        out_specs=[ANY] * 2,
        scratch_shapes=[
            pltpu.VMEM((tall, depth), jnp.float32),
            pltpu.VMEM((depth, columns), jnp.float32),
            pltpu.SemaphoreType.DMA((2, pieces)),
            pltpu.SemaphoreType.DMA,
            pltpu.SemaphoreType.DMA((2,)),
        ],
        compiler_params=pltpu.CompilerParams(vmem_limit_bytes=VMEM_BYTES),
        cost_estimate=pl.CostEstimate(
            flops=72 * width * width * columns,
            bytes_accessed=24 * width * columns,
            transcendentals=0,
        ),
    )(ids, place, *held[0], *held[1], rhs, *after)


def update_kernel(pieces, rows, width, tile, step, places, ids, place, *refs):
    held, refs = refs[: 2 * pieces], refs[2 * pieces :]
    rhs, refs = refs[0], refs[1:]
    solved, refs = refs[: 2 * places], refs[2 * places :]
    refs = refs[len(refs) - 11 :]
    out, lower, block, found, high, low, product, piece_sem, block_sem, found_sem, out_sem = refs
    depth = 2 * width
    start = place[0] * rhs.shape[0]

    def fetch(k, r):
        return pltpu.make_async_copy(
            solved[k * places + r], found.at[pl.ds(k * width, width)], found_sem.at[k]
        )

    def at(i):
        return pl.ds(pl.multiple_of(ids[i] * rows, 8), rows)

    def load(k, i, source):
        return pltpu.make_async_copy(
            held[source], lower.at[i, :, pl.ds(k * width, width)], piece_sem.at[k, i]
        )

    def load_block(i):
        return pltpu.make_async_copy(rhs.at[at(i)], block.at[i], block_sem.at[i])

    def store(i):
        return pltpu.make_async_copy(block.at[i], out.at[at(i)], out_sem.at[i])

    for r in range(places):

        @pl.when(place[0] == r)
        def _(r=r):
            for k in range(2):
                fetch(k, r).start()

    for i in range(pieces):
        for k in range(2):
            load(k, i, k * pieces + i).start()
        load_block(i).start()
    for k in range(2):
        fetch(k, 0).wait()
    high[...], low[...] = split16(found[...])

    @pl.loop(0, pieces)
    def _(i):
        for k in range(2):
            load(k, i, 0).wait()
        load_block(i).wait()

        @pl.loop(0, rows // tile)
        def _(t):
            inside = pl.multiple_of(t * tile, 8)
            top = start + ids[i] * rows + inside

            @pl.when(top + tile > depth)
            def _():
                product[...] = dot_split(
                    split16(lower[i, pl.ds(inside, tile)]), (high[...], low[...])
                )

            @pl.when(top >= depth)
            def _():
                block[i, pl.ds(inside, tile)] = block[i, pl.ds(inside, tile)] - product[...]

            @pl.when(top < depth)
            def _():
                @pl.loop(0, tile // step)
                def _(u):
                    part = pl.multiple_of(u * step, 8)
                    row = top + part
                    here = pl.ds(inside + part, step)

                    @pl.when(row < depth)
                    def _():
                        block[i, here] = found[pl.ds(pl.multiple_of(row, 8), step)]

                    @pl.when(row >= depth)
                    def _():
                        block[i, here] = block[i, here] - product[pl.ds(part, step)]

        store(i).start()

    @pl.loop(0, pieces)
    def _(i):
        store(i).wait()


def update(ids, place, held, rhs, solved, width, written=None):
    pieces, places = len(held[0]), len(solved[0])
    rows, columns = held[0][0].shape[0], rhs.shape[1]
    step = math.gcd(rows, 2 * width)
    tile = step * max(m for m in range(1, rows // step + 1) if rows // step % m == 0 and step * m <= 512)
    operands = [ids, place, *[piece for group in held for piece in group], rhs, *solved[0], *solved[1]]
    extra = [] if written is None else [written]
    return pl.pallas_call(
        functools.partial(update_kernel, pieces, rows, width, tile, step, places),
        out_shape=jax.ShapeDtypeStruct(rhs.shape, jnp.float32),
        in_specs=[SCALARS] * 2 + [ANY] * (len(operands) - 2 + len(extra)),
        out_specs=ANY,
        input_output_aliases={len(operands): 0} if extra else {},
        scratch_shapes=[
            pltpu.VMEM((pieces, rows, 2 * width), jnp.float32),
            pltpu.VMEM((pieces, rows, columns), jnp.float32),
            pltpu.VMEM((2 * width, columns), jnp.float32),
            pltpu.VMEM((2 * width, columns), jnp.bfloat16),
            pltpu.VMEM((2 * width, columns), jnp.bfloat16),
            pltpu.VMEM((tile, columns), jnp.float32),
            pltpu.SemaphoreType.DMA((2, pieces)),
            pltpu.SemaphoreType.DMA((pieces,)),
            pltpu.SemaphoreType.DMA((2,)),
            pltpu.SemaphoreType.DMA((pieces,)),
        ],
        compiler_params=pltpu.CompilerParams(vmem_limit_bytes=VMEM_BYTES),
        cost_estimate=pl.CostEstimate(
            flops=12 * pieces * rows * width * columns,
            bytes_accessed=8 * pieces * rows * (width + columns),
            transcendentals=0,
        ),
    )(*operands, *extra)


def gate_kernel(count, *refs):
    pass


def gate(blocks, tokens):
    count = len(blocks)
    return pl.pallas_call(
        functools.partial(gate_kernel, count),
        out_shape=[jax.ShapeDtypeStruct(block.shape, block.dtype) for block in blocks],
        in_specs=[ANY] * (count + len(tokens)),
        out_specs=[ANY] * count,
        input_output_aliases={i: i for i in range(count)},
        compiler_params=pltpu.CompilerParams(vmem_limit_bytes=VMEM_BYTES),
    )(*blocks, *tokens)


def ring_pass(starts, ring):
    count = len(ring)
    onward = [(ring[i], ring[(i + 1) % count]) for i in range(count)]
    back = [(b, a) for a, b in onward]
    held = [[starts[k][k]] for k in range(2)]
    going = [list(ways) for ways in starts]
    steps = []
    for step in range(1, count // 2 + 1):
        for k in range(2):
            for way, pairs in enumerate((onward, back)):
                if step == count // 2 and way != k:
                    continue
                going[k][way] = lax.ppermute(going[k][way], "src", pairs)
                held[k].append(going[k][way])
        steps.append([list(ways) for ways in going])
    return held, steps


def spread_far(block, count):
    found = {0: block}
    stride = count // 2
    while stride > 1:
        for r in list(found):
            found[r + stride] = lax.ppermute(found[r], "row", [(r, r + stride)])
        stride //= 2
    return found


def spread_near(found, count, tokens):
    found = dict(found)
    for r in sorted(found):
        if r and tokens:
            (found[r],) = gate([found[r]], tokens)
        if r + 1 < count:
            found[r + 1] = lax.ppermute(found[r], "row", [(r, r + 1)])
    return [found[r] for r in range(count)]


def swap_partners(count, tops):
    free = [s for s in range(count) if 2 * s >= tops]
    partners = []
    for s in range(count):
        if 2 * s + 1 < tops:
            pool = [f for f in free if f % 2 == s % 2] or free
            if not pool:
                return None
            partners.append(pool[-1])
            free.remove(pool[-1])
    return partners


def lookup(table, index):
    hit = index[:, None] == jnp.arange(len(table), dtype=jnp.int32)[None, :]
    return jnp.sum(jnp.where(hit, jnp.array(table, jnp.int32)[None, :], 0), axis=1)


def solution(mesh):
    count, places = mesh.shape["src"], mesh.shape["row"]
    axes = tuple(mesh.axis_names)

    def number(source, row):
        at, place = {"src": source, "row": row}, 0
        for axis in axes:
            place = place * mesh.shape[axis] + at[axis]
        return place

    def local(factor, right_side):
        rows, depth = factor.shape
        width, part = depth // 2, rows // 2
        block = math.gcd(math.gcd(rows, width), LANES)
        me = lax.axis_index("src").reshape(1).astype(jnp.int32)
        place = lax.axis_index("row").reshape(1).astype(jnp.int32)
        partners = swap_partners(count, -(-depth // part))
        ringed = count % 2 == 0 and count <= RING_LIMIT and part % 8 == 0 and partners is not None
        if not ringed:
            held = [
                [lax.all_gather(panel, "src", axis=0, tiled=True)]
                for panel in prepare(me, place, factor, block, 1, 0)
            ]
            top, top_spots = held, jnp.zeros_like(me)
            groups = [(held, top_spots)]
            after, near = [], [[], []]
        else:
            movers = len(partners)
            *halves, sent_first, sent_second = prepare(me, place, factor, block, 2, movers)
            pairs = [(s, f) for s, f in enumerate(partners)]
            swap = [(number(a, 0), number(b, 0)) for s, f in pairs for a, b in ((s, f), (f, s))]
            got = [lax.ppermute(sent, axes, swap) for sent in (sent_first, sent_second)]
            source = me[0]
            paired = functools.reduce(jnp.logical_or, [source == f for f in partners])
            takes = [(place[0] == 0) & paired, (place[0] == 0) & (source < movers)]
            own = [
                [jnp.where(takes[h], got[k], halves[2 * h + k]) for k in range(2)] for h in range(2)
            ]
            ring = list(range(0, count, 2)) + list(range(count - 1, 0, -2))
            position = jnp.where(source % 2 == 0, source // 2, count - 1 - source // 2)
            half = count // 2
            away = [0] + [d for step in range(1, half) for d in (-step, step)] + [half]
            position = (position + jnp.array(away, jnp.int32) + count) % count
            ids = jnp.where(position < half, 2 * position, 2 * (count - 1 - position) + 1)
            tables = [[2 * s + h for s in range(count)] for h in range(2)]
            for s, f in pairs:
                tables[0][f], tables[1][s] = 2 * s + 1, 2 * f
            spots = [
                jnp.where(place[0] == 0, lookup(tables[h], ids), 2 * ids + h).astype(jnp.int32)
                for h in range(2)
            ]
            top, steps = ring_pass([[piece] * 2 for piece in own[0]], ring)
            free = gate(own[1], [steps[-2][0][0]])
            full = gate(free, [steps[-1][0][0]])
            rest, steps = ring_pass([[full[0], free[0]], [free[1], full[1]]], ring)
            after = [steps[0][0][1], steps[0][1][0]]
            near = [steps[i][0] + steps[i][1] for i in (1, -2)]
            top_spots, cut = spots[0], 2 * half - 1
            groups = [
                (
                    [top[k] + rest[k][:cut] for k in range(2)],
                    jnp.concatenate([spots[0], spots[1][:cut]]),
                ),
                ([rest[k][cut:] for k in range(2)], spots[1][cut:]),
            ]
        first, second = solve_panels(top_spots, place, top, right_side, after, width, block)
        first = spread_near(spread_far(first, places), places, near[0])
        second = spread_near(spread_far(second, places), places, near[1] + first[1:2])
        solved = [first, second]
        result = None
        for held, spots in groups:
            result = update(spots, place, held, right_side, solved, width, result)
        return result

    placed = (P(("row", "src"), None), P("row", "src"))
    return jax.shard_map(
        local, mesh=mesh, in_specs=placed, out_specs=P("row", "src"), check_vma=False
    )
```

```python
import functools
import math

import jax
import jax.numpy as jnp
from jax import lax
from jax.experimental import pallas as pl
from jax.experimental.pallas import tpu as pltpu
from jax.sharding import PartitionSpec as P

VMEM_BYTES = 52 * 1024 * 1024
LANES = 128
SHORT = pl.CostEstimate(flops=1000, bytes_accessed=1000, transcendentals=0)
RING_LIMIT = 16

ANY = pl.BlockSpec(memory_space=pltpu.HBM)
SCALARS = pl.BlockSpec(memory_space=pltpu.SMEM)
WHOLE = pl.BlockSpec(memory_space=pltpu.VMEM)


def dot32(a, b):
    return jnp.dot(a, b, preferred_element_type=jnp.float32, precision=lax.Precision.HIGHEST)


def split16(value):
    high = value.astype(jnp.bfloat16)
    return high, (value - high.astype(jnp.float32)).astype(jnp.bfloat16)


def dot_split(a, b):
    (a_high, a_low), (b_high, b_low) = a, b
    dot = functools.partial(jnp.dot, preferred_element_type=jnp.float32)
    return dot(a_high, b_high) + dot(a_high, b_low) + dot(a_low, b_high)


def grid_ids(size):
    return [lax.broadcasted_iota(jnp.int32, (size, size), axis) for axis in range(2)]


def below_blocks(half, row, col):
    return (row // half % 2 == 1) & (col // half == row // half - 1)


def invert_lower(blocks):
    size = blocks[0].shape[0]
    row, col = grid_ids(size)
    inverses = []
    for block in blocks:
        diag = jnp.where(row == col, block, 0.0)
        down = 1.0 / jnp.sum(diag, axis=1, keepdims=True)
        across = 1.0 / jnp.sum(diag, axis=0, keepdims=True)
        below = below_blocks(1, row, col)
        inverses.append(
            jnp.where(row == col, down, 0.0) - jnp.where(below, down * block * across, 0.0)
        )
    half = 2
    while half < size:
        below = below_blocks(half, row, col)
        inner = [
            dot32(jnp.where(below, block, 0.0), inverse) for block, inverse in zip(blocks, inverses)
        ]
        inverses = [inverse - dot32(inverse, part) for inverse, part in zip(inverses, inner)]
        half *= 2
    return inverses


def prepare_kernel(rows, block, depth, cuts, movers, me, place, source, *refs):
    *outs, factor, load_sem, store_sem = refs
    width, part = depth // 2, rows // cuts
    load = pltpu.make_async_copy(source, factor, load_sem)
    load.start()
    load.wait()
    first = me[0] * rows

    @pl.when((place[0] == 0) & (first < depth))
    def _():
        blocks = []
        for j in range(0, rows, block):
            at = jnp.minimum(first + j, depth - block)
            near = pl.multiple_of(at // LANES * LANES, LANES)
            value = factor[j : j + block, pl.ds(near, LANES)]
            value = pltpu.roll(value, (LANES - at % LANES) % LANES, 1)
            blocks.append(value[:, :block])
        row, col = grid_ids(block)
        blocks = [
            jnp.where(first + i * block < depth, value, jnp.where(row == col, 1.0, 0.0))
            for i, value in enumerate(blocks)
        ]
        for i, inverse in enumerate(invert_lower(blocks)):

            @pl.when(first + i * block < depth)
            def _(i=i, inverse=inverse):
                factor[i * block : (i + 1) * block, depth - block :] = inverse

    moves = me[0] < movers
    copies = []
    for k in range(2):
        panel = pl.ds(k * width, width)
        for cut in range(cuts):
            at = pl.ds(cut * part, part)
            copies.append((factor.at[at, panel], outs[2 * cut + k], store_sem.at[2 * cut + k]))
        if cuts > 1:
            sent = pl.ds(pl.multiple_of(jnp.where(moves, part, 0), 8), part)
            copies.append((factor.at[sent, panel], outs[4 + k], store_sem.at[4 + k]))
    copies = [pltpu.make_async_copy(*copy) for copy in copies]
    for copy in copies:
        copy.start()
    for copy in copies:
        copy.wait()


def prepare(me, place, factor, block, cuts, movers):
    rows, depth = factor.shape
    count = 2 * cuts + (2 if cuts > 1 else 0)
    return pl.pallas_call(
        functools.partial(prepare_kernel, rows, block, depth, cuts, movers),
        out_shape=[jax.ShapeDtypeStruct((rows // cuts, depth // 2), jnp.float32)] * count,
        in_specs=[SCALARS] * 2 + [ANY],
        out_specs=[ANY] * count,
        scratch_shapes=[
            pltpu.VMEM((rows, depth), jnp.float32),
            pltpu.SemaphoreType.DMA,
            pltpu.SemaphoreType.DMA((count,)),
        ],
        compiler_params=pltpu.CompilerParams(vmem_limit_bytes=VMEM_BYTES),
        cost_estimate=SHORT,
    )(me, place, factor)


def solve_kernel(pieces, rows, width, chunk, block, panel, ids, place, *refs):
    held, refs = refs[: 2 * pieces], refs[2 * pieces :]
    rhs, refs = refs[0], refs[1:]
    earlier = refs[:panel]
    solved, lower, piece_sem, rhs_sem = refs[len(refs) - 4 :]
    first, last = panel * width, (panel + 1) * width
    side = lower.shape[1] - LANES

    @pl.when(place[0] == 0)
    def _():
        def copies(i):
            at = pl.ds(pl.multiple_of(ids[i] * rows, 8), rows)
            cut = 0 if panel else width - LANES
            return [
                pltpu.make_async_copy(
                    held[i], lower.at[at, pl.ds(0, width)], piece_sem.at[0, i]
                ),
                pltpu.make_async_copy(
                    held[pieces + i].at[:, pl.ds(cut, width - cut)],
                    lower.at[at, pl.ds(width, width - cut)],
                    piece_sem.at[1, i],
                ),
            ]

        def needed(i):
            return (ids[i] * rows < last) & ((ids[i] + 1) * rows > first)

        for i in range(pieces):

            @pl.when(needed(i))
            def _(i=i):
                for copy in copies(i):
                    copy.start()

        load = pltpu.make_async_copy(rhs.at[pl.ds(first, width)], solved, rhs_sem)
        load.start()
        for i in range(pieces):

            @pl.when(needed(i))
            def _(i=i):
                for copy in copies(i):
                    copy.wait()

        load.wait()
        row, col = grid_ids(chunk)
        lane = lax.broadcasted_iota(jnp.int32, (chunk, LANES), 1)
        starts = range(0, width, chunk)
        inverses = []
        for j in starts:
            value = lower[first + j : first + j + chunk, side:]
            value = jnp.where(lane >= LANES - block, value, 0.0)
            shift = block
            while shift < LANES:
                value = value + pltpu.roll(value, LANES - shift, 1)
                shift *= 2
            value = jnp.concatenate([value] * (chunk // LANES), axis=1)
            inverses.append(jnp.where(row // block == col // block, value, 0.0))
        half = block
        while half < chunk:
            below = below_blocks(half, row, col)
            parts = [split16(inverse) for inverse in inverses]
            inner = [
                dot_split(
                    split16(
                        jnp.where(
                            below,
                            lower[first + j : first + j + chunk, first + j : first + j + chunk],
                            0.0,
                        )
                    ),
                    part,
                )
                for j, part in zip(starts, parts)
            ]
            inverses = [
                inverse - dot_split(part, split16(value))
                for inverse, part, value in zip(inverses, parts, inner)
            ]
            half *= 2
        for k in range(panel):
            solved[...] = solved[...] - dot_split(
                split16(lower[first:last, k * width : (k + 1) * width]), split16(earlier[k][...])
            )
        for j in starts:
            value = solved[j : j + chunk]
            if j:
                at = slice(first + j, first + j + chunk)
                value = value - dot_split(
                    split16(lower[at, first : first + j]), split16(solved[:j])
                )
            solved[j : j + chunk] = dot_split(split16(inverses[j // chunk]), split16(value))


def solve_panel(panel, ids, place, held, rhs, earlier, after, width, block):
    pieces = len(held[0])
    rows = held[0][0].shape[0]
    columns = rhs.shape[1]
    tall = -(-(panel + 1) * width // rows) * rows
    chunk = math.gcd(width, 2 * LANES)
    return pl.pallas_call(
        functools.partial(solve_kernel, pieces, rows, width, chunk, block, panel),
        out_shape=jax.ShapeDtypeStruct((width, columns), jnp.float32),
        in_specs=[SCALARS] * 2
        + [ANY] * (2 * pieces + 1)
        + [WHOLE] * panel
        + [ANY] * len(after),
        out_specs=WHOLE,
        scratch_shapes=[
            pltpu.VMEM((tall, 2 * width if panel else width + LANES), jnp.float32),
            pltpu.SemaphoreType.DMA((2, pieces)),
            pltpu.SemaphoreType.DMA,
        ],
        compiler_params=pltpu.CompilerParams(vmem_limit_bytes=VMEM_BYTES),
        cost_estimate=pl.CostEstimate(
            flops=24 * (panel + 1) * width * width * columns,
            bytes_accessed=12 * width * columns,
            transcendentals=0,
        ),
    )(ids, place, *held[0], *held[1], rhs, *earlier, *after)


def update_kernel(pieces, rows, width, tile, step, places, ids, place, *refs):
    held, refs = refs[: 2 * pieces], refs[2 * pieces :]
    rhs, refs = refs[0], refs[1:]
    solved, refs = refs[: 2 * places], refs[2 * places :]
    refs = refs[len(refs) - 11 :]
    out, lower, block, found, high, low, product, piece_sem, block_sem, found_sem, out_sem = refs
    depth = 2 * width
    start = place[0] * rhs.shape[0]

    def fetch(k, r):
        return pltpu.make_async_copy(
            solved[k * places + r], found.at[pl.ds(k * width, width)], found_sem.at[k]
        )

    def at(i):
        return pl.ds(pl.multiple_of(ids[i] * rows, 8), rows)

    def load(k, i, source):
        return pltpu.make_async_copy(
            held[source], lower.at[i, :, pl.ds(k * width, width)], piece_sem.at[k, i]
        )

    def load_block(i):
        return pltpu.make_async_copy(rhs.at[at(i)], block.at[i], block_sem.at[i])

    def store(i):
        return pltpu.make_async_copy(block.at[i], out.at[at(i)], out_sem.at[i])

    for r in range(places):

        @pl.when(place[0] % places == r)
        def _(r=r):
            for k in range(2):
                fetch(k, r).start()

    for i in range(pieces):
        for k in range(2):
            load(k, i, k * pieces + i).start()
        load_block(i).start()
    for k in range(2):
        fetch(k, 0).wait()
    high[...], low[...] = split16(found[...])

    @pl.loop(0, pieces)
    def _(i):
        for k in range(2):
            load(k, i, 0).wait()
        load_block(i).wait()

        @pl.loop(0, rows // tile)
        def _(t):
            inside = pl.multiple_of(t * tile, 8)
            top = start + ids[i] * rows + inside

            @pl.when(top + tile > depth)
            def _():
                product[...] = dot_split(
                    split16(lower[i, pl.ds(inside, tile)]), (high[...], low[...])
                )

            @pl.when(top >= depth)
            def _():
                block[i, pl.ds(inside, tile)] = block[i, pl.ds(inside, tile)] - product[...]

            @pl.when(top < depth)
            def _():
                @pl.loop(0, tile // step)
                def _(u):
                    part = pl.multiple_of(u * step, 8)
                    row = top + part
                    here = pl.ds(inside + part, step)

                    @pl.when(row < depth)
                    def _():
                        block[i, here] = found[pl.ds(pl.multiple_of(row, 8), step)]

                    @pl.when(row >= depth)
                    def _():
                        block[i, here] = block[i, here] - product[pl.ds(part, step)]

        store(i).start()

    @pl.loop(0, pieces)
    def _(i):
        store(i).wait()


def update(ids, place, held, rhs, solved, width, written=None):
    pieces, places = len(held[0]), len(solved[0])
    rows, columns = held[0][0].shape[0], rhs.shape[1]
    step = math.gcd(rows, 2 * width)
    tile = step * max(m for m in range(1, rows // step + 1) if rows // step % m == 0 and step * m <= 512)
    operands = [ids, place, *[piece for group in held for piece in group], rhs, *solved[0], *solved[1]]
    extra = [] if written is None else [written]
    return pl.pallas_call(
        functools.partial(update_kernel, pieces, rows, width, tile, step, places),
        out_shape=jax.ShapeDtypeStruct(rhs.shape, jnp.float32),
        in_specs=[SCALARS] * 2 + [ANY] * (len(operands) - 2 + len(extra)),
        out_specs=ANY,
        input_output_aliases={len(operands): 0} if extra else {},
        scratch_shapes=[
            pltpu.VMEM((pieces, rows, 2 * width), jnp.float32),
            pltpu.VMEM((pieces, rows, columns), jnp.float32),
            pltpu.VMEM((2 * width, columns), jnp.float32),
            pltpu.VMEM((2 * width, columns), jnp.bfloat16),
            pltpu.VMEM((2 * width, columns), jnp.bfloat16),
            pltpu.VMEM((tile, columns), jnp.float32),
            pltpu.SemaphoreType.DMA((2, pieces)),
            pltpu.SemaphoreType.DMA((pieces,)),
            pltpu.SemaphoreType.DMA((2,)),
            pltpu.SemaphoreType.DMA((pieces,)),
        ],
        compiler_params=pltpu.CompilerParams(vmem_limit_bytes=VMEM_BYTES),
        cost_estimate=pl.CostEstimate(
            flops=12 * pieces * rows * width * columns,
            bytes_accessed=8 * pieces * rows * (width + columns),
            transcendentals=0,
        ),
    )(*operands, *extra)


def gate_kernel(count, *refs):
    pass


def gate(blocks, tokens):
    count = len(blocks)
    return pl.pallas_call(
        functools.partial(gate_kernel, count),
        out_shape=[jax.ShapeDtypeStruct(block.shape, block.dtype) for block in blocks],
        in_specs=[ANY] * (count + len(tokens)),
        out_specs=[ANY] * count,
        input_output_aliases={i: i for i in range(count)},
        compiler_params=pltpu.CompilerParams(vmem_limit_bytes=VMEM_BYTES),
    )(*blocks, *tokens)


def ring_pass(starts, ring):
    count = len(ring)
    onward = [(ring[i], ring[(i + 1) % count]) for i in range(count)]
    back = [(b, a) for a, b in onward]
    held = [[starts[k][k]] for k in range(2)]
    going = [list(ways) for ways in starts]
    steps = []
    for step in range(1, count // 2 + 1):
        for k in range(2):
            for way, pairs in enumerate((onward, back)):
                if step == count // 2 and way != k:
                    continue
                going[k][way] = lax.ppermute(going[k][way], "src", pairs)
                held[k].append(going[k][way])
        steps.append([list(ways) for ways in going])
    return held, steps


def spread_far(block, count, place):
    found = {0: block}
    stride = count // 2
    while stride > 1:
        for r in list(found):
            found[r + stride] = lax.ppermute(found[r], "row", [(r, r + stride)])
        stride //= 2
    for r in found:
        if r:
            block = jnp.where(place[0] == r, found[r], block)
    return block


def spread_near(block, count, tokens):
    if tokens:
        (block,) = gate([block], tokens)
    return [block, lax.ppermute(block, "row", [(r, r + 1) for r in range(0, count - 1, 2)])]


def swap_partners(count, tops):
    free = [s for s in range(count) if 2 * s >= tops]
    partners = []
    for s in range(count):
        if 2 * s + 1 < tops:
            pool = [f for f in free if f % 2 == s % 2] or free
            if not pool:
                return None
            partners.append(pool[-1])
            free.remove(pool[-1])
    return partners


def lookup(table, index):
    hit = index[:, None] == jnp.arange(len(table), dtype=jnp.int32)[None, :]
    return jnp.sum(jnp.where(hit, jnp.array(table, jnp.int32)[None, :], 0), axis=1)


def solution(mesh):
    count, places = mesh.shape["src"], mesh.shape["row"]
    axes = tuple(mesh.axis_names)

    def number(source, row):
        at, place = {"src": source, "row": row}, 0
        for axis in axes:
            place = place * mesh.shape[axis] + at[axis]
        return place

    def local(factor, right_side):
        rows, depth = factor.shape
        width, part = depth // 2, rows // 2
        block = math.gcd(math.gcd(rows, width), LANES)
        me = lax.axis_index("src").reshape(1).astype(jnp.int32)
        place = lax.axis_index("row").reshape(1).astype(jnp.int32)
        partners = swap_partners(count, -(-depth // part))
        ringed = count % 2 == 0 and count <= RING_LIMIT and part % 8 == 0 and partners is not None
        if not ringed:
            held = [
                [lax.all_gather(panel, "src", axis=0, tiled=True)]
                for panel in prepare(me, place, factor, block, 1, 0)
            ]
            top, top_spots = held, jnp.zeros_like(me)
            groups = [(held, top_spots)]
            after, near = [[], []], [[], []]
        else:
            movers = len(partners)
            *halves, sent_first, sent_second = prepare(me, place, factor, block, 2, movers)
            pairs = [(s, f) for s, f in enumerate(partners)]
            swap = [(number(a, 0), number(b, 0)) for s, f in pairs for a, b in ((s, f), (f, s))]
            got = [lax.ppermute(sent, axes, swap) for sent in (sent_first, sent_second)]
            source = me[0]
            paired = functools.reduce(jnp.logical_or, [source == f for f in partners])
            takes = [(place[0] == 0) & paired, (place[0] == 0) & (source < movers)]
            own = [
                [jnp.where(takes[h], got[k], halves[2 * h + k]) for k in range(2)] for h in range(2)
            ]
            ring = list(range(0, count, 2)) + list(range(count - 1, 0, -2))
            position = jnp.where(source % 2 == 0, source // 2, count - 1 - source // 2)
            half = count // 2
            away = [0] + [d for step in range(1, half) for d in (-step, step)] + [half]
            position = (position + jnp.array(away, jnp.int32) + count) % count
            ids = jnp.where(position < half, 2 * position, 2 * (count - 1 - position) + 1)
            tables = [[2 * s + h for s in range(count)] for h in range(2)]
            for s, f in pairs:
                tables[0][f], tables[1][s] = 2 * s + 1, 2 * f
            spots = [
                jnp.where(place[0] == 0, lookup(tables[h], ids), 2 * ids + h).astype(jnp.int32)
                for h in range(2)
            ]
            top, steps = ring_pass([[piece] * 2 for piece in own[0]], ring)
            free = gate(own[1], [steps[-2][0][0]])
            full = gate(free, [steps[-1][0][0]])
            rest, steps = ring_pass([[full[0], free[0]], [free[1], full[1]]], ring)
            after = [[steps[0][0][1], steps[0][1][0]], [steps[0][0][0], steps[0][1][1]]]
            near = [steps[i][0] + steps[i][1] for i in (1, -2)]
            top_spots, cut = spots[0], 2 * half - 1
            groups = [
                (
                    [top[k] + rest[k][:cut] for k in range(2)],
                    jnp.concatenate([spots[0], spots[1][:cut]]),
                ),
                ([rest[k][cut:] for k in range(2)], spots[1][cut:]),
            ]
        first = solve_panel(0, top_spots, place, top, right_side, [], after[0], width, block)
        second = solve_panel(1, top_spots, place, top, right_side, [first], after[1], width, block)
        solved = [
            spread_near(spread_far(first, places, place), places, near[0]),
            spread_near(spread_far(second, places, place), places, near[1]),
        ]
        result = None
        for held, spots in groups:
            result = update(spots, place, held, right_side, solved, width, result)
        return result

    placed = (P(("row", "src"), None), P("row", "src"))
    return jax.shard_map(
        local, mesh=mesh, in_specs=placed, out_specs=P("row", "src"), check_vma=False
    )
```

```python
import functools
import math

import jax
import jax.numpy as jnp
from jax import lax
from jax.experimental import pallas as pl
from jax.experimental.pallas import tpu as pltpu
from jax.sharding import PartitionSpec as P

VMEM_BYTES = 52 * 1024 * 1024
LANES = 128
SHORT = pl.CostEstimate(flops=1000, bytes_accessed=1000, transcendentals=0)
RING_LIMIT = 16

ANY = pl.BlockSpec(memory_space=pltpu.HBM)
SCALARS = pl.BlockSpec(memory_space=pltpu.SMEM)
WHOLE = pl.BlockSpec(memory_space=pltpu.VMEM)


def dot32(a, b):
    return jnp.dot(a, b, preferred_element_type=jnp.float32, precision=lax.Precision.HIGHEST)


def split16(value):
    high = value.astype(jnp.bfloat16)
    return high, (value - high.astype(jnp.float32)).astype(jnp.bfloat16)


def dot_split(a, b):
    (a_high, a_low), (b_high, b_low) = a, b
    dot = functools.partial(jnp.dot, preferred_element_type=jnp.float32)
    return dot(a_high, b_high) + dot(a_high, b_low) + dot(a_low, b_high)


def grid_ids(size):
    return [lax.broadcasted_iota(jnp.int32, (size, size), axis) for axis in range(2)]


def below_blocks(half, row, col):
    return (row // half % 2 == 1) & (col // half == row // half - 1)


def invert_lower(blocks):
    size = blocks[0].shape[0]
    row, col = grid_ids(size)
    inverses = []
    for block in blocks:
        diag = jnp.where(row == col, block, 0.0)
        down = 1.0 / jnp.sum(diag, axis=1, keepdims=True)
        across = 1.0 / jnp.sum(diag, axis=0, keepdims=True)
        below = below_blocks(1, row, col)
        inverses.append(
            jnp.where(row == col, down, 0.0) - jnp.where(below, down * block * across, 0.0)
        )
    half = 2
    while half < size:
        below = below_blocks(half, row, col)
        inner = [
            dot32(jnp.where(below, block, 0.0), inverse) for block, inverse in zip(blocks, inverses)
        ]
        inverses = [inverse - dot32(inverse, part) for inverse, part in zip(inverses, inner)]
        half *= 2
    return inverses


def prepare_kernel(rows, block, depth, cuts, movers, me, place, source, *refs):
    *outs, factor, load_sem, store_sem = refs
    width, part = depth // 2, rows // cuts
    load = pltpu.make_async_copy(source, factor, load_sem)
    load.start()
    load.wait()
    first = me[0] * rows

    @pl.when((place[0] == 0) & (first < depth))
    def _():
        blocks = []
        for j in range(0, rows, block):
            at = jnp.minimum(first + j, depth - block)
            near = pl.multiple_of(at // LANES * LANES, LANES)
            value = factor[j : j + block, pl.ds(near, LANES)]
            value = pltpu.roll(value, (LANES - at % LANES) % LANES, 1)
            blocks.append(value[:, :block])
        row, col = grid_ids(block)
        blocks = [
            jnp.where(first + i * block < depth, value, jnp.where(row == col, 1.0, 0.0))
            for i, value in enumerate(blocks)
        ]
        for i, inverse in enumerate(invert_lower(blocks)):

            @pl.when(first + i * block < depth)
            def _(i=i, inverse=inverse):
                factor[i * block : (i + 1) * block, depth - block :] = inverse

    moves = me[0] < movers
    copies = []
    for k in range(2):
        panel = pl.ds(k * width, width)
        for cut in range(cuts):
            at = pl.ds(cut * part, part)
            copies.append((factor.at[at, panel], outs[2 * cut + k], store_sem.at[2 * cut + k]))
        if cuts > 1:
            sent = pl.ds(pl.multiple_of(jnp.where(moves, part, 0), 8), part)
            copies.append((factor.at[sent, panel], outs[4 + k], store_sem.at[4 + k]))
    copies = [pltpu.make_async_copy(*copy) for copy in copies]
    for copy in copies:
        copy.start()
    for copy in copies:
        copy.wait()


def prepare(me, place, factor, block, cuts, movers):
    rows, depth = factor.shape
    count = 2 * cuts + (2 if cuts > 1 else 0)
    return pl.pallas_call(
        functools.partial(prepare_kernel, rows, block, depth, cuts, movers),
        out_shape=[jax.ShapeDtypeStruct((rows // cuts, depth // 2), jnp.float32)] * count,
        in_specs=[SCALARS] * 2 + [ANY],
        out_specs=[ANY] * count,
        scratch_shapes=[
            pltpu.VMEM((rows, depth), jnp.float32),
            pltpu.SemaphoreType.DMA,
            pltpu.SemaphoreType.DMA((count,)),
        ],
        compiler_params=pltpu.CompilerParams(vmem_limit_bytes=VMEM_BYTES),
        cost_estimate=SHORT,
    )(me, place, factor)


def solve_kernel(pieces, rows, width, chunk, block, panel, ids, place, *refs):
    held, refs = refs[: 2 * pieces], refs[2 * pieces :]
    rhs, refs = refs[0], refs[1:]
    earlier = refs[:panel]
    solved, lower, piece_sem, rhs_sem = refs[len(refs) - 4 :]
    first, last = panel * width, (panel + 1) * width
    side = lower.shape[1] - LANES

    @pl.when(place[0] == 0)
    def _():
        def copies(i):
            at = pl.ds(pl.multiple_of(ids[i] * rows, 8), rows)
            cut = 0 if panel else width - LANES
            return [
                pltpu.make_async_copy(
                    held[i], lower.at[at, pl.ds(0, width)], piece_sem.at[0, i]
                ),
                pltpu.make_async_copy(
                    held[pieces + i].at[:, pl.ds(cut, width - cut)],
                    lower.at[at, pl.ds(width, width - cut)],
                    piece_sem.at[1, i],
                ),
            ]

        def needed(i):
            return (ids[i] * rows < last) & ((ids[i] + 1) * rows > first)

        for i in range(pieces):

            @pl.when(needed(i))
            def _(i=i):
                for copy in copies(i):
                    copy.start()

        load = pltpu.make_async_copy(rhs.at[pl.ds(first, width)], solved, rhs_sem)
        load.start()
        for i in range(pieces):

            @pl.when(needed(i))
            def _(i=i):
                for copy in copies(i):
                    copy.wait()

        load.wait()
        row, col = grid_ids(chunk)
        lane = lax.broadcasted_iota(jnp.int32, (chunk, LANES), 1)
        starts = range(0, width, chunk)
        inverses = []
        for j in starts:
            value = lower[first + j : first + j + chunk, side:]
            value = jnp.where(lane >= LANES - block, value, 0.0)
            shift = block
            while shift < LANES:
                value = value + pltpu.roll(value, LANES - shift, 1)
                shift *= 2
            value = jnp.concatenate([value] * (chunk // LANES), axis=1)
            inverses.append(jnp.where(row // block == col // block, value, 0.0))
        half = block
        while half < chunk:
            below = below_blocks(half, row, col)
            parts = [split16(inverse) for inverse in inverses]
            inner = [
                dot_split(
                    split16(
                        jnp.where(
                            below,
                            lower[first + j : first + j + chunk, first + j : first + j + chunk],
                            0.0,
                        )
                    ),
                    part,
                )
                for j, part in zip(starts, parts)
            ]
            inverses = [
                inverse - dot_split(part, split16(value))
                for inverse, part, value in zip(inverses, parts, inner)
            ]
            half *= 2
        for k in range(panel):
            solved[...] = solved[...] - dot_split(
                split16(lower[first:last, k * width : (k + 1) * width]), split16(earlier[k][...])
            )
        for j in starts:
            value = solved[j : j + chunk]
            if j:
                at = slice(first + j, first + j + chunk)
                value = value - dot_split(
                    split16(lower[at, first : first + j]), split16(solved[:j])
                )
            solved[j : j + chunk] = dot_split(split16(inverses[j // chunk]), split16(value))


def solve_panel(panel, ids, place, held, rhs, earlier, after, width, block):
    pieces = len(held[0])
    rows = held[0][0].shape[0]
    columns = rhs.shape[1]
    tall = -(-(panel + 1) * width // rows) * rows
    chunk = math.gcd(width, 2 * LANES)
    return pl.pallas_call(
        functools.partial(solve_kernel, pieces, rows, width, chunk, block, panel),
        out_shape=jax.ShapeDtypeStruct((width, columns), jnp.float32),
        in_specs=[SCALARS] * 2
        + [ANY] * (2 * pieces + 1)
        + [WHOLE] * panel
        + [ANY] * len(after),
        out_specs=WHOLE,
        scratch_shapes=[
            pltpu.VMEM((tall, 2 * width if panel else width + LANES), jnp.float32),
            pltpu.SemaphoreType.DMA((2, pieces)),
            pltpu.SemaphoreType.DMA,
        ],
        compiler_params=pltpu.CompilerParams(vmem_limit_bytes=VMEM_BYTES),
        cost_estimate=pl.CostEstimate(
            flops=24 * (panel + 1) * width * width * columns,
            bytes_accessed=12 * width * columns,
            transcendentals=0,
        ),
    )(ids, place, *held[0], *held[1], rhs, *earlier, *after)


def update_kernel(pieces, rows, width, group, tile, step, places, ids, place, *refs):
    held, refs = refs[: 2 * pieces], refs[2 * pieces :]
    rhs, refs = refs[0], refs[1:]
    solved, refs = refs[: 2 * places], refs[2 * places :]
    refs = refs[len(refs) - 11 :]
    out, lower, block, found, high, low, product, piece_sem, block_sem, found_sem, out_sem = refs
    depth = 2 * width
    start = place[0] * rhs.shape[0]

    def fetch(k, r):
        return pltpu.make_async_copy(
            solved[k * places + r], found.at[pl.ds(k * width, width)], found_sem.at[k]
        )

    def at(i):
        return pl.ds(pl.multiple_of(ids[i] * rows, 8), rows)

    def load(k, i, source):
        return pltpu.make_async_copy(
            held[source],
            lower.at[pl.ds(pl.multiple_of(i * rows, 8), rows), pl.ds(k * width, width)],
            piece_sem.at[k, i],
        )

    def load_block(i):
        return pltpu.make_async_copy(rhs.at[at(i)], block.at[i], block_sem.at[i])

    def store(i):
        return pltpu.make_async_copy(block.at[i], out.at[at(i)], out_sem.at[i])

    for r in range(places):

        @pl.when(place[0] % places == r)
        def _(r=r):
            for k in range(2):
                fetch(k, r).start()

    for i in range(pieces):
        for k in range(2):
            load(k, i, k * pieces + i).start()
        load_block(i).start()
    for k in range(2):
        fetch(k, 0).wait()
    high[...], low[...] = split16(found[...])

    @pl.loop(0, pieces // group)
    def _(g):
        members = [g * group + u for u in range(group)]
        for i in members:
            for k in range(2):
                load(k, i, 0).wait()
            load_block(i).wait()

        @pl.loop(0, rows // tile)
        def _(t):
            inside = pl.multiple_of(t * tile, 8)
            tops = [start + ids[i] * rows + inside for i in members]
            highest = functools.reduce(jnp.maximum, tops)

            @pl.when(highest + tile > depth)
            def _():
                here = pl.ds(pl.multiple_of(g * group * rows + inside, 8), group * tile)
                product[...] = dot_split(split16(lower[here]), (high[...], low[...]))

            for u, (i, top) in enumerate(zip(members, tops)):

                @pl.when(top >= depth)
                def _(i=i, u=u):
                    here = pl.ds(inside, tile)
                    block[i, here] = block[i, here] - product[u * tile : (u + 1) * tile]

                @pl.when(top < depth)
                def _(i=i, u=u, top=top):
                    @pl.loop(0, tile // step)
                    def _(v):
                        part = pl.multiple_of(v * step, 8)
                        row = top + part
                        here = pl.ds(inside + part, step)

                        @pl.when(row < depth)
                        def _():
                            block[i, here] = found[pl.ds(pl.multiple_of(row, 8), step)]

                        @pl.when(row >= depth)
                        def _():
                            block[i, here] = (
                                block[i, here] - product[pl.ds(u * tile + part, step)]
                            )

        for i in members:
            store(i).start()

    @pl.loop(0, pieces)
    def _(i):
        store(i).wait()


def update(ids, place, held, rhs, solved, width, written=None):
    pieces, places = len(held[0]), len(solved[0])
    rows, columns = held[0][0].shape[0], rhs.shape[1]
    step = math.gcd(rows, 2 * width)
    tile = step * max(m for m in range(1, rows // step + 1) if rows // step % m == 0 and step * m <= 512)
    group = 2 if pieces % 2 == 0 and tile == rows else 1
    operands = [ids, place, *[piece for group in held for piece in group], rhs, *solved[0], *solved[1]]
    extra = [] if written is None else [written]
    return pl.pallas_call(
        functools.partial(update_kernel, pieces, rows, width, group, tile, step, places),
        out_shape=jax.ShapeDtypeStruct(rhs.shape, jnp.float32),
        in_specs=[SCALARS] * 2 + [ANY] * (len(operands) - 2 + len(extra)),
        out_specs=ANY,
        input_output_aliases={len(operands): 0} if extra else {},
        scratch_shapes=[
            pltpu.VMEM((pieces * rows, 2 * width), jnp.float32),
            pltpu.VMEM((pieces, rows, columns), jnp.float32),
            pltpu.VMEM((2 * width, columns), jnp.float32),
            pltpu.VMEM((2 * width, columns), jnp.bfloat16),
            pltpu.VMEM((2 * width, columns), jnp.bfloat16),
            pltpu.VMEM((group * tile, columns), jnp.float32),
            pltpu.SemaphoreType.DMA((2, pieces)),
            pltpu.SemaphoreType.DMA((pieces,)),
            pltpu.SemaphoreType.DMA((2,)),
            pltpu.SemaphoreType.DMA((pieces,)),
        ],
        compiler_params=pltpu.CompilerParams(vmem_limit_bytes=VMEM_BYTES),
        cost_estimate=pl.CostEstimate(
            flops=12 * pieces * rows * width * columns,
            bytes_accessed=8 * pieces * rows * (width + columns),
            transcendentals=0,
        ),
    )(*operands, *extra)


def gate_kernel(count, *refs):
    pass


def gate(blocks, tokens):
    count = len(blocks)
    return pl.pallas_call(
        functools.partial(gate_kernel, count),
        out_shape=[jax.ShapeDtypeStruct(block.shape, block.dtype) for block in blocks],
        in_specs=[ANY] * (count + len(tokens)),
        out_specs=[ANY] * count,
        input_output_aliases={i: i for i in range(count)},
        compiler_params=pltpu.CompilerParams(vmem_limit_bytes=VMEM_BYTES),
    )(*blocks, *tokens)


def ring_pass(starts, ring):
    count = len(ring)
    onward = [(ring[i], ring[(i + 1) % count]) for i in range(count)]
    back = [(b, a) for a, b in onward]
    held = [[starts[k][k]] for k in range(2)]
    going = [list(ways) for ways in starts]
    steps = []
    for step in range(1, count // 2 + 1):
        for k in range(2):
            for way, pairs in enumerate((onward, back)):
                if step == count // 2 and way != k:
                    continue
                going[k][way] = lax.ppermute(going[k][way], "src", pairs)
                held[k].append(going[k][way])
        steps.append([list(ways) for ways in going])
    return held, steps


def spread_far(block, count, place):
    found = {0: block}
    stride = count // 2
    while stride > 1:
        for r in list(found):
            found[r + stride] = lax.ppermute(found[r], "row", [(r, r + stride)])
        stride //= 2
    for r in found:
        if r:
            block = jnp.where(place[0] == r, found[r], block)
    return block


def spread_near(block, count, tokens):
    if tokens:
        (block,) = gate([block], tokens)
    return [block, lax.ppermute(block, "row", [(r, r + 1) for r in range(0, count - 1, 2)])]


def swap_partners(count, tops):
    free = [s for s in range(count) if 2 * s >= tops]
    partners = []
    for s in range(count):
        if 2 * s + 1 < tops:
            pool = [f for f in free if f % 2 == s % 2] or free
            if not pool:
                return None
            partners.append(pool[-1])
            free.remove(pool[-1])
    return partners


def lookup(table, index):
    hit = index[:, None] == jnp.arange(len(table), dtype=jnp.int32)[None, :]
    return jnp.sum(jnp.where(hit, jnp.array(table, jnp.int32)[None, :], 0), axis=1)


def solution(mesh):
    count, places = mesh.shape["src"], mesh.shape["row"]
    axes = tuple(mesh.axis_names)

    def number(source, row):
        at, place = {"src": source, "row": row}, 0
        for axis in axes:
            place = place * mesh.shape[axis] + at[axis]
        return place

    def local(factor, right_side):
        rows, depth = factor.shape
        width, part = depth // 2, rows // 2
        block = math.gcd(math.gcd(rows, width), LANES)
        me = lax.axis_index("src").reshape(1).astype(jnp.int32)
        place = lax.axis_index("row").reshape(1).astype(jnp.int32)
        partners = swap_partners(count, -(-depth // part))
        ringed = count % 2 == 0 and count <= RING_LIMIT and part % 8 == 0 and partners is not None
        if not ringed:
            held = [
                [lax.all_gather(panel, "src", axis=0, tiled=True)]
                for panel in prepare(me, place, factor, block, 1, 0)
            ]
            top, top_spots = held, jnp.zeros_like(me)
            groups = [(held, top_spots)]
            after, near = [[], []], [[], []]
        else:
            movers = len(partners)
            *halves, sent_first, sent_second = prepare(me, place, factor, block, 2, movers)
            pairs = [(s, f) for s, f in enumerate(partners)]
            swap = [(number(a, 0), number(b, 0)) for s, f in pairs for a, b in ((s, f), (f, s))]
            got = [lax.ppermute(sent, axes, swap) for sent in (sent_first, sent_second)]
            source = me[0]
            paired = functools.reduce(jnp.logical_or, [source == f for f in partners])
            takes = [(place[0] == 0) & paired, (place[0] == 0) & (source < movers)]
            own = [
                [jnp.where(takes[h], got[k], halves[2 * h + k]) for k in range(2)] for h in range(2)
            ]
            ring = list(range(0, count, 2)) + list(range(count - 1, 0, -2))
            position = jnp.where(source % 2 == 0, source // 2, count - 1 - source // 2)
            half = count // 2
            away = [0] + [d for step in range(1, half) for d in (-step, step)] + [half]
            position = (position + jnp.array(away, jnp.int32) + count) % count
            ids = jnp.where(position < half, 2 * position, 2 * (count - 1 - position) + 1)
            tables = [[2 * s + h for s in range(count)] for h in range(2)]
            for s, f in pairs:
                tables[0][f], tables[1][s] = 2 * s + 1, 2 * f
            spots = [
                jnp.where(place[0] == 0, lookup(tables[h], ids), 2 * ids + h).astype(jnp.int32)
                for h in range(2)
            ]
            top, steps = ring_pass([[piece] * 2 for piece in own[0]], ring)
            free = gate(own[1], [steps[-2][0][0]])
            full = gate(free, [steps[-1][0][0]])
            rest, steps = ring_pass([[full[0], free[0]], [free[1], full[1]]], ring)
            after = [[steps[0][0][1], steps[0][1][0]], [steps[0][0][0], steps[0][1][1]]]
            near = [steps[i][0] + steps[i][1] for i in (0, -2)]
            top_spots, cut = spots[0], 2 * half - 2
            groups = [
                (
                    [top[k] + rest[k][:cut] for k in range(2)],
                    jnp.concatenate([spots[0], spots[1][:cut]]),
                ),
                ([rest[k][cut:] for k in range(2)], spots[1][cut:]),
            ]
        first = solve_panel(0, top_spots, place, top, right_side, [], after[0], width, block)
        second = solve_panel(1, top_spots, place, top, right_side, [first], after[1], width, block)
        solved = [
            spread_near(spread_far(first, places, place), places, near[0]),
            spread_near(spread_far(second, places, place), places, near[1]),
        ]
        result = None
        for held, spots in groups:
            result = update(spots, place, held, right_side, solved, width, result)
        return result

    placed = (P(("row", "src"), None), P("row", "src"))
    return jax.shard_map(
        local, mesh=mesh, in_specs=placed, out_specs=P("row", "src"), check_vma=False
    )
```

```python
import functools
import math

import jax
import jax.numpy as jnp
from jax import lax
from jax.experimental import pallas as pl
from jax.experimental.pallas import tpu as pltpu
from jax.sharding import PartitionSpec as P

VMEM_BYTES = 52 * 1024 * 1024
LANES = 128
SHORT = pl.CostEstimate(flops=1000, bytes_accessed=1000, transcendentals=0)
RING_LIMIT = 16

ANY = pl.BlockSpec(memory_space=pltpu.HBM)
SCALARS = pl.BlockSpec(memory_space=pltpu.SMEM)
WHOLE = pl.BlockSpec(memory_space=pltpu.VMEM)


def dot32(a, b):
    return jnp.dot(a, b, preferred_element_type=jnp.float32, precision=lax.Precision.HIGHEST)


def split16(value):
    high = value.astype(jnp.bfloat16)
    return high, (value - high.astype(jnp.float32)).astype(jnp.bfloat16)


def dot_split(a, b):
    (a_high, a_low), (b_high, b_low) = a, b
    dot = functools.partial(jnp.dot, preferred_element_type=jnp.float32)
    return dot(a_high, b_high) + dot(a_high, b_low) + dot(a_low, b_high)


def grid_ids(size):
    return [lax.broadcasted_iota(jnp.int32, (size, size), axis) for axis in range(2)]


def below_blocks(half, row, col):
    return (row // half % 2 == 1) & (col // half == row // half - 1)


def invert_lower(blocks):
    size = blocks[0].shape[0]
    row, col = grid_ids(size)
    inverses = []
    for block in blocks:
        diag = jnp.where(row == col, block, 0.0)
        down = 1.0 / jnp.sum(diag, axis=1, keepdims=True)
        across = 1.0 / jnp.sum(diag, axis=0, keepdims=True)
        below = below_blocks(1, row, col)
        inverses.append(
            jnp.where(row == col, down, 0.0) - jnp.where(below, down * block * across, 0.0)
        )
    half = 2
    while half < size:
        below = below_blocks(half, row, col)
        inner = [
            dot32(jnp.where(below, block, 0.0), inverse) for block, inverse in zip(blocks, inverses)
        ]
        inverses = [inverse - dot32(inverse, part) for inverse, part in zip(inverses, inner)]
        half *= 2
    return inverses


def prepare_kernel(rows, block, depth, cuts, movers, me, place, source, *refs):
    *outs, factor, load_sem, store_sem = refs
    width, part = depth // 2, rows // cuts
    load = pltpu.make_async_copy(source, factor, load_sem)
    load.start()
    load.wait()
    first = me[0] * rows

    @pl.when((place[0] == 0) & (first < depth))
    def _():
        blocks = []
        for j in range(0, rows, block):
            at = jnp.minimum(first + j, depth - block)
            near = pl.multiple_of(at // LANES * LANES, LANES)
            value = factor[j : j + block, pl.ds(near, LANES)]
            value = pltpu.roll(value, (LANES - at % LANES) % LANES, 1)
            blocks.append(value[:, :block])
        row, col = grid_ids(block)
        blocks = [
            jnp.where(first + i * block < depth, value, jnp.where(row == col, 1.0, 0.0))
            for i, value in enumerate(blocks)
        ]
        for i, inverse in enumerate(invert_lower(blocks)):

            @pl.when(first + i * block < depth)
            def _(i=i, inverse=inverse):
                factor[i * block : (i + 1) * block, depth - block :] = inverse

    moves = me[0] < movers
    panel = pl.ds(width, width)
    copies = [
        (factor.at[pl.ds(cut * part, part), panel], outs[cut], store_sem.at[cut])
        for cut in range(cuts)
    ]
    if cuts > 1:
        sent = pl.ds(pl.multiple_of(jnp.where(moves, part, 0), 8), part)
        copies.append((factor.at[sent, panel], outs[cuts], store_sem.at[cuts]))
    copies = [pltpu.make_async_copy(*copy) for copy in copies]
    for copy in copies:
        copy.start()
    for copy in copies:
        copy.wait()


def prepare(me, place, factor, block, cuts, movers):
    rows, depth = factor.shape
    count = cuts + (1 if cuts > 1 else 0)
    return pl.pallas_call(
        functools.partial(prepare_kernel, rows, block, depth, cuts, movers),
        out_shape=[jax.ShapeDtypeStruct((rows // cuts, depth // 2), jnp.float32)] * count,
        in_specs=[SCALARS] * 2 + [ANY],
        out_specs=[ANY] * count,
        scratch_shapes=[
            pltpu.VMEM((rows, depth), jnp.float32),
            pltpu.SemaphoreType.DMA,
            pltpu.SemaphoreType.DMA((count,)),
        ],
        compiler_params=pltpu.CompilerParams(vmem_limit_bytes=VMEM_BYTES),
        cost_estimate=SHORT,
    )(me, place, factor)


def solve_kernel(pieces, rows, width, chunk, block, ids, place, *refs):
    held, rhs = refs[: 2 * pieces], refs[2 * pieces]
    *outs, lower, solved, piece_sem, rhs_sem, out_sem = refs[len(refs) - 7 :]
    depth = 2 * width

    @pl.when(place[0] == 0)
    def _():
        def copies(i):
            at = pl.ds(pl.multiple_of(ids[i] * rows, 8), rows)
            return [
                pltpu.make_async_copy(
                    held[k * pieces + i], lower.at[at, pl.ds(k * width, width)], piece_sem.at[k, i]
                )
                for k in range(2)
            ]

        for i in range(pieces):

            @pl.when(ids[i] * rows < depth)
            def _(i=i):
                for copy in copies(i):
                    copy.start()

        load = pltpu.make_async_copy(rhs.at[pl.ds(0, depth)], solved, rhs_sem)
        load.start()
        for i in range(pieces):

            @pl.when(ids[i] * rows < depth)
            def _(i=i):
                for copy in copies(i):
                    copy.wait()

        row, col = grid_ids(chunk)
        lane = lax.broadcasted_iota(jnp.int32, (chunk, LANES), 1)
        starts = range(0, depth, chunk)
        inverses = []
        for j in starts:
            value = lower[j : j + chunk, depth - LANES :]
            value = jnp.where(lane >= LANES - block, value, 0.0)
            shift = block
            while shift < LANES:
                value = value + pltpu.roll(value, LANES - shift, 1)
                shift *= 2
            value = jnp.concatenate([value] * (chunk // LANES), axis=1)
            inverses.append(jnp.where(row // block == col // block, value, 0.0))
        half = block
        while half < chunk:
            below = below_blocks(half, row, col)
            parts = [split16(inverse) for inverse in inverses]
            inner = [
                dot_split(
                    split16(jnp.where(below, lower[j : j + chunk, j : j + chunk], 0.0)), part
                )
                for j, part in zip(starts, parts)
            ]
            inverses = [
                inverse - dot_split(part, split16(value))
                for inverse, part, value in zip(inverses, parts, inner)
            ]
            half *= 2
        load.wait()
        stores = [
            pltpu.make_async_copy(solved.at[pl.ds(k * width, width)], outs[k], out_sem.at[k])
            for k in range(2)
        ]
        for j in starts:
            value = solved[j : j + chunk]
            if j:
                value = value - dot_split(
                    split16(lower[j : j + chunk, :j]), split16(solved[:j])
                )
            solved[j : j + chunk] = dot_split(split16(inverses[j // chunk]), split16(value))
            if (j + chunk) % width == 0:
                stores[j // width].start()
        for store in stores:
            store.wait()


def solve_panels(ids, place, held, rhs, after, width, block):
    pieces = len(held[0])
    rows = held[0][0].shape[0]
    columns, depth = rhs.shape[1], 2 * width
    tall = -(-depth // rows) * rows
    chunk = math.gcd(width, 2 * LANES)
    return pl.pallas_call(
        functools.partial(solve_kernel, pieces, rows, width, chunk, block),
        out_shape=[jax.ShapeDtypeStruct((width, columns), jnp.float32)] * 2,
        in_specs=[SCALARS] * 2 + [ANY] * (2 * pieces + 1 + len(after)),
        out_specs=[ANY] * 2,
        scratch_shapes=[
            pltpu.VMEM((tall, depth), jnp.float32),
            pltpu.VMEM((depth, columns), jnp.float32),
            pltpu.SemaphoreType.DMA((2, pieces)),
            pltpu.SemaphoreType.DMA,
            pltpu.SemaphoreType.DMA((2,)),
        ],
        compiler_params=pltpu.CompilerParams(vmem_limit_bytes=VMEM_BYTES),
        cost_estimate=pl.CostEstimate(
            flops=72 * width * width * columns,
            bytes_accessed=24 * width * columns,
            transcendentals=0,
        ),
    )(ids, place, *held[0], *held[1], rhs, *after)


def update_kernel(pieces, rows, width, group, tile, step, places, ids, place, *refs):
    held, refs = refs[: 2 * pieces], refs[2 * pieces :]
    rhs, refs = refs[0], refs[1:]
    solved, refs = refs[: 2 * places], refs[2 * places :]
    refs = refs[len(refs) - 11 :]
    out, lower, block, found, high, low, product, piece_sem, block_sem, found_sem, out_sem = refs
    depth = 2 * width
    start = place[0] * rhs.shape[0]

    def fetch(k, r):
        return pltpu.make_async_copy(
            solved[k * places + r], found.at[pl.ds(k * width, width)], found_sem.at[k]
        )

    def at(i):
        return pl.ds(pl.multiple_of(ids[i] * rows, 8), rows)

    def load(k, i, source):
        return pltpu.make_async_copy(
            held[source],
            lower.at[pl.ds(pl.multiple_of(i * rows, 8), rows), pl.ds(k * width, width)],
            piece_sem.at[k, i],
        )

    def load_block(i):
        return pltpu.make_async_copy(rhs.at[at(i)], block.at[i], block_sem.at[i])

    def store(i):
        return pltpu.make_async_copy(block.at[i], out.at[at(i)], out_sem.at[i])

    for r in range(places):

        @pl.when(place[0] % places == r)
        def _(r=r):
            for k in range(2):
                fetch(k, r).start()

    for i in range(pieces):
        for k in range(2):
            load(k, i, k * pieces + i).start()
        load_block(i).start()
    for k in range(2):
        fetch(k, 0).wait()
    high[...], low[...] = split16(found[...])

    @pl.loop(0, pieces // group)
    def _(g):
        members = [g * group + u for u in range(group)]
        for i in members:
            for k in range(2):
                load(k, i, 0).wait()
            load_block(i).wait()

        @pl.loop(0, rows // tile)
        def _(t):
            inside = pl.multiple_of(t * tile, 8)
            tops = [start + ids[i] * rows + inside for i in members]
            highest = functools.reduce(jnp.maximum, tops)

            @pl.when(highest + tile > depth)
            def _():
                here = pl.ds(pl.multiple_of(g * group * rows + inside, 8), group * tile)
                product[...] = dot_split(split16(lower[here]), (high[...], low[...]))

            for u, (i, top) in enumerate(zip(members, tops)):

                @pl.when(top >= depth)
                def _(i=i, u=u):
                    here = pl.ds(inside, tile)
                    block[i, here] = block[i, here] - product[u * tile : (u + 1) * tile]

                @pl.when(top < depth)
                def _(i=i, u=u, top=top):
                    @pl.loop(0, tile // step)
                    def _(v):
                        part = pl.multiple_of(v * step, 8)
                        row = top + part
                        here = pl.ds(inside + part, step)

                        @pl.when(row < depth)
                        def _():
                            block[i, here] = found[pl.ds(pl.multiple_of(row, 8), step)]

                        @pl.when(row >= depth)
                        def _():
                            block[i, here] = (
                                block[i, here] - product[pl.ds(u * tile + part, step)]
                            )

        for i in members:
            store(i).start()

    @pl.loop(0, pieces)
    def _(i):
        store(i).wait()


def update(ids, place, held, rhs, solved, width, written=None):
    pieces, places = len(held[0]), len(solved[0])
    rows, columns = held[0][0].shape[0], rhs.shape[1]
    step = math.gcd(rows, 2 * width)
    tile = step * max(m for m in range(1, rows // step + 1) if rows // step % m == 0 and step * m <= 512)
    group = 2 if pieces % 2 == 0 and tile == rows else 1
    operands = [ids, place, *[piece for group in held for piece in group], rhs, *solved[0], *solved[1]]
    extra = [] if written is None else [written]
    return pl.pallas_call(
        functools.partial(update_kernel, pieces, rows, width, group, tile, step, places),
        out_shape=jax.ShapeDtypeStruct(rhs.shape, jnp.float32),
        in_specs=[SCALARS] * 2 + [ANY] * (len(operands) - 2 + len(extra)),
        out_specs=ANY,
        input_output_aliases={len(operands): 0} if extra else {},
        scratch_shapes=[
            pltpu.VMEM((pieces * rows, 2 * width), jnp.float32),
            pltpu.VMEM((pieces, rows, columns), jnp.float32),
            pltpu.VMEM((2 * width, columns), jnp.float32),
            pltpu.VMEM((2 * width, columns), jnp.bfloat16),
            pltpu.VMEM((2 * width, columns), jnp.bfloat16),
            pltpu.VMEM((group * tile, columns), jnp.float32),
            pltpu.SemaphoreType.DMA((2, pieces)),
            pltpu.SemaphoreType.DMA((pieces,)),
            pltpu.SemaphoreType.DMA((2,)),
            pltpu.SemaphoreType.DMA((pieces,)),
        ],
        compiler_params=pltpu.CompilerParams(vmem_limit_bytes=VMEM_BYTES),
        cost_estimate=pl.CostEstimate(
            flops=12 * pieces * rows * width * columns,
            bytes_accessed=8 * pieces * rows * (width + columns),
            transcendentals=0,
        ),
    )(*operands, *extra)


def gate_kernel(count, *refs):
    pass


def gate(blocks, tokens):
    count = len(blocks)
    return pl.pallas_call(
        functools.partial(gate_kernel, count),
        out_shape=[jax.ShapeDtypeStruct(block.shape, block.dtype) for block in blocks],
        in_specs=[ANY] * (count + len(tokens)),
        out_specs=[ANY] * count,
        input_output_aliases={i: i for i in range(count)},
        compiler_params=pltpu.CompilerParams(vmem_limit_bytes=VMEM_BYTES),
    )(*blocks, *tokens)


def ring_pass(starts, ring):
    count = len(ring)
    onward = [(ring[i], ring[(i + 1) % count]) for i in range(count)]
    back = [(b, a) for a, b in onward]
    held = [[starts[k][k]] for k in range(2)]
    going = [list(ways) for ways in starts]
    steps = []
    for step in range(1, count // 2 + 1):
        for k in range(2):
            for way, pairs in enumerate((onward, back)):
                if step == count // 2 and way != k:
                    continue
                going[k][way] = lax.ppermute(going[k][way], "src", pairs)
                held[k].append(going[k][way])
        steps.append([list(ways) for ways in going])
    return held, steps


def spread_far(block, count, place):
    found = {0: block}
    stride = count // 2
    while stride > 1:
        for r in list(found):
            found[r + stride] = lax.ppermute(found[r], "row", [(r, r + stride)])
        stride //= 2
    for r in found:
        if r:
            block = jnp.where(place[0] == r, found[r], block)
    return block


def spread_near(block, count, tokens):
    if tokens:
        (block,) = gate([block], tokens)
    return [block, lax.ppermute(block, "row", [(r, r + 1) for r in range(0, count - 1, 2)])]


def swap_partners(count, tops):
    free = [s for s in range(count) if 2 * s >= tops]
    partners = []
    for s in range(count):
        if 2 * s + 1 < tops:
            pool = [f for f in free if f % 2 == s % 2] or free
            if not pool:
                return None
            partners.append(pool[-1])
            free.remove(pool[-1])
    return partners


def lookup(table, index):
    hit = index[:, None] == jnp.arange(len(table), dtype=jnp.int32)[None, :]
    return jnp.sum(jnp.where(hit, jnp.array(table, jnp.int32)[None, :], 0), axis=1)


def solution(mesh):
    count, places = mesh.shape["src"], mesh.shape["row"]
    axes = tuple(mesh.axis_names)

    def number(source, row):
        at, place = {"src": source, "row": row}, 0
        for axis in axes:
            place = place * mesh.shape[axis] + at[axis]
        return place

    def local(factor, right_side):
        rows, depth = factor.shape
        width, part = depth // 2, rows // 2
        block = math.gcd(math.gcd(rows, width), LANES)
        me = lax.axis_index("src").reshape(1).astype(jnp.int32)
        place = lax.axis_index("row").reshape(1).astype(jnp.int32)
        partners = swap_partners(count, -(-depth // part))
        ringed = count % 2 == 0 and count <= RING_LIMIT and part % 8 == 0 and partners is not None
        if not ringed:
            held = [
                [lax.all_gather(panel, "src", axis=0, tiled=True)]
                for panel in (factor[:, :width], *prepare(me, place, factor, block, 1, 0))
            ]
            top, top_spots = held, jnp.zeros_like(me)
            groups = [(held, top_spots)]
            after, near = [], [[], []]
        else:
            movers = len(partners)
            left = factor[:, :width]
            sent_first = jnp.where(me[0] < movers, left[part:], left[:part])
            *right, sent_second = prepare(me, place, factor, block, 2, movers)
            halves = [left[:part], right[0], left[part:], right[1]]
            pairs = [(s, f) for s, f in enumerate(partners)]
            swap = [(number(a, 0), number(b, 0)) for s, f in pairs for a, b in ((s, f), (f, s))]
            got = [lax.ppermute(sent, axes, swap) for sent in (sent_first, sent_second)]
            source = me[0]
            paired = functools.reduce(jnp.logical_or, [source == f for f in partners])
            takes = [(place[0] == 0) & paired, (place[0] == 0) & (source < movers)]
            own = [
                [jnp.where(takes[h], got[k], halves[2 * h + k]) for k in range(2)] for h in range(2)
            ]
            ring = list(range(0, count, 2)) + list(range(count - 1, 0, -2))
            position = jnp.where(source % 2 == 0, source // 2, count - 1 - source // 2)
            half = count // 2
            away = [0] + [d for step in range(1, half) for d in (-step, step)] + [half]
            position = (position + jnp.array(away, jnp.int32) + count) % count
            ids = jnp.where(position < half, 2 * position, 2 * (count - 1 - position) + 1)
            tables = [[2 * s + h for s in range(count)] for h in range(2)]
            for s, f in pairs:
                tables[0][f], tables[1][s] = 2 * s + 1, 2 * f
            spots = [
                jnp.where(place[0] == 0, lookup(tables[h], ids), 2 * ids + h).astype(jnp.int32)
                for h in range(2)
            ]
            top, steps = ring_pass([[piece] * 2 for piece in own[0]], ring)
            free = gate(own[1], [steps[-2][0][0]])
            full = gate(free, [steps[-1][0][0]])
            rest, steps = ring_pass([[full[0], free[0]], [free[1], full[1]]], ring)
            after = [steps[0][0][1], steps[0][1][0]]
            near = [steps[i][0] + steps[i][1] for i in (0, -2)]
            top_spots, cut = spots[0], 2 * half - 2
            groups = [
                (
                    [top[k] + rest[k][:cut] for k in range(2)],
                    jnp.concatenate([spots[0], spots[1][:cut]]),
                ),
                ([rest[k][cut:] for k in range(2)], spots[1][cut:]),
            ]
        first, second = solve_panels(top_spots, place, top, right_side, after, width, block)
        solved = [
            spread_near(spread_far(first, places, place), places, near[0]),
            spread_near(spread_far(second, places, place), places, near[1]),
        ]
        result = None
        for held, spots in groups:
            result = update(spots, place, held, right_side, solved, width, result)
        return result

    placed = (P(("row", "src"), None), P("row", "src"))
    return jax.shard_map(
        local, mesh=mesh, in_specs=placed, out_specs=P("row", "src"), check_vma=False
    )
```

```python
import functools
import math

import jax
import jax.numpy as jnp
from jax import lax
from jax.experimental import pallas as pl
from jax.experimental.pallas import tpu as pltpu
from jax.sharding import PartitionSpec as P

VMEM_BYTES = 52 * 1024 * 1024
LANES = 128
SHORT = pl.CostEstimate(flops=1000, bytes_accessed=1000, transcendentals=0)
RING_LIMIT = 16

ANY = pl.BlockSpec(memory_space=pltpu.HBM)
SCALARS = pl.BlockSpec(memory_space=pltpu.SMEM)
WHOLE = pl.BlockSpec(memory_space=pltpu.VMEM)


def dot32(a, b):
    return jnp.dot(a, b, preferred_element_type=jnp.float32, precision=lax.Precision.HIGHEST)


def split16(value):
    high = value.astype(jnp.bfloat16)
    return high, (value - high.astype(jnp.float32)).astype(jnp.bfloat16)


def dot_split(a, b):
    (a_high, a_low), (b_high, b_low) = a, b
    dot = functools.partial(jnp.dot, preferred_element_type=jnp.float32)
    return dot(a_high, b_high) + dot(a_high, b_low) + dot(a_low, b_high)


def grid_ids(size):
    return [lax.broadcasted_iota(jnp.int32, (size, size), axis) for axis in range(2)]


def below_blocks(half, row, col):
    return (row // half % 2 == 1) & (col // half == row // half - 1)


def invert_lower(blocks):
    size = blocks[0].shape[0]
    row, col = grid_ids(size)
    inverses = []
    for block in blocks:
        diag = jnp.where(row == col, block, 0.0)
        down = 1.0 / jnp.sum(diag, axis=1, keepdims=True)
        across = 1.0 / jnp.sum(diag, axis=0, keepdims=True)
        below = below_blocks(1, row, col)
        inverses.append(
            jnp.where(row == col, down, 0.0) - jnp.where(below, down * block * across, 0.0)
        )
    half = 2
    while half < size:
        below = below_blocks(half, row, col)
        inner = [
            dot32(jnp.where(below, block, 0.0), inverse) for block, inverse in zip(blocks, inverses)
        ]
        inverses = [inverse - dot32(inverse, part) for inverse, part in zip(inverses, inner)]
        half *= 2
    return inverses


def prepare_kernel(rows, block, depth, cuts, movers, me, place, source, *refs):
    *outs, factor, load_sem, store_sem = refs
    width, part = depth // 2, rows // cuts
    load = pltpu.make_async_copy(source, factor, load_sem)
    load.start()
    load.wait()
    first = me[0] * rows

    @pl.when((place[0] == 0) & (first < depth))
    def _():
        blocks = []
        for j in range(0, rows, block):
            at = jnp.minimum(first + j, depth - block)
            near = pl.multiple_of(at // LANES * LANES, LANES)
            value = factor[j : j + block, pl.ds(near, LANES)]
            value = pltpu.roll(value, (LANES - at % LANES) % LANES, 1)
            blocks.append(value[:, :block])
        row, col = grid_ids(block)
        blocks = [
            jnp.where(first + i * block < depth, value, jnp.where(row == col, 1.0, 0.0))
            for i, value in enumerate(blocks)
        ]
        for i, inverse in enumerate(invert_lower(blocks)):

            @pl.when(first + i * block < depth)
            def _(i=i, inverse=inverse):
                factor[i * block : (i + 1) * block, depth - block :] = inverse

    moves = me[0] < movers
    panel = pl.ds(width, width)
    copies = [
        (factor.at[pl.ds(cut * part, part), panel], outs[cut], store_sem.at[cut])
        for cut in range(cuts)
    ]
    if cuts > 1:
        sent = pl.ds(pl.multiple_of(jnp.where(moves, part, 0), 8), part)
        copies.append((factor.at[sent, panel], outs[cuts], store_sem.at[cuts]))
    copies = [pltpu.make_async_copy(*copy) for copy in copies]
    for copy in copies:
        copy.start()
    for copy in copies:
        copy.wait()


def prepare(me, place, factor, block, cuts, movers):
    rows, depth = factor.shape
    count = cuts + (1 if cuts > 1 else 0)
    return pl.pallas_call(
        functools.partial(prepare_kernel, rows, block, depth, cuts, movers),
        out_shape=[jax.ShapeDtypeStruct((rows // cuts, depth // 2), jnp.float32)] * count,
        in_specs=[SCALARS] * 2 + [ANY],
        out_specs=[ANY] * count,
        scratch_shapes=[
            pltpu.VMEM((rows, depth), jnp.float32),
            pltpu.SemaphoreType.DMA,
            pltpu.SemaphoreType.DMA((count,)),
        ],
        compiler_params=pltpu.CompilerParams(vmem_limit_bytes=VMEM_BYTES),
        cost_estimate=SHORT,
    )(me, place, factor)


def solve_kernel(pieces, rows, width, chunk, block, ids, place, *refs):
    held, rhs = refs[: 2 * pieces], refs[2 * pieces]
    *outs, lower, solved, piece_sem, rhs_sem, out_sem = refs[len(refs) - 7 :]
    depth = 2 * width

    @pl.when(place[0] == 0)
    def _():
        def copies(i):
            at = pl.ds(pl.multiple_of(ids[i] * rows, 8), rows)
            return [
                pltpu.make_async_copy(
                    held[k * pieces + i], lower.at[at, pl.ds(k * width, width)], piece_sem.at[k, i]
                )
                for k in range(2)
            ]

        for i in range(pieces):

            @pl.when(ids[i] * rows < depth)
            def _(i=i):
                for copy in copies(i):
                    copy.start()

        load = pltpu.make_async_copy(rhs.at[pl.ds(0, depth)], solved, rhs_sem)
        load.start()
        for i in range(pieces):

            @pl.when(ids[i] * rows < depth)
            def _(i=i):
                for copy in copies(i):
                    copy.wait()

        row, col = grid_ids(chunk)
        lane = lax.broadcasted_iota(jnp.int32, (chunk, LANES), 1)
        starts = range(0, depth, chunk)
        inverses = []
        for j in starts:
            value = lower[j : j + chunk, depth - LANES :]
            value = jnp.where(lane >= LANES - block, value, 0.0)
            shift = block
            while shift < LANES:
                value = value + pltpu.roll(value, LANES - shift, 1)
                shift *= 2
            value = jnp.concatenate([value] * (chunk // LANES), axis=1)
            inverses.append(jnp.where(row // block == col // block, value, 0.0))
        half = block
        while half < chunk:
            below = below_blocks(half, row, col)
            parts = [split16(inverse) for inverse in inverses]
            inner = [
                dot_split(
                    split16(jnp.where(below, lower[j : j + chunk, j : j + chunk], 0.0)), part
                )
                for j, part in zip(starts, parts)
            ]
            inverses = [
                inverse - dot_split(part, split16(value))
                for inverse, part, value in zip(inverses, parts, inner)
            ]
            half *= 2
        load.wait()
        stores = [
            pltpu.make_async_copy(solved.at[pl.ds(k * width, width)], outs[k], out_sem.at[k])
            for k in range(2)
        ]
        for j in starts:
            value = solved[j : j + chunk]
            if j:
                value = value - dot_split(
                    split16(lower[j : j + chunk, :j]), split16(solved[:j])
                )
            solved[j : j + chunk] = dot_split(split16(inverses[j // chunk]), split16(value))
            if (j + chunk) % width == 0:
                stores[j // width].start()
        for store in stores:
            store.wait()


def solve_panels(ids, place, held, rhs, after, width, block):
    pieces = len(held[0])
    rows = held[0][0].shape[0]
    columns, depth = rhs.shape[1], 2 * width
    tall = -(-depth // rows) * rows
    chunk = math.gcd(width, 2 * LANES)
    return pl.pallas_call(
        functools.partial(solve_kernel, pieces, rows, width, chunk, block),
        out_shape=[jax.ShapeDtypeStruct((width, columns), jnp.float32)] * 2,
        in_specs=[SCALARS] * 2 + [ANY] * (2 * pieces + 1 + len(after)),
        out_specs=[ANY] * 2,
        scratch_shapes=[
            pltpu.VMEM((tall, depth), jnp.float32),
            pltpu.VMEM((depth, columns), jnp.float32),
            pltpu.SemaphoreType.DMA((2, pieces)),
            pltpu.SemaphoreType.DMA,
            pltpu.SemaphoreType.DMA((2,)),
        ],
        compiler_params=pltpu.CompilerParams(vmem_limit_bytes=VMEM_BYTES),
        cost_estimate=pl.CostEstimate(
            flops=72 * width * width * columns,
            bytes_accessed=24 * width * columns,
            transcendentals=0,
        ),
    )(ids, place, *held[0], *held[1], rhs, *after)


def update_kernel(pieces, rows, width, group, tile, step, places, ids, place, *refs):
    held, refs = refs[: 2 * pieces], refs[2 * pieces :]
    rhs, refs = refs[0], refs[1:]
    solved, refs = refs[: 2 * places], refs[2 * places :]
    refs = refs[len(refs) - 11 :]
    out, lower, block, found, high, low, product, piece_sem, block_sem, found_sem, out_sem = refs
    depth = 2 * width
    start = place[0] * rhs.shape[0]

    def fetch(k, r):
        return pltpu.make_async_copy(
            solved[k * places + r], found.at[pl.ds(k * width, width)], found_sem.at[k]
        )

    def at(i):
        return pl.ds(pl.multiple_of(ids[i] * rows, 8), rows)

    def load(k, i, source):
        return pltpu.make_async_copy(
            held[source],
            lower.at[pl.ds(pl.multiple_of(i * rows, 8), rows), pl.ds(k * width, width)],
            piece_sem.at[k, i],
        )

    def load_block(i):
        return pltpu.make_async_copy(rhs.at[at(i)], block.at[i], block_sem.at[i])

    def store(i):
        return pltpu.make_async_copy(block.at[i], out.at[at(i)], out_sem.at[i])

    for r in range(places):

        @pl.when(place[0] % places == r)
        def _(r=r):
            for k in range(2):
                fetch(k, r).start()

    for i in range(pieces):
        for k in range(2):
            load(k, i, k * pieces + i).start()
        load_block(i).start()
    for k in range(2):
        fetch(k, 0).wait()
    high[...], low[...] = split16(found[...])

    @pl.loop(0, pieces // group)
    def _(g):
        members = [g * group + u for u in range(group)]
        for i in members:
            for k in range(2):
                load(k, i, 0).wait()
            load_block(i).wait()

        @pl.loop(0, rows // tile)
        def _(t):
            inside = pl.multiple_of(t * tile, 8)
            tops = [start + ids[i] * rows + inside for i in members]
            highest = functools.reduce(jnp.maximum, tops)

            @pl.when(highest + tile > depth)
            def _():
                here = pl.ds(pl.multiple_of(g * group * rows + inside, 8), group * tile)
                product[...] = dot_split(split16(lower[here]), (high[...], low[...]))

            for u, (i, top) in enumerate(zip(members, tops)):

                @pl.when(top >= depth)
                def _(i=i, u=u):
                    here = pl.ds(inside, tile)
                    block[i, here] = block[i, here] - product[u * tile : (u + 1) * tile]

                @pl.when(top < depth)
                def _(i=i, u=u, top=top):
                    @pl.loop(0, tile // step)
                    def _(v):
                        part = pl.multiple_of(v * step, 8)
                        row = top + part
                        here = pl.ds(inside + part, step)

                        @pl.when(row < depth)
                        def _():
                            block[i, here] = found[pl.ds(pl.multiple_of(row, 8), step)]

                        @pl.when(row >= depth)
                        def _():
                            block[i, here] = (
                                block[i, here] - product[pl.ds(u * tile + part, step)]
                            )

        for i in members:
            store(i).start()

    @pl.loop(0, pieces)
    def _(i):
        store(i).wait()


def update(ids, place, held, rhs, solved, width, written=None):
    pieces, places = len(held[0]), len(solved[0])
    rows, columns = held[0][0].shape[0], rhs.shape[1]
    step = math.gcd(rows, 2 * width)
    tile = step * max(m for m in range(1, rows // step + 1) if rows // step % m == 0 and step * m <= 512)
    group = 2 if pieces % 2 == 0 and tile == rows else 1
    operands = [ids, place, *[piece for group in held for piece in group], rhs, *solved[0], *solved[1]]
    extra = [] if written is None else [written]
    return pl.pallas_call(
        functools.partial(update_kernel, pieces, rows, width, group, tile, step, places),
        out_shape=jax.ShapeDtypeStruct(rhs.shape, jnp.float32),
        in_specs=[SCALARS] * 2 + [ANY] * (len(operands) - 2 + len(extra)),
        out_specs=ANY,
        input_output_aliases={len(operands): 0} if extra else {},
        scratch_shapes=[
            pltpu.VMEM((pieces * rows, 2 * width), jnp.float32),
            pltpu.VMEM((pieces, rows, columns), jnp.float32),
            pltpu.VMEM((2 * width, columns), jnp.float32),
            pltpu.VMEM((2 * width, columns), jnp.bfloat16),
            pltpu.VMEM((2 * width, columns), jnp.bfloat16),
            pltpu.VMEM((group * tile, columns), jnp.float32),
            pltpu.SemaphoreType.DMA((2, pieces)),
            pltpu.SemaphoreType.DMA((pieces,)),
            pltpu.SemaphoreType.DMA((2,)),
            pltpu.SemaphoreType.DMA((pieces,)),
        ],
        compiler_params=pltpu.CompilerParams(vmem_limit_bytes=VMEM_BYTES),
        cost_estimate=pl.CostEstimate(
            flops=12 * pieces * rows * width * columns,
            bytes_accessed=8 * pieces * rows * (width + columns),
            transcendentals=0,
        ),
    )(*operands, *extra)


def gate_kernel(count, *refs):
    pass


def gate(blocks, tokens):
    count = len(blocks)
    return pl.pallas_call(
        functools.partial(gate_kernel, count),
        out_shape=[jax.ShapeDtypeStruct(block.shape, block.dtype) for block in blocks],
        in_specs=[ANY] * (count + len(tokens)),
        out_specs=[ANY] * count,
        input_output_aliases={i: i for i in range(count)},
        compiler_params=pltpu.CompilerParams(vmem_limit_bytes=VMEM_BYTES),
    )(*blocks, *tokens)


def ring_pass(starts, ring):
    count = len(ring)
    onward = [(ring[i], ring[(i + 1) % count]) for i in range(count)]
    back = [(b, a) for a, b in onward]
    held = [[starts[k][k]] for k in range(2)]
    going = [list(ways) for ways in starts]
    steps = []
    for step in range(1, count // 2 + 1):
        for k in range(2):
            for way, pairs in enumerate((onward, back)):
                if step == count // 2 and way != k:
                    continue
                going[k][way] = lax.ppermute(going[k][way], "src", pairs)
                held[k].append(going[k][way])
        steps.append([list(ways) for ways in going])
    return held, steps


def spread_far(block, count, place):
    found = {0: block}
    stride = count // 2
    while stride > 1:
        for r in list(found):
            found[r + stride] = lax.ppermute(found[r], "row", [(r, r + stride)])
        stride //= 2
    for r in found:
        if r:
            block = jnp.where(place[0] == r, found[r], block)
    return block


def spread_near(block, count, tokens):
    if tokens:
        (block,) = gate([block], tokens)
    return [block, lax.ppermute(block, "row", [(r, r + 1) for r in range(0, count - 1, 2)])]


def swap_partners(count, tops):
    free = [s for s in range(count) if 2 * s >= tops]
    partners = []
    for s in range(count):
        if 2 * s + 1 < tops:
            pool = [f for f in free if f % 2 == s % 2] or free
            if not pool:
                return None
            partners.append(pool[-1])
            free.remove(pool[-1])
    return partners


def lookup(table, index):
    hit = index[:, None] == jnp.arange(len(table), dtype=jnp.int32)[None, :]
    return jnp.sum(jnp.where(hit, jnp.array(table, jnp.int32)[None, :], 0), axis=1)


def solution(mesh):
    count, places = mesh.shape["src"], mesh.shape["row"]
    axes = tuple(mesh.axis_names)

    def number(source, row):
        at, place = {"src": source, "row": row}, 0
        for axis in axes:
            place = place * mesh.shape[axis] + at[axis]
        return place

    def local(factor, right_side):
        rows, depth = factor.shape
        width, part = depth // 2, rows // 2
        block = math.gcd(math.gcd(rows, width), LANES)
        me = lax.axis_index("src").reshape(1).astype(jnp.int32)
        place = lax.axis_index("row").reshape(1).astype(jnp.int32)
        partners = swap_partners(count, -(-depth // part))
        ringed = count % 2 == 0 and count <= RING_LIMIT and part % 8 == 0 and partners is not None
        if not ringed:
            held = [
                [lax.all_gather(panel, "src", axis=0, tiled=True)]
                for panel in (factor[:, :width], *prepare(me, place, factor, block, 1, 0))
            ]
            top, top_spots = held, jnp.zeros_like(me)
            groups = [(held, top_spots)]
            after, sends, near = [], [], [[], []]
        else:
            movers = len(partners)
            left = factor[:, :width]
            sent_first = jnp.where(me[0] < movers, left[part:], left[:part])
            *right, sent_second = prepare(me, place, factor, block, 2, movers)
            halves = [left[:part], right[0], left[part:], right[1]]
            pairs = [(s, f) for s, f in enumerate(partners)]
            swap = [(number(a, 0), number(b, 0)) for s, f in pairs for a, b in ((s, f), (f, s))]
            got = [lax.ppermute(sent, axes, swap) for sent in (sent_first, sent_second)]
            source = me[0]
            paired = functools.reduce(jnp.logical_or, [source == f for f in partners])
            takes = [(place[0] == 0) & paired, (place[0] == 0) & (source < movers)]
            own = [
                [jnp.where(takes[h], got[k], halves[2 * h + k]) for k in range(2)] for h in range(2)
            ]
            ring = list(range(0, count, 2)) + list(range(count - 1, 0, -2))
            position = jnp.where(source % 2 == 0, source // 2, count - 1 - source // 2)
            half = count // 2
            away = [0] + [d for step in range(1, half) for d in (-step, step)] + [half]
            position = (position + jnp.array(away, jnp.int32) + count) % count
            ids = jnp.where(position < half, 2 * position, 2 * (count - 1 - position) + 1)
            tables = [[2 * s + h for s in range(count)] for h in range(2)]
            for s, f in pairs:
                tables[0][f], tables[1][s] = 2 * s + 1, 2 * f
            spots = [
                jnp.where(place[0] == 0, lookup(tables[h], ids), 2 * ids + h).astype(jnp.int32)
                for h in range(2)
            ]
            top, steps = ring_pass([[piece] * 2 for piece in own[0]], ring)
            free = gate(own[1], [steps[-2][0][0]])
            full = gate(free, [steps[-1][0][0]])
            rest, steps = ring_pass([[full[0], free[0]], [free[1], full[1]]], ring)
            after, sends = [steps[0][0][1], steps[0][1][0]], [steps[0][0][0], steps[0][1][1]]
            near = [steps[i][0] + steps[i][1] for i in (0, -2)]
            top_spots, cut = spots[0], 2 * half - 2
            groups = [
                (
                    [top[k] + rest[k][:cut] for k in range(2)],
                    jnp.concatenate([spots[0], spots[1][:cut]]),
                ),
                ([rest[k][cut:] for k in range(2)], spots[1][cut:]),
            ]
        first, second = solve_panels(top_spots, place, top, right_side, after, width, block)
        if sends:
            first, second = gate([first, second], sends)
        solved = [
            spread_near(spread_far(first, places, place), places, near[0]),
            spread_near(spread_far(second, places, place), places, near[1]),
        ]
        result = None
        for held, spots in groups:
            result = update(spots, place, held, right_side, solved, width, result)
        return result

    placed = (P(("row", "src"), None), P("row", "src"))
    return jax.shard_map(
        local, mesh=mesh, in_specs=placed, out_specs=P("row", "src"), check_vma=False
    )
```

```python
import functools
import math

import jax
import jax.numpy as jnp
from jax import lax
from jax.experimental import pallas as pl
from jax.experimental.pallas import tpu as pltpu
from jax.sharding import PartitionSpec as P

VMEM_BYTES = 52 * 1024 * 1024
LANES = 128
SHORT = pl.CostEstimate(flops=1000, bytes_accessed=1000, transcendentals=0)
RING_LIMIT = 16

ANY = pl.BlockSpec(memory_space=pltpu.HBM)
SCALARS = pl.BlockSpec(memory_space=pltpu.SMEM)
WHOLE = pl.BlockSpec(memory_space=pltpu.VMEM)


def dot32(a, b):
    return jnp.dot(a, b, preferred_element_type=jnp.float32, precision=lax.Precision.HIGHEST)


def split16(value):
    high = value.astype(jnp.bfloat16)
    return high, (value - high.astype(jnp.float32)).astype(jnp.bfloat16)


def dot_split(a, b):
    (a_high, a_low), (b_high, b_low) = a, b
    dot = functools.partial(jnp.dot, preferred_element_type=jnp.float32)
    return dot(a_high, b_high) + dot(a_high, b_low) + dot(a_low, b_high)


def grid_ids(size):
    return [lax.broadcasted_iota(jnp.int32, (size, size), axis) for axis in range(2)]


def below_blocks(half, row, col):
    return (row // half % 2 == 1) & (col // half == row // half - 1)


def invert_lower(blocks):
    size = blocks[0].shape[0]
    row, col = grid_ids(size)
    inverses = []
    for block in blocks:
        diag = jnp.where(row == col, block, 0.0)
        down = 1.0 / jnp.sum(diag, axis=1, keepdims=True)
        across = 1.0 / jnp.sum(diag, axis=0, keepdims=True)
        below = below_blocks(1, row, col)
        inverses.append(
            jnp.where(row == col, down, 0.0) - jnp.where(below, down * block * across, 0.0)
        )
    half = 2
    while half < size:
        below = below_blocks(half, row, col)
        inner = [
            dot32(jnp.where(below, block, 0.0), inverse) for block, inverse in zip(blocks, inverses)
        ]
        inverses = [inverse - dot32(inverse, part) for inverse, part in zip(inverses, inner)]
        half *= 2
    return inverses


def prepare_kernel(rows, block, depth, cuts, movers, me, place, source, *refs):
    *outs, factor, load_sem, store_sem = refs
    width, part = depth // 2, rows // cuts
    load = pltpu.make_async_copy(source, factor, load_sem)
    load.start()
    load.wait()
    first = me[0] * rows

    @pl.when((place[0] == 0) & (first < depth))
    def _():
        blocks = []
        for j in range(0, rows, block):
            at = jnp.minimum(first + j, depth - block)
            near = pl.multiple_of(at // LANES * LANES, LANES)
            value = factor[j : j + block, pl.ds(near, LANES)]
            value = pltpu.roll(value, (LANES - at % LANES) % LANES, 1)
            blocks.append(value[:, :block])
        row, col = grid_ids(block)
        blocks = [
            jnp.where(first + i * block < depth, value, jnp.where(row == col, 1.0, 0.0))
            for i, value in enumerate(blocks)
        ]
        for i, inverse in enumerate(invert_lower(blocks)):

            @pl.when(first + i * block < depth)
            def _(i=i, inverse=inverse):
                factor[i * block : (i + 1) * block, depth - block :] = inverse

    moves = me[0] < movers
    panel = pl.ds(width, width)
    copies = [
        (factor.at[pl.ds(cut * part, part), panel], outs[cut], store_sem.at[cut])
        for cut in range(cuts)
    ]
    if cuts > 1:
        sent = pl.ds(pl.multiple_of(jnp.where(moves, part, 0), 8), part)
        copies.append((factor.at[sent, panel], outs[cuts], store_sem.at[cuts]))
    copies = [pltpu.make_async_copy(*copy) for copy in copies]
    for copy in copies:
        copy.start()
    for copy in copies:
        copy.wait()


def prepare(me, place, factor, block, cuts, movers):
    rows, depth = factor.shape
    count = cuts + (1 if cuts > 1 else 0)
    return pl.pallas_call(
        functools.partial(prepare_kernel, rows, block, depth, cuts, movers),
        out_shape=[jax.ShapeDtypeStruct((rows // cuts, depth // 2), jnp.float32)] * count,
        in_specs=[SCALARS] * 2 + [ANY],
        out_specs=[ANY] * count,
        scratch_shapes=[
            pltpu.VMEM((rows, depth), jnp.float32),
            pltpu.SemaphoreType.DMA,
            pltpu.SemaphoreType.DMA((count,)),
        ],
        compiler_params=pltpu.CompilerParams(vmem_limit_bytes=VMEM_BYTES),
        cost_estimate=SHORT,
    )(me, place, factor)


def solve_kernel(pieces, rows, width, chunk, block, panel, ids, place, *refs):
    held, refs = refs[: 2 * pieces], refs[2 * pieces :]
    rhs, refs = refs[0], refs[1:]
    earlier = refs[:panel]
    solved, lower, piece_sem, rhs_sem = refs[len(refs) - 4 :]
    first, last = panel * width, (panel + 1) * width
    side = lower.shape[1] - LANES

    @pl.when(place[0] == 0)
    def _():
        def copies(i):
            at = pl.ds(pl.multiple_of(ids[i] * rows, 8), rows)
            cut = 0 if panel else width - LANES
            return [
                pltpu.make_async_copy(
                    held[i], lower.at[at, pl.ds(0, width)], piece_sem.at[0, i]
                ),
                pltpu.make_async_copy(
                    held[pieces + i].at[:, pl.ds(cut, width - cut)],
                    lower.at[at, pl.ds(width, width - cut)],
                    piece_sem.at[1, i],
                ),
            ]

        def needed(i):
            return (ids[i] * rows < last) & ((ids[i] + 1) * rows > first)

        for i in range(pieces):

            @pl.when(needed(i))
            def _(i=i):
                for copy in copies(i):
                    copy.start()

        load = pltpu.make_async_copy(rhs.at[pl.ds(first, width)], solved, rhs_sem)
        load.start()
        for i in range(pieces):

            @pl.when(needed(i))
            def _(i=i):
                for copy in copies(i):
                    copy.wait()

        load.wait()
        row, col = grid_ids(chunk)
        lane = lax.broadcasted_iota(jnp.int32, (chunk, LANES), 1)
        starts = range(0, width, chunk)
        inverses = []
        for j in starts:
            value = lower[first + j : first + j + chunk, side:]
            value = jnp.where(lane >= LANES - block, value, 0.0)
            shift = block
            while shift < LANES:
                value = value + pltpu.roll(value, LANES - shift, 1)
                shift *= 2
            value = jnp.concatenate([value] * (chunk // LANES), axis=1)
            inverses.append(jnp.where(row // block == col // block, value, 0.0))
        half = block
        while half < chunk:
            below = below_blocks(half, row, col)
            parts = [split16(inverse) for inverse in inverses]
            inner = [
                dot_split(
                    split16(
                        jnp.where(
                            below,
                            lower[first + j : first + j + chunk, first + j : first + j + chunk],
                            0.0,
                        )
                    ),
                    part,
                )
                for j, part in zip(starts, parts)
            ]
            inverses = [
                inverse - dot_split(part, split16(value))
                for inverse, part, value in zip(inverses, parts, inner)
            ]
            half *= 2
        for k in range(panel):
            solved[...] = solved[...] - dot_split(
                split16(lower[first:last, k * width : (k + 1) * width]), split16(earlier[k][...])
            )
        for j in starts:
            value = solved[j : j + chunk]
            if j:
                at = slice(first + j, first + j + chunk)
                value = value - dot_split(
                    split16(lower[at, first : first + j]), split16(solved[:j])
                )
            solved[j : j + chunk] = dot_split(split16(inverses[j // chunk]), split16(value))


def solve_panel(panel, ids, place, held, rhs, earlier, after, width, block):
    pieces = len(held[0])
    rows = held[0][0].shape[0]
    columns = rhs.shape[1]
    tall = -(-(panel + 1) * width // rows) * rows
    chunk = math.gcd(width, 2 * LANES)
    return pl.pallas_call(
        functools.partial(solve_kernel, pieces, rows, width, chunk, block, panel),
        out_shape=jax.ShapeDtypeStruct((width, columns), jnp.float32),
        in_specs=[SCALARS] * 2
        + [ANY] * (2 * pieces + 1)
        + [WHOLE] * panel
        + [ANY] * len(after),
        out_specs=WHOLE,
        scratch_shapes=[
            pltpu.VMEM((tall, 2 * width if panel else width + LANES), jnp.float32),
            pltpu.SemaphoreType.DMA((2, pieces)),
            pltpu.SemaphoreType.DMA,
        ],
        compiler_params=pltpu.CompilerParams(vmem_limit_bytes=VMEM_BYTES),
        cost_estimate=pl.CostEstimate(
            flops=24 * (panel + 1) * width * width * columns,
            bytes_accessed=12 * width * columns,
            transcendentals=0,
        ),
    )(ids, place, *held[0], *held[1], rhs, *earlier, *after)


def update_kernel(pieces, rows, width, group, tile, step, places, ids, place, *refs):
    held, refs = refs[: 2 * pieces], refs[2 * pieces :]
    rhs, refs = refs[0], refs[1:]
    solved, refs = refs[: 2 * places], refs[2 * places :]
    refs = refs[len(refs) - 11 :]
    out, lower, block, found, high, low, product, piece_sem, block_sem, found_sem, out_sem = refs
    depth = 2 * width
    start = place[0] * rhs.shape[0]

    def fetch(k, r):
        return pltpu.make_async_copy(
            solved[k * places + r], found.at[pl.ds(k * width, width)], found_sem.at[k]
        )

    def at(i):
        return pl.ds(pl.multiple_of(ids[i] * rows, 8), rows)

    def load(k, i, source):
        return pltpu.make_async_copy(
            held[source],
            lower.at[pl.ds(pl.multiple_of(i * rows, 8), rows), pl.ds(k * width, width)],
            piece_sem.at[k, i],
        )

    def load_block(i):
        return pltpu.make_async_copy(rhs.at[at(i)], block.at[i], block_sem.at[i])

    def store(i):
        return pltpu.make_async_copy(block.at[i], out.at[at(i)], out_sem.at[i])

    for r in range(places):

        @pl.when(place[0] % places == r)
        def _(r=r):
            for k in range(2):
                fetch(k, r).start()

    for i in range(pieces):
        for k in range(2):
            load(k, i, k * pieces + i).start()
        load_block(i).start()
    for k in range(2):
        fetch(k, 0).wait()
    high[...], low[...] = split16(found[...])

    @pl.loop(0, pieces // group)
    def _(g):
        members = [g * group + u for u in range(group)]
        for i in members:
            for k in range(2):
                load(k, i, 0).wait()
            load_block(i).wait()

        @pl.loop(0, rows // tile)
        def _(t):
            inside = pl.multiple_of(t * tile, 8)
            tops = [start + ids[i] * rows + inside for i in members]
            highest = functools.reduce(jnp.maximum, tops)

            @pl.when(highest + tile > depth)
            def _():
                here = pl.ds(pl.multiple_of(g * group * rows + inside, 8), group * tile)
                product[...] = dot_split(split16(lower[here]), (high[...], low[...]))

            for u, (i, top) in enumerate(zip(members, tops)):

                @pl.when(top >= depth)
                def _(i=i, u=u):
                    here = pl.ds(inside, tile)
                    block[i, here] = block[i, here] - product[u * tile : (u + 1) * tile]

                @pl.when(top < depth)
                def _(i=i, u=u, top=top):
                    @pl.loop(0, tile // step)
                    def _(v):
                        part = pl.multiple_of(v * step, 8)
                        row = top + part
                        here = pl.ds(inside + part, step)

                        @pl.when(row < depth)
                        def _():
                            block[i, here] = found[pl.ds(pl.multiple_of(row, 8), step)]

                        @pl.when(row >= depth)
                        def _():
                            block[i, here] = (
                                block[i, here] - product[pl.ds(u * tile + part, step)]
                            )

        for i in members:
            store(i).start()

    @pl.loop(0, pieces)
    def _(i):
        store(i).wait()


def update(ids, place, held, rhs, solved, width, written=None):
    pieces, places = len(held[0]), len(solved[0])
    rows, columns = held[0][0].shape[0], rhs.shape[1]
    step = math.gcd(rows, 2 * width)
    tile = step * max(m for m in range(1, rows // step + 1) if rows // step % m == 0 and step * m <= 512)
    group = 2 if pieces % 2 == 0 and tile == rows else 1
    operands = [ids, place, *[piece for group in held for piece in group], rhs, *solved[0], *solved[1]]
    extra = [] if written is None else [written]
    return pl.pallas_call(
        functools.partial(update_kernel, pieces, rows, width, group, tile, step, places),
        out_shape=jax.ShapeDtypeStruct(rhs.shape, jnp.float32),
        in_specs=[SCALARS] * 2 + [ANY] * (len(operands) - 2 + len(extra)),
        out_specs=ANY,
        input_output_aliases={len(operands): 0} if extra else {},
        scratch_shapes=[
            pltpu.VMEM((pieces * rows, 2 * width), jnp.float32),
            pltpu.VMEM((pieces, rows, columns), jnp.float32),
            pltpu.VMEM((2 * width, columns), jnp.float32),
            pltpu.VMEM((2 * width, columns), jnp.bfloat16),
            pltpu.VMEM((2 * width, columns), jnp.bfloat16),
            pltpu.VMEM((group * tile, columns), jnp.float32),
            pltpu.SemaphoreType.DMA((2, pieces)),
            pltpu.SemaphoreType.DMA((pieces,)),
            pltpu.SemaphoreType.DMA((2,)),
            pltpu.SemaphoreType.DMA((pieces,)),
        ],
        compiler_params=pltpu.CompilerParams(vmem_limit_bytes=VMEM_BYTES),
        cost_estimate=pl.CostEstimate(
            flops=12 * pieces * rows * width * columns,
            bytes_accessed=8 * pieces * rows * (width + columns),
            transcendentals=0,
        ),
    )(*operands, *extra)


def gate_kernel(count, *refs):
    pass


def gate(blocks, tokens):
    count = len(blocks)
    return pl.pallas_call(
        functools.partial(gate_kernel, count),
        out_shape=[jax.ShapeDtypeStruct(block.shape, block.dtype) for block in blocks],
        in_specs=[ANY] * (count + len(tokens)),
        out_specs=[ANY] * count,
        input_output_aliases={i: i for i in range(count)},
        compiler_params=pltpu.CompilerParams(vmem_limit_bytes=VMEM_BYTES),
    )(*blocks, *tokens)


def ring_pass(starts, ring):
    count = len(ring)
    onward = [(ring[i], ring[(i + 1) % count]) for i in range(count)]
    back = [(b, a) for a, b in onward]
    held = [[starts[k][k]] for k in range(2)]
    going = [list(ways) for ways in starts]
    steps = []
    for step in range(1, count // 2 + 1):
        for k in range(2):
            for way, pairs in enumerate((onward, back)):
                if step == count // 2 and way != k:
                    continue
                going[k][way] = lax.ppermute(going[k][way], "src", pairs)
                held[k].append(going[k][way])
        steps.append([list(ways) for ways in going])
    return held, steps


def spread_far(block, count):
    found = {0: block}
    stride = count // 2
    while stride > 1:
        for r in list(found):
            found[r + stride] = lax.ppermute(found[r], "row", [(r, r + stride)])
        stride //= 2
    return found


def spread_near(found, count, tokens):
    found = dict(found)
    for r in sorted(found):
        if r and tokens:
            (found[r],) = gate([found[r]], tokens)
        if r + 1 < count:
            found[r + 1] = lax.ppermute(found[r], "row", [(r, r + 1)])
    return [found[r] for r in range(count)]


def swap_partners(count, tops):
    free = [s for s in range(count) if 2 * s >= tops]
    partners = []
    for s in range(count):
        if 2 * s + 1 < tops:
            pool = [f for f in free if f % 2 == s % 2] or free
            if not pool:
                return None
            partners.append(pool[-1])
            free.remove(pool[-1])
    return partners


def lookup(table, index):
    hit = index[:, None] == jnp.arange(len(table), dtype=jnp.int32)[None, :]
    return jnp.sum(jnp.where(hit, jnp.array(table, jnp.int32)[None, :], 0), axis=1)


def solution(mesh):
    count, places = mesh.shape["src"], mesh.shape["row"]
    axes = tuple(mesh.axis_names)

    def number(source, row):
        at, place = {"src": source, "row": row}, 0
        for axis in axes:
            place = place * mesh.shape[axis] + at[axis]
        return place

    def local(factor, right_side):
        rows, depth = factor.shape
        width, part = depth // 2, rows // 2
        block = math.gcd(math.gcd(rows, width), LANES)
        me = lax.axis_index("src").reshape(1).astype(jnp.int32)
        place = lax.axis_index("row").reshape(1).astype(jnp.int32)
        partners = swap_partners(count, -(-depth // part))
        ringed = count % 2 == 0 and count <= RING_LIMIT and part % 8 == 0 and partners is not None
        if not ringed:
            held = [
                [lax.all_gather(panel, "src", axis=0, tiled=True)]
                for panel in (factor[:, :width], *prepare(me, place, factor, block, 1, 0))
            ]
            top, top_spots = held, jnp.zeros_like(me)
            groups = [(held, top_spots)]
            after, near = [[], []], [[], []]
        else:
            movers = len(partners)
            left = factor[:, :width]
            sent_first = jnp.where(me[0] < movers, left[part:], left[:part])
            *right, sent_second = prepare(me, place, factor, block, 2, movers)
            halves = [left[:part], right[0], left[part:], right[1]]
            pairs = [(s, f) for s, f in enumerate(partners)]
            swap = [(number(a, 0), number(b, 0)) for s, f in pairs for a, b in ((s, f), (f, s))]
            got = [lax.ppermute(sent, axes, swap) for sent in (sent_first, sent_second)]
            source = me[0]
            paired = functools.reduce(jnp.logical_or, [source == f for f in partners])
            takes = [(place[0] == 0) & paired, (place[0] == 0) & (source < movers)]
            own = [
                [jnp.where(takes[h], got[k], halves[2 * h + k]) for k in range(2)] for h in range(2)
            ]
            ring = list(range(0, count, 2)) + list(range(count - 1, 0, -2))
            position = jnp.where(source % 2 == 0, source // 2, count - 1 - source // 2)
            half = count // 2
            away = [0] + [d for step in range(1, half) for d in (-step, step)] + [half]
            position = (position + jnp.array(away, jnp.int32) + count) % count
            ids = jnp.where(position < half, 2 * position, 2 * (count - 1 - position) + 1)
            tables = [[2 * s + h for s in range(count)] for h in range(2)]
            for s, f in pairs:
                tables[0][f], tables[1][s] = 2 * s + 1, 2 * f
            spots = [
                jnp.where(place[0] == 0, lookup(tables[h], ids), 2 * ids + h).astype(jnp.int32)
                for h in range(2)
            ]
            top, steps = ring_pass([[piece] * 2 for piece in own[0]], ring)
            free = gate(own[1], [steps[-2][0][0]])
            full = gate(free, [steps[-1][0][0]])
            rest, steps = ring_pass([[full[0], free[0]], [free[1], full[1]]], ring)
            after = [[steps[0][0][1], steps[0][1][0]], [steps[0][0][0], steps[0][1][1]]]
            near = [steps[i][0] + steps[i][1] for i in (1, -2)]
            top_spots, cut = spots[0], 2 * half - 2
            groups = [
                (
                    [top[k] + rest[k][:cut] for k in range(2)],
                    jnp.concatenate([spots[0], spots[1][:cut]]),
                ),
                ([rest[k][cut:] for k in range(2)], spots[1][cut:]),
            ]
        first = solve_panel(0, top_spots, place, top, right_side, [], after[0], width, block)
        second = solve_panel(1, top_spots, place, top, right_side, [first], after[1], width, block)
        solved = [
            spread_near(spread_far(first, places), places, near[0]),
            spread_near(spread_far(second, places), places, near[1]),
        ]
        result = None
        for held, spots in groups:
            result = update(spots, place, held, right_side, solved, width, result)
        return result

    placed = (P(("row", "src"), None), P("row", "src"))
    return jax.shard_map(
        local, mesh=mesh, in_specs=placed, out_specs=P("row", "src"), check_vma=False
    )
```

```python
import functools
import math

import jax
import jax.numpy as jnp
from jax import lax
from jax.experimental import pallas as pl
from jax.experimental.pallas import tpu as pltpu
from jax.sharding import PartitionSpec as P

VMEM_BYTES = 52 * 1024 * 1024
LANES = 128
SHORT = pl.CostEstimate(flops=1000, bytes_accessed=1000, transcendentals=0)
RING_LIMIT = 16

ANY = pl.BlockSpec(memory_space=pltpu.HBM)
SCALARS = pl.BlockSpec(memory_space=pltpu.SMEM)
WHOLE = pl.BlockSpec(memory_space=pltpu.VMEM)


def dot32(a, b):
    return jnp.dot(a, b, preferred_element_type=jnp.float32, precision=lax.Precision.HIGHEST)


def split16(value):
    high = value.astype(jnp.bfloat16)
    return high, (value - high.astype(jnp.float32)).astype(jnp.bfloat16)


def dot_split(a, b):
    (a_high, a_low), (b_high, b_low) = a, b
    dot = functools.partial(jnp.dot, preferred_element_type=jnp.float32)
    return dot(a_high, b_high) + dot(a_high, b_low) + dot(a_low, b_high)


def grid_ids(size):
    return [lax.broadcasted_iota(jnp.int32, (size, size), axis) for axis in range(2)]


def below_blocks(half, row, col):
    return (row // half % 2 == 1) & (col // half == row // half - 1)


def invert_lower(blocks):
    size = blocks[0].shape[0]
    row, col = grid_ids(size)
    inverses = []
    for block in blocks:
        diag = jnp.where(row == col, block, 0.0)
        down = 1.0 / jnp.sum(diag, axis=1, keepdims=True)
        across = 1.0 / jnp.sum(diag, axis=0, keepdims=True)
        below = below_blocks(1, row, col)
        inverses.append(
            jnp.where(row == col, down, 0.0) - jnp.where(below, down * block * across, 0.0)
        )
    half = 2
    while half < size:
        below = below_blocks(half, row, col)
        inner = [
            dot32(jnp.where(below, block, 0.0), inverse) for block, inverse in zip(blocks, inverses)
        ]
        inverses = [inverse - dot32(inverse, part) for inverse, part in zip(inverses, inner)]
        half *= 2
    return inverses


def prepare_kernel(rows, block, depth, cuts, movers, me, place, source, *refs):
    *outs, factor, load_sem, store_sem = refs
    width, part = depth // 2, rows // cuts
    load = pltpu.make_async_copy(source, factor, load_sem)
    load.start()
    load.wait()
    first = me[0] * rows

    @pl.when((place[0] == 0) & (first < depth))
    def _():
        blocks = []
        for j in range(0, rows, block):
            at = jnp.minimum(first + j, depth - block)
            near = pl.multiple_of(at // LANES * LANES, LANES)
            value = factor[j : j + block, pl.ds(near, LANES)]
            value = pltpu.roll(value, (LANES - at % LANES) % LANES, 1)
            blocks.append(value[:, :block])
        row, col = grid_ids(block)
        blocks = [
            jnp.where(first + i * block < depth, value, jnp.where(row == col, 1.0, 0.0))
            for i, value in enumerate(blocks)
        ]
        for i, inverse in enumerate(invert_lower(blocks)):

            @pl.when(first + i * block < depth)
            def _(i=i, inverse=inverse):
                factor[i * block : (i + 1) * block, depth - block :] = inverse

    moves = me[0] < movers
    panel = pl.ds(width, width)
    copies = [
        (factor.at[pl.ds(cut * part, part), panel], outs[cut], store_sem.at[cut])
        for cut in range(cuts)
    ]
    if cuts > 1:
        sent = pl.ds(pl.multiple_of(jnp.where(moves, part, 0), 8), part)
        copies.append((factor.at[sent, panel], outs[cuts], store_sem.at[cuts]))
    copies = [pltpu.make_async_copy(*copy) for copy in copies]
    for copy in copies:
        copy.start()
    for copy in copies:
        copy.wait()


def prepare(me, place, factor, block, cuts, movers):
    rows, depth = factor.shape
    count = cuts + (1 if cuts > 1 else 0)
    return pl.pallas_call(
        functools.partial(prepare_kernel, rows, block, depth, cuts, movers),
        out_shape=[jax.ShapeDtypeStruct((rows // cuts, depth // 2), jnp.float32)] * count,
        in_specs=[SCALARS] * 2 + [ANY],
        out_specs=[ANY] * count,
        scratch_shapes=[
            pltpu.VMEM((rows, depth), jnp.float32),
            pltpu.SemaphoreType.DMA,
            pltpu.SemaphoreType.DMA((count,)),
        ],
        compiler_params=pltpu.CompilerParams(vmem_limit_bytes=VMEM_BYTES),
        cost_estimate=SHORT,
    )(me, place, factor)


def solve_kernel(pieces, rows, width, chunk, block, ids, place, *refs):
    held, rhs = refs[: 2 * pieces], refs[2 * pieces]
    *outs, lower, solved, piece_sem, rhs_sem, out_sem = refs[len(refs) - 7 :]
    depth = 2 * width

    @pl.when(place[0] == 0)
    def _():
        def copies(i):
            at = pl.ds(pl.multiple_of(ids[i] * rows, 8), rows)
            return [
                pltpu.make_async_copy(
                    held[k * pieces + i], lower.at[at, pl.ds(k * width, width)], piece_sem.at[k, i]
                )
                for k in range(2)
            ]

        for i in range(pieces):

            @pl.when(ids[i] * rows < depth)
            def _(i=i):
                for copy in copies(i):
                    copy.start()

        load = pltpu.make_async_copy(rhs.at[pl.ds(0, depth)], solved, rhs_sem)
        load.start()
        for i in range(pieces):

            @pl.when(ids[i] * rows < depth)
            def _(i=i):
                for copy in copies(i):
                    copy.wait()

        row, col = grid_ids(chunk)
        lane = lax.broadcasted_iota(jnp.int32, (chunk, LANES), 1)
        starts = range(0, depth, chunk)
        inverses = []
        for j in starts:
            value = lower[j : j + chunk, depth - LANES :]
            value = jnp.where(lane >= LANES - block, value, 0.0)
            shift = block
            while shift < LANES:
                value = value + pltpu.roll(value, LANES - shift, 1)
                shift *= 2
            value = jnp.concatenate([value] * (chunk // LANES), axis=1)
            inverses.append(jnp.where(row // block == col // block, value, 0.0))
        half = block
        while half < chunk:
            below = below_blocks(half, row, col)
            parts = [split16(inverse) for inverse in inverses]
            inner = [
                dot_split(
                    split16(jnp.where(below, lower[j : j + chunk, j : j + chunk], 0.0)), part
                )
                for j, part in zip(starts, parts)
            ]
            inverses = [
                inverse - dot_split(part, split16(value))
                for inverse, part, value in zip(inverses, parts, inner)
            ]
            half *= 2
        load.wait()
        stores = [
            pltpu.make_async_copy(solved.at[pl.ds(k * width, width)], outs[k], out_sem.at[k])
            for k in range(2)
        ]
        for j in starts:
            value = solved[j : j + chunk]
            if j:
                value = value - dot_split(
                    split16(lower[j : j + chunk, :j]), split16(solved[:j])
                )
            solved[j : j + chunk] = dot_split(split16(inverses[j // chunk]), split16(value))
            if (j + chunk) % width == 0:
                stores[j // width].start()
        for store in stores:
            store.wait()


def solve_panels(ids, place, held, rhs, after, width, block):
    pieces = len(held[0])
    rows = held[0][0].shape[0]
    columns, depth = rhs.shape[1], 2 * width
    tall = -(-depth // rows) * rows
    chunk = math.gcd(width, 2 * LANES)
    return pl.pallas_call(
        functools.partial(solve_kernel, pieces, rows, width, chunk, block),
        out_shape=[jax.ShapeDtypeStruct((width, columns), jnp.float32)] * 2,
        in_specs=[SCALARS] * 2 + [ANY] * (2 * pieces + 1 + len(after)),
        out_specs=[ANY] * 2,
        scratch_shapes=[
            pltpu.VMEM((tall, depth), jnp.float32),
            pltpu.VMEM((depth, columns), jnp.float32),
            pltpu.SemaphoreType.DMA((2, pieces)),
            pltpu.SemaphoreType.DMA,
            pltpu.SemaphoreType.DMA((2,)),
        ],
        compiler_params=pltpu.CompilerParams(vmem_limit_bytes=VMEM_BYTES),
        cost_estimate=pl.CostEstimate(
            flops=72 * width * width * columns,
            bytes_accessed=24 * width * columns,
            transcendentals=0,
        ),
    )(ids, place, *held[0], *held[1], rhs, *after)


def update_kernel(pieces, rows, width, group, tile, step, places, ids, place, *refs):
    held, refs = refs[: 2 * pieces], refs[2 * pieces :]
    rhs, refs = refs[0], refs[1:]
    solved, refs = refs[: 2 * places], refs[2 * places :]
    refs = refs[len(refs) - 11 :]
    out, lower, block, found, high, low, product, piece_sem, block_sem, found_sem, out_sem = refs
    depth = 2 * width
    start = place[0] * rhs.shape[0]

    def fetch(k, r):
        return pltpu.make_async_copy(
            solved[k * places + r], found.at[pl.ds(k * width, width)], found_sem.at[k]
        )

    def at(i):
        return pl.ds(pl.multiple_of(ids[i] * rows, 8), rows)

    def load(k, i, source):
        return pltpu.make_async_copy(
            held[source],
            lower.at[pl.ds(pl.multiple_of(i * rows, 8), rows), pl.ds(k * width, width)],
            piece_sem.at[k, i],
        )

    def load_block(i):
        return pltpu.make_async_copy(rhs.at[at(i)], block.at[i], block_sem.at[i])

    def store(i):
        return pltpu.make_async_copy(block.at[i], out.at[at(i)], out_sem.at[i])

    for r in range(places):

        @pl.when(place[0] % places == r)
        def _(r=r):
            for k in range(2):
                fetch(k, r).start()

    for i in range(pieces):
        for k in range(2):
            load(k, i, k * pieces + i).start()
        load_block(i).start()
    for k in range(2):
        fetch(k, 0).wait()
    high[...], low[...] = split16(found[...])

    @pl.loop(0, pieces // group)
    def _(g):
        members = [g * group + u for u in range(group)]
        for i in members:
            for k in range(2):
                load(k, i, 0).wait()
            load_block(i).wait()

        @pl.loop(0, rows // tile)
        def _(t):
            inside = pl.multiple_of(t * tile, 8)
            tops = [start + ids[i] * rows + inside for i in members]
            highest = functools.reduce(jnp.maximum, tops)

            @pl.when(highest + tile > depth)
            def _():
                here = pl.ds(pl.multiple_of(g * group * rows + inside, 8), group * tile)
                product[...] = dot_split(split16(lower[here]), (high[...], low[...]))

            for u, (i, top) in enumerate(zip(members, tops)):

                @pl.when(top >= depth)
                def _(i=i, u=u):
                    here = pl.ds(inside, tile)
                    block[i, here] = block[i, here] - product[u * tile : (u + 1) * tile]

                @pl.when(top < depth)
                def _(i=i, u=u, top=top):
                    @pl.loop(0, tile // step)
                    def _(v):
                        part = pl.multiple_of(v * step, 8)
                        row = top + part
                        here = pl.ds(inside + part, step)

                        @pl.when(row < depth)
                        def _():
                            block[i, here] = found[pl.ds(pl.multiple_of(row, 8), step)]

                        @pl.when(row >= depth)
                        def _():
                            block[i, here] = (
                                block[i, here] - product[pl.ds(u * tile + part, step)]
                            )

        for i in members:
            store(i).start()

    @pl.loop(0, pieces)
    def _(i):
        store(i).wait()


def update(ids, place, held, rhs, solved, width, written=None):
    pieces, places = len(held[0]), len(solved[0])
    rows, columns = held[0][0].shape[0], rhs.shape[1]
    step = math.gcd(rows, 2 * width)
    tile = step * max(m for m in range(1, rows // step + 1) if rows // step % m == 0 and step * m <= 512)
    group = 2 if pieces % 2 == 0 and tile == rows else 1
    operands = [ids, place, *[piece for group in held for piece in group], rhs, *solved[0], *solved[1]]
    extra = [] if written is None else [written]
    return pl.pallas_call(
        functools.partial(update_kernel, pieces, rows, width, group, tile, step, places),
        out_shape=jax.ShapeDtypeStruct(rhs.shape, jnp.float32),
        in_specs=[SCALARS] * 2 + [ANY] * (len(operands) - 2 + len(extra)),
        out_specs=ANY,
        input_output_aliases={len(operands): 0} if extra else {},
        scratch_shapes=[
            pltpu.VMEM((pieces * rows, 2 * width), jnp.float32),
            pltpu.VMEM((pieces, rows, columns), jnp.float32),
            pltpu.VMEM((2 * width, columns), jnp.float32),
            pltpu.VMEM((2 * width, columns), jnp.bfloat16),
            pltpu.VMEM((2 * width, columns), jnp.bfloat16),
            pltpu.VMEM((group * tile, columns), jnp.float32),
            pltpu.SemaphoreType.DMA((2, pieces)),
            pltpu.SemaphoreType.DMA((pieces,)),
            pltpu.SemaphoreType.DMA((2,)),
            pltpu.SemaphoreType.DMA((pieces,)),
        ],
        compiler_params=pltpu.CompilerParams(vmem_limit_bytes=VMEM_BYTES),
        cost_estimate=pl.CostEstimate(
            flops=12 * pieces * rows * width * columns,
            bytes_accessed=8 * pieces * rows * (width + columns),
            transcendentals=0,
        ),
    )(*operands, *extra)


def gate_kernel(count, *refs):
    pass


def gate(blocks, tokens):
    count = len(blocks)
    return pl.pallas_call(
        functools.partial(gate_kernel, count),
        out_shape=[jax.ShapeDtypeStruct(block.shape, block.dtype) for block in blocks],
        in_specs=[ANY] * (count + len(tokens)),
        out_specs=[ANY] * count,
        input_output_aliases={i: i for i in range(count)},
        compiler_params=pltpu.CompilerParams(vmem_limit_bytes=VMEM_BYTES),
    )(*blocks, *tokens)


def ring_pass(starts, ring):
    count = len(ring)
    onward = [(ring[i], ring[(i + 1) % count]) for i in range(count)]
    back = [(b, a) for a, b in onward]
    held = [[starts[k][k]] for k in range(2)]
    going = [list(ways) for ways in starts]
    steps = []
    for step in range(1, count // 2 + 1):
        for k in range(2):
            for way, pairs in enumerate((onward, back)):
                if step == count // 2 and way != k:
                    continue
                going[k][way] = lax.ppermute(going[k][way], "src", pairs)
                held[k].append(going[k][way])
        steps.append([list(ways) for ways in going])
    return held, steps


def spread_far(block, count, place):
    found = {0: block}
    stride = count // 2
    while stride > 1:
        for r in list(found):
            found[r + stride] = lax.ppermute(found[r], "row", [(r, r + stride)])
        stride //= 2
    for r in found:
        if r:
            block = jnp.where(place[0] == r, found[r], block)
    return block


def spread_near(block, count, tokens):
    if tokens:
        (block,) = gate([block], tokens)
    return [block, lax.ppermute(block, "row", [(r, r + 1) for r in range(0, count - 1, 2)])]


def swap_partners(count, tops):
    free = [s for s in range(count) if 2 * s >= tops]
    partners = []
    for s in range(count):
        if 2 * s + 1 < tops:
            pool = [f for f in free if f % 2 == s % 2] or free
            if not pool:
                return None
            partners.append(pool[-1])
            free.remove(pool[-1])
    return partners


def lookup(table, index):
    hit = index[:, None] == jnp.arange(len(table), dtype=jnp.int32)[None, :]
    return jnp.sum(jnp.where(hit, jnp.array(table, jnp.int32)[None, :], 0), axis=1)


def solution(mesh):
    count, places = mesh.shape["src"], mesh.shape["row"]
    axes = tuple(mesh.axis_names)

    def number(source, row):
        at, place = {"src": source, "row": row}, 0
        for axis in axes:
            place = place * mesh.shape[axis] + at[axis]
        return place

    def local(factor, right_side):
        rows, depth = factor.shape
        width, part = depth // 2, rows // 2
        block = math.gcd(math.gcd(rows, width), LANES)
        me = lax.axis_index("src").reshape(1).astype(jnp.int32)
        place = lax.axis_index("row").reshape(1).astype(jnp.int32)
        partners = swap_partners(count, -(-depth // part))
        ringed = count % 2 == 0 and count <= RING_LIMIT and part % 8 == 0 and partners is not None
        if not ringed:
            held = [
                [lax.all_gather(panel, "src", axis=0, tiled=True)]
                for panel in (factor[:, :width], *prepare(me, place, factor, block, 1, 0))
            ]
            top, top_spots = held, jnp.zeros_like(me)
            groups = [(held, top_spots)]
            after, sends, near = [], [], [[], []]
        else:
            movers = len(partners)
            left = factor[:, :width]
            sent_first = jnp.where(me[0] < movers, left[part:], left[:part])
            *right, sent_second = prepare(me, place, factor, block, 2, movers)
            halves = [left[:part], right[0], left[part:], right[1]]
            pairs = [(s, f) for s, f in enumerate(partners)]
            swap = [(number(a, 0), number(b, 0)) for s, f in pairs for a, b in ((s, f), (f, s))]
            got = [lax.ppermute(sent, axes, swap) for sent in (sent_first, sent_second)]
            source = me[0]
            paired = functools.reduce(jnp.logical_or, [source == f for f in partners])
            takes = [(place[0] == 0) & paired, (place[0] == 0) & (source < movers)]
            own = [
                [jnp.where(takes[h], got[k], halves[2 * h + k]) for k in range(2)] for h in range(2)
            ]
            ring = list(range(0, count, 2)) + list(range(count - 1, 0, -2))
            position = jnp.where(source % 2 == 0, source // 2, count - 1 - source // 2)
            half = count // 2
            away = [0] + [d for step in range(1, half) for d in (-step, step)] + [half]
            position = (position + jnp.array(away, jnp.int32) + count) % count
            ids = jnp.where(position < half, 2 * position, 2 * (count - 1 - position) + 1)
            tables = [[2 * s + h for s in range(count)] for h in range(2)]
            for s, f in pairs:
                tables[0][f], tables[1][s] = 2 * s + 1, 2 * f
            spots = [
                jnp.where(place[0] == 0, lookup(tables[h], ids), 2 * ids + h).astype(jnp.int32)
                for h in range(2)
            ]
            top, steps = ring_pass([[piece] * 2 for piece in own[0]], ring)
            free = gate(own[1], [steps[-2][0][0]])
            full = gate(free, [steps[-1][0][0], steps[-1][1][1]])
            rest, steps = ring_pass([[full[0], free[0]], [free[1], full[1]]], ring)
            after, sends = [steps[0][0][1], steps[0][1][0]], [steps[0][0][0], steps[0][1][1]]
            near = [steps[i][0] + steps[i][1] for i in (0, -2)]
            top_spots, cut = spots[0], 2 * half - 2
            groups = [
                (
                    [top[k] + rest[k][:cut] for k in range(2)],
                    jnp.concatenate([spots[0], spots[1][:cut]]),
                ),
                ([rest[k][cut:] for k in range(2)], spots[1][cut:]),
            ]
        first, second = solve_panels(top_spots, place, top, right_side, after, width, block)
        if sends:
            first, second = gate([first, second], sends)
        solved = [
            spread_near(spread_far(first, places, place), places, near[0]),
            spread_near(spread_far(second, places, place), places, near[1]),
        ]
        result = None
        for held, spots in groups:
            result = update(spots, place, held, right_side, solved, width, result)
        return result

    placed = (P(("row", "src"), None), P("row", "src"))
    return jax.shard_map(
        local, mesh=mesh, in_specs=placed, out_specs=P("row", "src"), check_vma=False
    )
```

```python
import functools
import math

import jax
import jax.numpy as jnp
from jax import lax
from jax.experimental import pallas as pl
from jax.experimental.pallas import tpu as pltpu
from jax.sharding import PartitionSpec as P

VMEM_BYTES = 52 * 1024 * 1024
LANES = 128
SHORT = pl.CostEstimate(flops=1000, bytes_accessed=1000, transcendentals=0)
RING_LIMIT = 16

ANY = pl.BlockSpec(memory_space=pltpu.HBM)
SCALARS = pl.BlockSpec(memory_space=pltpu.SMEM)
WHOLE = pl.BlockSpec(memory_space=pltpu.VMEM)


def dot32(a, b):
    return jnp.dot(a, b, preferred_element_type=jnp.float32, precision=lax.Precision.HIGHEST)


def split16(value):
    high = value.astype(jnp.bfloat16)
    return high, (value - high.astype(jnp.float32)).astype(jnp.bfloat16)


def dot_split(a, b):
    (a_high, a_low), (b_high, b_low) = a, b
    dot = functools.partial(jnp.dot, preferred_element_type=jnp.float32)
    return dot(a_high, b_high) + dot(a_high, b_low) + dot(a_low, b_high)


def grid_ids(size):
    return [lax.broadcasted_iota(jnp.int32, (size, size), axis) for axis in range(2)]


def below_blocks(half, row, col):
    return (row // half % 2 == 1) & (col // half == row // half - 1)


def invert_lower(blocks):
    size = blocks[0].shape[0]
    row, col = grid_ids(size)
    inverses = []
    for block in blocks:
        diag = jnp.where(row == col, block, 0.0)
        down = 1.0 / jnp.sum(diag, axis=1, keepdims=True)
        across = 1.0 / jnp.sum(diag, axis=0, keepdims=True)
        below = below_blocks(1, row, col)
        inverses.append(
            jnp.where(row == col, down, 0.0) - jnp.where(below, down * block * across, 0.0)
        )
    half = 2
    while half < size:
        below = below_blocks(half, row, col)
        inner = [
            dot32(jnp.where(below, block, 0.0), inverse) for block, inverse in zip(blocks, inverses)
        ]
        inverses = [inverse - dot32(inverse, part) for inverse, part in zip(inverses, inner)]
        half *= 2
    return inverses


def prepare_kernel(rows, block, depth, cuts, movers, me, place, source, *refs):
    *outs, factor, load_sem, store_sem = refs
    width, part = depth // 2, rows // cuts
    load = pltpu.make_async_copy(source, factor, load_sem)
    load.start()
    load.wait()
    first = me[0] * rows

    @pl.when((place[0] == 0) & (first < depth))
    def _():
        blocks = []
        for j in range(0, rows, block):
            at = jnp.minimum(first + j, depth - block)
            near = pl.multiple_of(at // LANES * LANES, LANES)
            value = factor[j : j + block, pl.ds(near, LANES)]
            value = pltpu.roll(value, (LANES - at % LANES) % LANES, 1)
            blocks.append(value[:, :block])
        row, col = grid_ids(block)
        blocks = [
            jnp.where(first + i * block < depth, value, jnp.where(row == col, 1.0, 0.0))
            for i, value in enumerate(blocks)
        ]
        for i, inverse in enumerate(invert_lower(blocks)):

            @pl.when(first + i * block < depth)
            def _(i=i, inverse=inverse):
                factor[i * block : (i + 1) * block, depth - block :] = inverse

    moves = me[0] < movers
    panel = pl.ds(width, width)
    copies = [
        (factor.at[pl.ds(cut * part, part), panel], outs[cut], store_sem.at[cut])
        for cut in range(cuts)
    ]
    if cuts > 1:
        sent = pl.ds(pl.multiple_of(jnp.where(moves, part, 0), 8), part)
        copies.append((factor.at[sent, panel], outs[cuts], store_sem.at[cuts]))
    copies = [pltpu.make_async_copy(*copy) for copy in copies]
    for copy in copies:
        copy.start()
    for copy in copies:
        copy.wait()


def prepare(me, place, factor, block, cuts, movers):
    rows, depth = factor.shape
    count = cuts + (1 if cuts > 1 else 0)
    return pl.pallas_call(
        functools.partial(prepare_kernel, rows, block, depth, cuts, movers),
        out_shape=[jax.ShapeDtypeStruct((rows // cuts, depth // 2), jnp.float32)] * count,
        in_specs=[SCALARS] * 2 + [ANY],
        out_specs=[ANY] * count,
        scratch_shapes=[
            pltpu.VMEM((rows, depth), jnp.float32),
            pltpu.SemaphoreType.DMA,
            pltpu.SemaphoreType.DMA((count,)),
        ],
        compiler_params=pltpu.CompilerParams(vmem_limit_bytes=VMEM_BYTES),
        cost_estimate=SHORT,
    )(me, place, factor)


def solve_kernel(pieces, rows, width, chunk, block, ids, place, *refs):
    held, rhs = refs[: 2 * pieces], refs[2 * pieces]
    *outs, lower, solved, piece_sem, rhs_sem, out_sem = refs[len(refs) - 7 :]
    depth = 2 * width

    @pl.when(place[0] == 0)
    def _():
        def copies(i):
            at = pl.ds(pl.multiple_of(ids[i] * rows, 8), rows)
            return [
                pltpu.make_async_copy(
                    held[k * pieces + i], lower.at[at, pl.ds(k * width, width)], piece_sem.at[k, i]
                )
                for k in range(2)
            ]

        for i in range(pieces):

            @pl.when(ids[i] * rows < depth)
            def _(i=i):
                for copy in copies(i):
                    copy.start()

        load = pltpu.make_async_copy(rhs.at[pl.ds(0, depth)], solved, rhs_sem)
        load.start()
        for i in range(pieces):

            @pl.when(ids[i] * rows < depth)
            def _(i=i):
                for copy in copies(i):
                    copy.wait()

        row, col = grid_ids(chunk)
        lane = lax.broadcasted_iota(jnp.int32, (chunk, LANES), 1)
        starts = range(0, depth, chunk)
        inverses = []
        for j in starts:
            value = lower[j : j + chunk, depth - LANES :]
            value = jnp.where(lane >= LANES - block, value, 0.0)
            shift = block
            while shift < LANES:
                value = value + pltpu.roll(value, LANES - shift, 1)
                shift *= 2
            value = jnp.concatenate([value] * (chunk // LANES), axis=1)
            inverses.append(jnp.where(row // block == col // block, value, 0.0))
        half = block
        while half < chunk:
            below = below_blocks(half, row, col)
            parts = [split16(inverse) for inverse in inverses]
            inner = [
                dot_split(
                    split16(jnp.where(below, lower[j : j + chunk, j : j + chunk], 0.0)), part
                )
                for j, part in zip(starts, parts)
            ]
            inverses = [
                inverse - dot_split(part, split16(value))
                for inverse, part, value in zip(inverses, parts, inner)
            ]
            half *= 2
        load.wait()
        stores = [
            pltpu.make_async_copy(solved.at[pl.ds(k * width, width)], outs[k], out_sem.at[k])
            for k in range(2)
        ]
        for j in starts:
            value = solved[j : j + chunk]
            if j:
                value = value - dot_split(
                    split16(lower[j : j + chunk, :j]), split16(solved[:j])
                )
            solved[j : j + chunk] = dot_split(split16(inverses[j // chunk]), split16(value))
            if (j + chunk) % width == 0:
                stores[j // width].start()
        for store in stores:
            store.wait()


def solve_panels(ids, place, held, rhs, after, width, block):
    pieces = len(held[0])
    rows = held[0][0].shape[0]
    columns, depth = rhs.shape[1], 2 * width
    tall = -(-depth // rows) * rows
    chunk = math.gcd(width, 2 * LANES)
    return pl.pallas_call(
        functools.partial(solve_kernel, pieces, rows, width, chunk, block),
        out_shape=[jax.ShapeDtypeStruct((width, columns), jnp.float32)] * 2,
        in_specs=[SCALARS] * 2 + [ANY] * (2 * pieces + 1 + len(after)),
        out_specs=[ANY] * 2,
        scratch_shapes=[
            pltpu.VMEM((tall, depth), jnp.float32),
            pltpu.VMEM((depth, columns), jnp.float32),
            pltpu.SemaphoreType.DMA((2, pieces)),
            pltpu.SemaphoreType.DMA,
            pltpu.SemaphoreType.DMA((2,)),
        ],
        compiler_params=pltpu.CompilerParams(vmem_limit_bytes=VMEM_BYTES),
        cost_estimate=pl.CostEstimate(
            flops=72 * width * width * columns,
            bytes_accessed=24 * width * columns,
            transcendentals=0,
        ),
    )(ids, place, *held[0], *held[1], rhs, *after)


def update_kernel(pieces, rows, width, group, tile, step, places, ids, place, *refs):
    held, refs = refs[: 2 * pieces], refs[2 * pieces :]
    rhs, refs = refs[0], refs[1:]
    solved, refs = refs[: 2 * places], refs[2 * places :]
    refs = refs[len(refs) - 11 :]
    out, lower, block, found, high, low, product, piece_sem, block_sem, found_sem, out_sem = refs
    depth = 2 * width
    start = place[0] * rhs.shape[0]

    def fetch(k, r):
        return pltpu.make_async_copy(
            solved[k * places + r], found.at[pl.ds(k * width, width)], found_sem.at[k]
        )

    def at(i):
        return pl.ds(pl.multiple_of(ids[i] * rows, 8), rows)

    def load(k, i, source):
        return pltpu.make_async_copy(
            held[source],
            lower.at[pl.ds(pl.multiple_of(i * rows, 8), rows), pl.ds(k * width, width)],
            piece_sem.at[k, i],
        )

    def load_block(i):
        return pltpu.make_async_copy(rhs.at[at(i)], block.at[i], block_sem.at[i])

    def store(i):
        return pltpu.make_async_copy(block.at[i], out.at[at(i)], out_sem.at[i])

    for r in range(places):

        @pl.when(place[0] % places == r)
        def _(r=r):
            for k in range(2):
                fetch(k, r).start()

    for i in range(pieces):
        for k in range(2):
            load(k, i, k * pieces + i).start()
        load_block(i).start()
    for k in range(2):
        fetch(k, 0).wait()
    high[...], low[...] = split16(found[...])

    @pl.loop(0, pieces // group)
    def _(g):
        members = [g * group + u for u in range(group)]
        for i in members:
            for k in range(2):
                load(k, i, 0).wait()
            load_block(i).wait()

        @pl.loop(0, rows // tile)
        def _(t):
            inside = pl.multiple_of(t * tile, 8)
            tops = [start + ids[i] * rows + inside for i in members]
            highest = functools.reduce(jnp.maximum, tops)

            @pl.when(highest + tile > depth)
            def _():
                here = pl.ds(pl.multiple_of(g * group * rows + inside, 8), group * tile)
                product[...] = dot_split(split16(lower[here]), (high[...], low[...]))

            for u, (i, top) in enumerate(zip(members, tops)):

                @pl.when(top >= depth)
                def _(i=i, u=u):
                    here = pl.ds(inside, tile)
                    block[i, here] = block[i, here] - product[u * tile : (u + 1) * tile]

                @pl.when(top < depth)
                def _(i=i, u=u, top=top):
                    @pl.loop(0, tile // step)
                    def _(v):
                        part = pl.multiple_of(v * step, 8)
                        row = top + part
                        here = pl.ds(inside + part, step)

                        @pl.when(row < depth)
                        def _():
                            block[i, here] = found[pl.ds(pl.multiple_of(row, 8), step)]

                        @pl.when(row >= depth)
                        def _():
                            block[i, here] = (
                                block[i, here] - product[pl.ds(u * tile + part, step)]
                            )

        for i in members:
            store(i).start()

    @pl.loop(0, pieces)
    def _(i):
        store(i).wait()


def update(ids, place, held, rhs, solved, width, written=None):
    pieces, places = len(held[0]), len(solved[0])
    rows, columns = held[0][0].shape[0], rhs.shape[1]
    step = math.gcd(rows, 2 * width)
    tile = step * max(m for m in range(1, rows // step + 1) if rows // step % m == 0 and step * m <= 512)
    group = 2 if pieces % 2 == 0 and tile == rows else 1
    operands = [ids, place, *[piece for group in held for piece in group], rhs, *solved[0], *solved[1]]
    extra = [] if written is None else [written]
    return pl.pallas_call(
        functools.partial(update_kernel, pieces, rows, width, group, tile, step, places),
        out_shape=jax.ShapeDtypeStruct(rhs.shape, jnp.float32),
        in_specs=[SCALARS] * 2 + [ANY] * (len(operands) - 2 + len(extra)),
        out_specs=ANY,
        input_output_aliases={len(operands): 0} if extra else {},
        scratch_shapes=[
            pltpu.VMEM((pieces * rows, 2 * width), jnp.float32),
            pltpu.VMEM((pieces, rows, columns), jnp.float32),
            pltpu.VMEM((2 * width, columns), jnp.float32),
            pltpu.VMEM((2 * width, columns), jnp.bfloat16),
            pltpu.VMEM((2 * width, columns), jnp.bfloat16),
            pltpu.VMEM((group * tile, columns), jnp.float32),
            pltpu.SemaphoreType.DMA((2, pieces)),
            pltpu.SemaphoreType.DMA((pieces,)),
            pltpu.SemaphoreType.DMA((2,)),
            pltpu.SemaphoreType.DMA((pieces,)),
        ],
        compiler_params=pltpu.CompilerParams(vmem_limit_bytes=VMEM_BYTES),
        cost_estimate=pl.CostEstimate(
            flops=12 * pieces * rows * width * columns,
            bytes_accessed=8 * pieces * rows * (width + columns),
            transcendentals=0,
        ),
    )(*operands, *extra)


def gate_kernel(count, *refs):
    pass


def gate(blocks, tokens):
    count = len(blocks)
    return pl.pallas_call(
        functools.partial(gate_kernel, count),
        out_shape=[jax.ShapeDtypeStruct(block.shape, block.dtype) for block in blocks],
        in_specs=[ANY] * (count + len(tokens)),
        out_specs=[ANY] * count,
        input_output_aliases={i: i for i in range(count)},
        compiler_params=pltpu.CompilerParams(vmem_limit_bytes=VMEM_BYTES),
    )(*blocks, *tokens)


def ring_pass(starts, ring):
    count = len(ring)
    onward = [(ring[i], ring[(i + 1) % count]) for i in range(count)]
    back = [(b, a) for a, b in onward]
    held = [[starts[k][k]] for k in range(2)]
    going = [list(ways) for ways in starts]
    steps = []
    for step in range(1, count // 2 + 1):
        for k in range(2):
            for way, pairs in enumerate((onward, back)):
                if step == count // 2 and way != k:
                    continue
                going[k][way] = lax.ppermute(going[k][way], "src", pairs)
                held[k].append(going[k][way])
        steps.append([list(ways) for ways in going])
    return held, steps


def spread_far(block, count, place):
    found = {0: block}
    stride = count // 2
    while stride > 1:
        for r in list(found):
            found[r + stride] = lax.ppermute(found[r], "row", [(r, r + stride)])
        stride //= 2
    for r in found:
        if r:
            block = jnp.where(place[0] == r, found[r], block)
    return block


def spread_near(block, count, tokens):
    if tokens:
        (block,) = gate([block], tokens)
    return [block, lax.ppermute(block, "row", [(r, r + 1) for r in range(0, count - 1, 2)])]


def swap_partners(count, tops):
    free = [s for s in range(count) if 2 * s >= tops]
    partners = []
    for s in range(count):
        if 2 * s + 1 < tops:
            pool = [f for f in free if f % 2 == s % 2] or free
            if not pool:
                return None
            partners.append(pool[-1])
            free.remove(pool[-1])
    return partners


def lookup(table, index):
    hit = index[:, None] == jnp.arange(len(table), dtype=jnp.int32)[None, :]
    return jnp.sum(jnp.where(hit, jnp.array(table, jnp.int32)[None, :], 0), axis=1)


def solution(mesh):
    count, places = mesh.shape["src"], mesh.shape["row"]
    axes = tuple(mesh.axis_names)

    def number(source, row):
        at, place = {"src": source, "row": row}, 0
        for axis in axes:
            place = place * mesh.shape[axis] + at[axis]
        return place

    def local(factor, right_side):
        rows, depth = factor.shape
        width, part = depth // 2, rows // 2
        block = math.gcd(math.gcd(rows, width), LANES)
        me = lax.axis_index("src").reshape(1).astype(jnp.int32)
        place = lax.axis_index("row").reshape(1).astype(jnp.int32)
        partners = swap_partners(count, -(-depth // part))
        ringed = count % 2 == 0 and count <= RING_LIMIT and part % 8 == 0 and partners is not None
        if not ringed:
            held = [
                [lax.all_gather(panel, "src", axis=0, tiled=True)]
                for panel in (factor[:, :width], *prepare(me, place, factor, block, 1, 0))
            ]
            top, top_spots = held, jnp.zeros_like(me)
            groups = [(held, top_spots)]
            after, near = [], [[], []]
        else:
            movers = len(partners)
            left = factor[:, :width]
            sent_first = jnp.where(me[0] < movers, left[part:], left[:part])
            *right, sent_second = prepare(me, place, factor, block, 2, movers)
            halves = [left[:part], right[0], left[part:], right[1]]
            pairs = [(s, f) for s, f in enumerate(partners)]
            swap = [(number(a, 0), number(b, 0)) for s, f in pairs for a, b in ((s, f), (f, s))]
            got = [lax.ppermute(sent, axes, swap) for sent in (sent_first, sent_second)]
            source = me[0]
            paired = functools.reduce(jnp.logical_or, [source == f for f in partners])
            takes = [(place[0] == 0) & paired, (place[0] == 0) & (source < movers)]
            own = [
                [jnp.where(takes[h], got[k], halves[2 * h + k]) for k in range(2)] for h in range(2)
            ]
            ring = list(range(0, count, 2)) + list(range(count - 1, 0, -2))
            position = jnp.where(source % 2 == 0, source // 2, count - 1 - source // 2)
            half = count // 2
            away = [0] + [d for step in range(1, half) for d in (-step, step)] + [half]
            position = (position + jnp.array(away, jnp.int32) + count) % count
            ids = jnp.where(position < half, 2 * position, 2 * (count - 1 - position) + 1)
            tables = [[2 * s + h for s in range(count)] for h in range(2)]
            for s, f in pairs:
                tables[0][f], tables[1][s] = 2 * s + 1, 2 * f
            spots = [
                jnp.where(place[0] == 0, lookup(tables[h], ids), 2 * ids + h).astype(jnp.int32)
                for h in range(2)
            ]
            top, steps = ring_pass([[piece] * 2 for piece in own[0]], ring)
            free = gate(own[1], [steps[-2][0][0]])
            full = gate(free, [steps[-1][0][0]])
            rest, steps = ring_pass([[full[0], free[0]], [free[1], full[1]]], ring)
            after = [steps[0][0][1], steps[0][1][0]]
            near = [steps[1][0] + steps[1][1], [steps[-2][0][0], steps[-2][1][1]]]
            top_spots, cut = spots[0], 2 * half - 2
            groups = [
                (
                    [top[k] + rest[k][:cut] for k in range(2)],
                    jnp.concatenate([spots[0], spots[1][:cut]]),
                ),
                ([rest[k][cut:] for k in range(2)], spots[1][cut:]),
            ]
        first, second = solve_panels(top_spots, place, top, right_side, after, width, block)
        solved = [
            spread_near(spread_far(first, places, place), places, near[0]),
            spread_near(spread_far(second, places, place), places, near[1]),
        ]
        result = None
        for held, spots in groups:
            result = update(spots, place, held, right_side, solved, width, result)
        return result

    placed = (P(("row", "src"), None), P("row", "src"))
    return jax.shard_map(
        local, mesh=mesh, in_specs=placed, out_specs=P("row", "src"), check_vma=False
    )
```
